512 devices in a mesh: wide: 8 (over x, z_hi), narrow: 64 (over z_lo, y, core).
Axes of the slice: x: 4, y: 8, z: 8 (z_hi: 2, z_lo: 4; z = z_hi * 4 + z_lo), core: 2. Of those that a mesh axis runs over, the one named last changes fastest.
Arguments:
- queries: bfloat16 [262144, 512], P(('wide', 'narrow')), as said below
- targets: int32 [262144], P(('wide', 'narrow')), may hold values from 0 to 1535
- lengths: int32 [1024], P(('wide', 'narrow')), may hold values from 1 to 256, as said below
- contrast_items: bfloat16 [1536, 512], P(('wide', 'narrow')), as said below
Outputs:
- query_grads: bfloat16 [262144, 512], P(('wide', 'narrow'))
- item_grads: float32 [1536, 512], P(('wide', 'narrow'))
- query_loss: float32 [262144], P(('wide', 'narrow'))
The draws below stay inside these ranges and needn't reach their ends.
Inputs may be any that keep to these rules, and one draw needn't show every extreme that they name: `lengths`: each sequence's count of valid positions; some sequence has all 256 valid. `contrast_items`: rows of roughly unit length. `queries`: entries within -2 and 2.
All inputs are finite; a program needn't handle non-finite values.
Results may differ from the reference program's by a relative error of at most 0.0034.
Values may be sent and summed in bfloat16 or wider, within the bound.
A program may use at most 64 MiB of HBM per device.

```python
import jax
import jax.numpy as jnp
from jax import lax

D = 512
SEQ_LEN = 256
QRY_DEV = 512
SEQS = 1024
TOKENS = 262144
POOL = 1536


def pool_rows(key):
    first = jax.random.fold_in(key, 0)
    normal_part = jnp.clip(jax.random.normal(first, (POOL, D), jnp.float32), -6.0, 6.0)
    base = normal_part * D ** (-0.5)
    return base


def draw_contrast_items(key, part):
    return pool_rows(key).astype(jnp.bfloat16)


def draw_queries(key, part):
    key = jax.random.fold_in(key, 11)
    first = jax.random.fold_in(key, 0)
    return (jnp.clip(jax.random.normal(first, (TOKENS, D), jnp.float32), -6.0, 6.0) * 0.1).astype(jnp.bfloat16)


def draw_lengths(key, part):
    key = jax.random.fold_in(key, 5)
    counts = jax.random.randint(key, (SEQS,), 1, SEQ_LEN + 1, jnp.int32)
    return counts.at[0].set(SEQ_LEN)


def set_ends(drawn, rng, low, top_value):
    index_at = [jax.random.randint(jax.random.fold_in(rng, axis), (), 0, length) for axis, length in enumerate(drawn.shape)]
    longest = drawn.shape.index(max(drawn.shape))
    next_to = index_at[:longest] + [(index_at[longest] + 1) % drawn.shape[longest]] + index_at[longest + 1:]
    return drawn.at[tuple(index_at)].set(low).at[tuple(next_to)].set(top_value)


def setup_inputs(seed: int = 0) -> dict:
    splits = jax.random.split(jax.random.key(seed), 5)
    return {
        "queries": draw_queries(jax.random.fold_in(splits[4], 71), 0),
        "targets": set_ends(jax.random.randint(splits[1], (TOKENS,), 0, POOL), jax.random.fold_in(splits[1], 1), 0, POOL - 1).astype(jnp.int32),
        "lengths": draw_lengths(jax.random.fold_in(splits[4], 71), 0),
        "contrast_items": draw_contrast_items(jax.random.fold_in(splits[4], 71), 0),
    }


sharpness_factor = 20.0


def reference(queries, targets, lengths, contrast_items):
    total_rows = queries.shape[0]
    position = jnp.arange(total_rows, dtype=jnp.int32) % SEQ_LEN
    validity_mask = (position < jnp.repeat(lengths, SEQ_LEN)).astype(jnp.float32)
    blocks = total_rows // QRY_DEV
    query_blocks = queries.reshape(blocks, QRY_DEV, D)
    target_blocks = targets.reshape(blocks, QRY_DEV)
    valid_blocks = validity_mask.reshape(blocks, QRY_DEV)
    item_index = jnp.arange(POOL, dtype=jnp.int32)

    def step(carry, item):
        request_embeds, target_rows, live_entries = item
        affinity_matrix = lax.dot_general(request_embeds, contrast_items, (((1,), (1,)), ((), ())), preferred_element_type=jnp.float32) * sharpness_factor
        positive_indicator = (target_rows[:, None] == item_index[None, :]).astype(jnp.float32)
        largest = jnp.max(affinity_matrix, axis=1)
        normalizer_term = largest + jnp.log(jnp.sum(jnp.exp(affinity_matrix - largest[:, None]), axis=1))
        target_score = jnp.sum(positive_indicator * affinity_matrix, axis=1)
        loss_rows = live_entries * (normalizer_term - target_score)
        score_derivative = (live_entries[:, None] * (jnp.exp(affinity_matrix - normalizer_term[:, None]) - positive_indicator) * sharpness_factor).astype(jnp.bfloat16)
        query_rows_grad = jnp.dot(score_derivative, contrast_items, preferred_element_type=jnp.float32).astype(jnp.bfloat16)
        carry = carry + lax.dot_general(score_derivative, request_embeds, (((0,), (0,)), ((), ())), preferred_element_type=jnp.float32)
        return carry, (query_rows_grad, loss_rows)

    start = jnp.zeros((POOL, D), jnp.float32)
    item_grads, (query_grads, query_loss) = lax.scan(step, start, (query_blocks, target_blocks, valid_blocks))
    return query_grads.reshape(total_rows, D), item_grads, query_loss.reshape(total_rows)
```

```python
import functools

import jax
import jax.numpy as jnp
from jax import lax
from jax.experimental import pallas as pl
from jax.experimental.pallas import tpu as pltpu
from jax.sharding import PartitionSpec as P

MESH = pl.DeviceIdType.MESH
SEQ_LEN = 256
SHARPNESS = 20.0
LOG2E = 1.4426950408889634
ZHI = 2
OWNED = 3
BLK = 16


def kernel(X, Y, Z, q_hbm, tgt_ref, len_ref, it_ref, qg_ref, ig_ref, loss_ref,
           q_all, info, stat, pool, pack, blk, land, scores, grads, out_items, in_items,
           acc, pieces, land2, qpart, qland,
           q_sem, pair_ssem, pair_rsem, s1_ssem, s1_rsem, s2_ssem, s2_rsem,
           r1_ssem, r1_rsem, r2_ssem, r2_rsem):
    zlo = Z // ZHI
    wide, narrow = lax.axis_index("wide"), lax.axis_index("narrow")
    x, c = wide // ZHI, narrow % 2
    y, z = (narrow // 2) % Y, (wide % ZHI) * zlo + narrow // (2 * Y)
    qd, width = q_hbm.shape
    chunks = width // 128
    slab = Y * Z * OWNED
    half = X * slab // 2
    yrows, zrows = half // Y, half // Z
    items = X * slab
    even = x % 2 == 0

    def dev(px, py, pz, pc):
        return (px * ZHI + pz // zlo, ((pz % zlo) * Y + py) * 2 + pc)

    def yz_peer(i):
        return (y + i // Z) % Y, (z + i % Z) % Z

    def xz_peer(i):
        return (x + i // Z) % X, (z + i % Z) % Z

    def xy_peer(i):
        return (x + i // Y) % X, (y + i % Y) % Y

    def remote(src, dst, ssem, rsem, to):
        return pltpu.make_async_remote_copy(
            src_ref=src, dst_ref=dst, send_sem=ssem, recv_sem=rsem, device_id=to, device_id_type=MESH)

    def bytes_of(ref, sem):
        return pltpu.make_async_copy(ref, ref, sem)

    def loop(lo, hi, f):
        def step(i, carry):
            f(i)
            return carry
        lax.fori_loop(lo, hi, step, 0)

    load_q = pltpu.make_async_copy(q_hbm, q_all.at[c], q_sem)
    load_q.start()

    barrier = pltpu.get_barrier_semaphore()
    partner = dev(x, y, z, 1 - c)

    def greet(to):
        pl.semaphore_signal(barrier, inc=1, device_id=to, device_id_type=MESH)

    greet(partner)

    @pl.when(c == 0)
    def _():
        def one(i):
            py, pz = yz_peer(i)
            greet(dev(x, py, pz, 0))
        loop(1, Y * Z, one)
        loop(1, X, lambda i: greet(dev((x + i) % X, y, z, 0)))

    @pl.when(c == 1)
    def _():
        def one(i):
            px, pz = xz_peer(i)
            greet(dev(px, y, pz, 1))
        loop(1, X * Z, one)

        def two(i):
            px, py = xy_peer(i)
            greet(dev(px, py, z, 1))
        loop(1, X * Y, two)

    own = it_ref[...].astype(jnp.float32)
    pack[pl.ds(0, BLK), :] = jnp.zeros((BLK, 128), jnp.float32)
    for a in range(chunks):
        pack[pl.ds(a * OWNED, OWNED), :] = own[:, a * 128:(a + 1) * 128]
    blk[...] = pack[pl.ds(0, BLK), :].astype(jnp.bfloat16)

    pos = lax.broadcasted_iota(jnp.int32, (1, qd), 1)
    live = jnp.where(pos < SEQ_LEN, (pos < len_ref[0]).astype(jnp.float32),
                     (pos - SEQ_LEN < len_ref[1]).astype(jnp.float32))
    info[c, pl.ds(0, 1), :] = tgt_ref[...].astype(jnp.float32)
    info[c, pl.ds(1, 1), :] = live
    info[c, pl.ds(2, 6), :] = jnp.zeros((6, qd), jnp.float32)
    load_q.wait()

    @pl.when(c == 0)
    def _():
        pl.semaphore_wait(barrier, Y * Z - 1 + X - 1 + 1)

    @pl.when(c == 1)
    def _():
        pl.semaphore_wait(barrier, X * Z - 1 + X * Y - 1 + 1)

    def rows(i):
        return pl.ds(pl.multiple_of(i * BLK, BLK), BLK)

    s1_copies = []

    @pl.when(c == 0)
    def _():
        me = y * Z + z
        land[rows(me), :] = blk[...]

        def one(i):
            py, pz = yz_peer(i)
            remote(blk, land.at[rows(me)], s1_ssem, s1_rsem, dev(x, py, pz, 0)).start()
        loop(1, Y * Z, one)

    @pl.when(jnp.logical_and(c == 1, even))
    def _():
        me = (x // 2) * Z + z
        land[rows(me), :] = blk[...]

        def one(i):
            px, pz = xz_peer(i)
            remote(blk, land.at[rows(me)], s1_ssem, s1_rsem, dev(px, y, pz, 1)).start()
        loop(1, X * Z, one)

    @pl.when(jnp.logical_and(c == 1, jnp.logical_not(even)))
    def _():
        me = X // 2 * Z + (x // 2) * Y + y
        land[rows(me), :] = blk[...]

        def one(i):
            px, py = xy_peer(i)
            remote(blk, land.at[rows(me)], s1_ssem, s1_rsem, dev(px, py, z, 1)).start()
        loop(1, X * Y, one)

    q_copy = remote(q_all.at[c], q_all.at[c], pair_ssem.at[0], pair_rsem.at[0], partner)
    q_copy.start()
    info_copy = remote(info.at[c], info.at[c], pair_ssem.at[1], pair_rsem.at[1], partner)
    info_copy.start()

    @pl.when(c == 0)
    def _():
        bytes_of(land.at[pl.ds(0, (Y * Z - 1) * BLK)], s1_rsem).wait()

    @pl.when(c == 1)
    def _():
        bytes_of(land.at[pl.ds(0, (X * Z - 1) * BLK)], s1_rsem).wait()

    def unpack(first, owners, base):
        n = owners * BLK
        pack[pl.ds(0, n), :] = land[pl.ds(first * BLK, n), :].astype(jnp.float32)
        for r in range(OWNED):
            for a in range(chunks):
                piece = pack[pl.ds(a * OWNED + r, owners, stride=BLK), :]
                at = base + r * owners
                pool[pl.ds(pl.multiple_of(at, 16), owners), a * 128:(a + 1) * 128] = piece.astype(jnp.bfloat16)

    xz_own, xy_own = X // 2 * Z, X // 2 * Y

    def slab0(px):
        return pl.ds(pl.multiple_of(px * slab, 16), slab)

    def slab_y(py):
        return pl.ds(pl.multiple_of(py * yrows, 16), yrows)

    def slab_z(pz):
        return pl.ds(pl.multiple_of(half + pz * zrows, 16), zrows)

    @pl.when(c == 0)
    def _():
        unpack(0, Y * Z, x * slab)

        def one(i):
            px = (x + i) % X
            remote(pool.at[slab0(x)], pool.at[slab0(x)], s2_ssem, s2_rsem, dev(px, y, z, 0)).start()
        loop(1, X, one)
        bytes_of(pool.at[pl.ds(0, (X - 1) * slab)], s2_rsem).wait()

    @pl.when(c == 1)
    def _():
        unpack(0, xz_own, y * yrows)

        def one(i):
            remote(pool.at[slab_y(y)], pool.at[slab_y(y)], s2_ssem, s2_rsem, dev(x, (y + i) % Y, z, 1)).start()
        loop(1, Y, one)
        unpack(xz_own, xy_own, half + z * zrows)

        def two(i):
            remote(pool.at[slab_z(z)], pool.at[slab_z(z)], s2_ssem, s2_rsem, dev(x, y, (z + i) % Z, 1)).start()
        loop(1, Z, two)
        bytes_of(pool.at[pl.ds(0, (Y - 1) * yrows + (Z - 1) * zrows)], s2_rsem).wait()

    q_copy.wait()
    info_copy.wait()

    def local_row(h):
        t = info[h, pl.ds(0, 1), :].astype(jnp.int32)
        o = (t * 21846) >> 16
        r = t - o * OWNED
        w, n = o // (zlo * Y * 2), o % (zlo * Y * 2)
        tx, tc = w // ZHI, n % 2
        ty, tz = (n // 2) % Y, (w % ZHI) * zlo + n // (2 * Y)
        on0 = tx * slab + r * (Y * Z) + ty * Z + tz
        on1 = jnp.where(tx % 2 == 0, ty * yrows + r * xz_own + (tx // 2) * Z + tz,
                        half + tz * zrows + r * xy_own + (tx // 2) * Y + ty)
        return jnp.where(tc == c, jnp.where(tc == 0, on0, on1), -1)

    tile = items // 3
    step = max(8, items // 12)
    fold = functools.partial(jnp.reshape, shape=(step // 8, 8, qd))
    row_iota = lax.broadcasted_iota(jnp.int32, (step, qd), 0)
    K = SHARPNESS * LOG2E

    def first_pass(h):
        m8 = jnp.full((8, qd), -3e38, jnp.float32)
        for i in range(3):
            s = lax.dot_general(pool[pl.ds(i * tile, tile), :], q_all[h], (((1,), (1,)), ((), ())),
                                preferred_element_type=jnp.float32)
            scores[h, pl.ds(i * tile, tile), :] = s
            m8 = jnp.maximum(m8, jnp.max(s.reshape(tile // 8, 8, qd), axis=0))
        m = jnp.max(m8, axis=0, keepdims=True)
        target = local_row(h)

        def body(i, carry):
            l8, t8 = carry
            at = pl.ds(pl.multiple_of(i * step, 8), step)
            s = scores[h, at, :]
            hit = row_iota == target - i * step
            e = jnp.exp2((s - m) * K)
            scores[h, at, :] = e
            return l8 + jnp.sum(fold(e), axis=0), t8 + jnp.sum(fold(jnp.where(hit, s, 0.0)), axis=0)

        zero = jnp.zeros((8, qd), jnp.float32)
        l8, t8 = lax.fori_loop(0, items // step, body, (zero, zero))
        stat[0, h, pl.ds(0, 1), :] = m
        stat[0, h, pl.ds(1, 1), :] = jnp.sum(l8, axis=0, keepdims=True)
        stat[0, h, pl.ds(2, 1), :] = jnp.sum(t8, axis=0, keepdims=True)
        stat[0, h, pl.ds(3, 5), :] = jnp.zeros((5, qd), jnp.float32)
        remote(stat.at[0, h], stat.at[1, h], pair_ssem.at[2 + h], pair_rsem.at[2 + h], partner).start()

    loop(0, 2, first_pass)

    def second_pass(h):
        remote(stat.at[0, h], stat.at[1, h], pair_ssem.at[2 + h], pair_rsem.at[2 + h], partner).wait()
        m, l, t = (stat[0, h, pl.ds(k, 1), :] for k in range(3))
        m2, l2, t2 = (stat[1, h, pl.ds(k, 1), :] for k in range(3))
        top = jnp.maximum(m, m2)
        mine = jnp.exp2((m - top) * K)
        total = l * mine + l2 * jnp.exp2((m2 - top) * K)
        valid = info[h, pl.ds(1, 1), :]
        weight = SHARPNESS * valid
        factor = weight * mine / total
        target = local_row(h)

        @pl.when(h == c)
        def _():
            loss_ref[...] = valid * (SHARPNESS * (top - (t + t2)) + jnp.log(total))

        def body(i):
            at = pl.ds(pl.multiple_of(i * step, 16), step)
            hit = row_iota == target - i * step
            g = scores[h, at, :] * factor - jnp.where(hit, weight, 0.0)
            grads[h, at, :] = g.astype(jnp.bfloat16)
        loop(0, items // step, body)

    loop(0, 2, second_pass)

    def item_tile(i):
        px = (x + 1 + i) % X
        at = slab0(px)
        g = jnp.dot(grads[0, at, :], q_all[0], preferred_element_type=jnp.float32)
        g = g + jnp.dot(grads[1, at, :], q_all[1], preferred_element_type=jnp.float32)
        out_items[at, :] = g.astype(jnp.bfloat16)

        @pl.when(jnp.logical_and(c == 0, px != x))
        def _():
            remote(out_items.at[at], in_items.at[slab0(x)], r1_ssem, r1_rsem, dev(px, y, z, 0)).start()

    loop(0, X, item_tile)

    @pl.when(c == 1)
    def _():
        def one(i):
            py = (y + i) % Y
            remote(out_items.at[slab_y(py)], in_items.at[slab_y(y)], r1_ssem, r1_rsem, dev(x, py, z, 1)).start()
        loop(1, Y, one)

        def two(i):
            pz = (z + i) % Z
            remote(out_items.at[slab_z(pz)], in_items.at[slab_z(z)], r1_ssem, r1_rsem, dev(x, y, pz, 1)).start()
        loop(1, Z, two)

    def query_part(h):
        return lax.dot_general(grads[h], pool[...], (((0,), (0,)), ((), ())), preferred_element_type=jnp.float32)

    qpart[...] = query_part(1 - c)
    part_copy = remote(qpart, qland, pair_ssem.at[4], pair_rsem.at[4], partner)
    part_copy.start()
    scores[0, pl.ds(0, qd), :] = query_part(c)

    def spread(rows_sum, owners, first):
        n = owners * BLK
        pack[pl.ds(0, n), :] = jnp.zeros((n, 128), jnp.float32)
        for r in range(OWNED):
            for a in range(chunks):
                pack[pl.ds(a * OWNED + r, owners, stride=BLK), :] = \
                    rows_sum[r * owners:(r + 1) * owners, a * 128:(a + 1) * 128]
        pieces[pl.ds(first * BLK, n), :] = pack[pl.ds(0, n), :].astype(jnp.bfloat16)

    @pl.when(c == 0)
    def _():
        bytes_of(in_items.at[pl.ds(0, (X - 1) * slab)], r1_rsem).wait()
        total = out_items[slab0(x), :].astype(jnp.float32)
        for i in range(1, X):
            total = total + in_items[slab0((x + i) % X), :].astype(jnp.float32)
        acc[pl.ds(0, slab), :] = total
        spread(acc[pl.ds(0, slab), :], Y * Z, 0)
        me = y * Z + z
        land2[rows(me), :] = pieces[rows(me), :]

        def one(i):
            py, pz = yz_peer(i)
            remote(pieces.at[rows(py * Z + pz)], land2.at[rows(me)], r2_ssem, r2_rsem, dev(x, py, pz, 0)).start()
        loop(1, Y * Z, one)

    @pl.when(c == 1)
    def _():
        bytes_of(in_items.at[pl.ds(0, (Y - 1) * yrows + (Z - 1) * zrows)], r1_rsem).wait()
        acc[pl.ds(0, yrows), :] = out_items[slab_y(y), :].astype(jnp.float32)
        acc[pl.ds(yrows, zrows), :] = out_items[slab_z(z), :].astype(jnp.float32)

        def one(i):
            acc[pl.ds(0, yrows), :] += in_items[slab_y((y + i) % Y), :].astype(jnp.float32)
        loop(1, Y, one)

        def two(i):
            acc[pl.ds(yrows, zrows), :] += in_items[slab_z((z + i) % Z), :].astype(jnp.float32)
        loop(1, Z, two)
        spread(acc[pl.ds(0, yrows), :], xz_own, 0)
        spread(acc[pl.ds(yrows, zrows), :], xy_own, xz_own)

        def to_even(i):
            px, pz = 2 * (i // Z), i % Z

            @pl.when(jnp.logical_or(px != x, pz != z))
            def _():
                remote(pieces.at[rows(i)], land2.at[rows(x * Z + z)], r2_ssem, r2_rsem, dev(px, y, pz, 1)).start()

            @pl.when(jnp.logical_and(px == x, pz == z))
            def _():
                land2[rows(x * Z + z), :] = pieces[rows(i), :]
        loop(0, xz_own, to_even)

        def to_odd(i):
            px, py = 2 * (i // Y) + 1, i % Y

            @pl.when(jnp.logical_or(px != x, py != y))
            def _():
                remote(pieces.at[rows(xz_own + i)], land2.at[rows(x * Y + y)], r2_ssem, r2_rsem, dev(px, py, z, 1)).start()

            @pl.when(jnp.logical_and(px == x, py == y))
            def _():
                land2[rows(x * Y + y), :] = pieces[rows(xz_own + i), :]
        loop(0, xy_own, to_odd)

    part_copy.wait()
    qg_ref[...] = (scores[0, pl.ds(0, qd), :] + qland[...]).astype(jnp.bfloat16)

    @pl.when(c == 0)
    def _():
        bytes_of(land2.at[pl.ds(0, (Y * Z - 1) * BLK)], r2_rsem).wait()

    @pl.when(c == 1)
    def _():
        bytes_of(land2.at[pl.ds(0, (X * Z - 1) * BLK)], r2_rsem).wait()

    def gather(n):
        def body(i, carry):
            return carry + land2[rows(i), :].astype(jnp.float32)
        pack[pl.ds(0, BLK), :] = lax.fori_loop(0, n, body, jnp.zeros((BLK, 128), jnp.float32))

    @pl.when(c == 0)
    def _():
        gather(Y * Z)

    @pl.when(c == 1)
    def _():
        gather(X * Z)
    for a in range(chunks):
        ig_ref[:, a * 128:(a + 1) * 128] = pack[pl.ds(a * OWNED, OWNED), :]

    @pl.when(c == 0)
    def _():
        bytes_of(land.at[pl.ds(0, (Y * Z - 1) * BLK)], s1_ssem).wait()
        bytes_of(pool.at[pl.ds(0, (X - 1) * slab)], s2_ssem).wait()
        bytes_of(pool.at[pl.ds(0, (X - 1) * slab)], r1_ssem).wait()
        bytes_of(land2.at[pl.ds(0, (Y * Z - 1) * BLK)], r2_ssem).wait()

    @pl.when(c == 1)
    def _():
        bytes_of(land.at[pl.ds(0, (X * Z - 1) * BLK)], s1_ssem).wait()
        bytes_of(pool.at[pl.ds(0, (Y - 1) * yrows + (Z - 1) * zrows)], s2_ssem).wait()
        bytes_of(pool.at[pl.ds(0, (Y - 1) * yrows + (Z - 1) * zrows)], r1_ssem).wait()
        bytes_of(land2.at[pl.ds(0, (X * Z - 1) * BLK)], r2_ssem).wait()


def solution(mesh):
    X = mesh.shape["wide"] // ZHI

    def body(queries, targets, lengths, contrast_items):
        qd, width = queries.shape
        zlo = 4 if mesh.shape["narrow"] == 64 else 1
        Y = mesh.shape["narrow"] // (2 * zlo)
        Z = zlo * ZHI
        items = X * Y * Z * OWNED
        blocks = max(Y * Z, X * Z, X * Y) * BLK
        vmem = pl.BlockSpec(memory_space=pltpu.VMEM)
        f32, bf16 = jnp.float32, jnp.bfloat16
        qg, ig, loss = pl.pallas_call(
            functools.partial(kernel, X, Y, Z),
            out_shape=(
                jax.ShapeDtypeStruct((qd, width), bf16),
                jax.ShapeDtypeStruct((OWNED, width), f32),
                jax.ShapeDtypeStruct((1, qd), f32),
            ),
            in_specs=[pl.BlockSpec(memory_space=pl.ANY), vmem, pl.BlockSpec(memory_space=pltpu.SMEM), vmem],
            out_specs=(vmem, vmem, vmem),
            scratch_shapes=[
                pltpu.VMEM((2, qd, width), bf16),
                pltpu.VMEM((2, 8, qd), f32),
                pltpu.VMEM((2, 2, 8, qd), f32),
                pltpu.VMEM((items, width), bf16),
                pltpu.VMEM((blocks, 128), f32),
                pltpu.VMEM((BLK, 128), bf16),
                pltpu.VMEM((blocks, 128), bf16),
                pltpu.VMEM((2, max(items, qd), qd), f32),
                pltpu.VMEM((2, items, qd), bf16),
                pltpu.VMEM((items, width), bf16),
                pltpu.VMEM((items, width), bf16),
                pltpu.VMEM((items // X, width), f32),
                pltpu.VMEM((blocks, 128), bf16),
                pltpu.VMEM((blocks, 128), bf16),
                pltpu.VMEM((qd, width), f32),
                pltpu.VMEM((qd, width), f32),
                pltpu.SemaphoreType.DMA,
                pltpu.SemaphoreType.DMA((5,)),
                pltpu.SemaphoreType.DMA((5,)),
                *[pltpu.SemaphoreType.DMA] * 8,
            ],
            compiler_params=pltpu.CompilerParams(
                collective_id=0, has_side_effects=True, vmem_limit_bytes=40 << 20),
        )(queries, targets.reshape(1, qd), lengths, contrast_items)
        return qg, ig, loss.reshape(qd)

    rows = P(("wide", "narrow"), None)
    flat = P(("wide", "narrow"))
    return jax.shard_map(
        body, mesh=mesh, in_specs=(rows, flat, flat, rows), out_specs=(rows, rows, flat), check_vma=False)
```

```python
import functools

import jax
import jax.numpy as jnp
from jax import lax
from jax.experimental import pallas as pl
from jax.experimental.pallas import tpu as pltpu
from jax.sharding import PartitionSpec as P

MESH = pl.DeviceIdType.MESH
SEQ_LEN = 256
SHARPNESS = 20.0
LOG2E = 1.4426950408889634
ZHI = 2
OWNED = 3
BLK = 16


def hops(d, n):
    return min(d % n, -d % n)


def far_first(A, B):
    offsets = [(a, b) for a in range(A) for b in range(B) if a or b]
    return sorted(offsets, key=lambda o: -hops(o[0], A) - hops(o[1], B))


def far_ring(n):
    return sorted(range(1, n), key=lambda d: -hops(d, n))


def kernel(X, Y, Z, q_hbm, tgt_hbm, len_hbm, it_hbm, qg_hbm, ig_hbm, loss_hbm,
           tgt_ref, len_ref, it_ref, qg_ref, ig_ref, loss_ref, q_all, info, stat, pool, pack, blk, land, scores, grads, out_items, in_items,
           acc, pieces, land2, qpart, qland,
           q_sem, in_sem, out_sem, pair_ssem, pair_rsem, s1_ssem, s1_rsem, s2_ssem, s2_rsem,
           r1_ssem, r1_rsem, r2_ssem, r2_rsem):
    zlo = Z // ZHI
    wide, narrow = lax.axis_index("wide"), lax.axis_index("narrow")
    x, c = wide // ZHI, narrow % 2
    y, z = (narrow // 2) % Y, (wide % ZHI) * zlo + narrow // (2 * Y)
    qd, width = q_hbm.shape
    chunks = width // 128
    slab = Y * Z * OWNED
    half = X * slab // 2
    yrows, zrows = half // Y, half // Z
    items = X * slab
    even = x % 2 == 0

    def dev(px, py, pz, pc):
        return (px * ZHI + pz // zlo, ((pz % zlo) * Y + py) * 2 + pc)

    yz, xz, xy = far_first(Y, Z), far_first(X, Z), far_first(X, Y)

    def remote(src, dst, ssem, rsem, to):
        return pltpu.make_async_remote_copy(
            src_ref=src, dst_ref=dst, send_sem=ssem, recv_sem=rsem, device_id=to, device_id_type=MESH)

    def bytes_of(ref, sem):
        return pltpu.make_async_copy(ref, ref, sem)

    def loop(lo, hi, f):
        def step(i, carry):
            f(i)
            return carry
        lax.fori_loop(lo, hi, step, 0)

    loads = [pltpu.make_async_copy(a, b, in_sem.at[k])
             for k, (a, b) in enumerate([(it_hbm, it_ref), (tgt_hbm, tgt_ref), (len_hbm, len_ref)])]
    load_q = pltpu.make_async_copy(q_hbm, q_all.at[c], q_sem)
    for load in loads:
        load.start()
    load_q.start()

    barrier = pltpu.get_barrier_semaphore()
    partner = dev(x, y, z, 1 - c)

    def greet(to):
        pl.semaphore_signal(barrier, inc=1, device_id=to, device_id_type=MESH)

    @pl.when(c == 0)
    def _():
        for dy, dz in yz:
            greet(dev(x, (y + dy) % Y, (z + dz) % Z, 0))
        for dx in far_ring(X):
            greet(dev((x + dx) % X, y, z, 0))

    @pl.when(c == 1)
    def _():
        for dx, dz in xz:
            greet(dev((x + dx) % X, y, (z + dz) % Z, 1))
        for dx, dy in xy:
            greet(dev((x + dx) % X, (y + dy) % Y, z, 1))

    greet(partner)

    loads[0].wait()
    own = it_ref[...].astype(jnp.float32)
    pack[pl.ds(0, BLK), :] = jnp.zeros((BLK, 128), jnp.float32)
    for a in range(chunks):
        pack[pl.ds(a * OWNED, OWNED), :] = own[:, a * 128:(a + 1) * 128]
    blk[...] = pack[pl.ds(0, BLK), :].astype(jnp.bfloat16)

    loads[1].wait()
    loads[2].wait()
    pos = lax.broadcasted_iota(jnp.int32, (1, qd), 1)
    live = jnp.where(pos < SEQ_LEN, (pos < len_ref[0]).astype(jnp.float32),
                     (pos - SEQ_LEN < len_ref[1]).astype(jnp.float32))
    info[c, pl.ds(0, 1), :] = tgt_ref[...].astype(jnp.float32)
    info[c, pl.ds(1, 1), :] = live
    info[c, pl.ds(2, 6), :] = jnp.zeros((6, qd), jnp.float32)
    load_q.wait()

    @pl.when(c == 0)
    def _():
        pl.semaphore_wait(barrier, Y * Z - 1 + X - 1 + 1)

    @pl.when(c == 1)
    def _():
        pl.semaphore_wait(barrier, X * Z - 1 + X * Y - 1 + 1)

    def rows(i):
        return pl.ds(pl.multiple_of(i * BLK, BLK), BLK)

    @pl.when(c == 0)
    def _():
        me = y * Z + z
        land[rows(me), :] = blk[...]

        for dy, dz in yz:
            remote(blk, land.at[rows(me)], s1_ssem, s1_rsem, dev(x, (y + dy) % Y, (z + dz) % Z, 0)).start()

    @pl.when(jnp.logical_and(c == 1, even))
    def _():
        me = (x // 2) * Z + z
        land[rows(me), :] = blk[...]

        for dx, dz in xz:
            remote(blk, land.at[rows(me)], s1_ssem, s1_rsem, dev((x + dx) % X, y, (z + dz) % Z, 1)).start()

    @pl.when(jnp.logical_and(c == 1, jnp.logical_not(even)))
    def _():
        me = X // 2 * Z + (x // 2) * Y + y
        land[rows(me), :] = blk[...]

        for dx, dy in xy:
            remote(blk, land.at[rows(me)], s1_ssem, s1_rsem, dev((x + dx) % X, (y + dy) % Y, z, 1)).start()

    q_copy = remote(q_all.at[c], q_all.at[c], pair_ssem.at[0], pair_rsem.at[0], partner)
    q_copy.start()
    info_copy = remote(info.at[c], info.at[c], pair_ssem.at[1], pair_rsem.at[1], partner)
    info_copy.start()

    @pl.when(c == 0)
    def _():
        bytes_of(land.at[pl.ds(0, (Y * Z - 1) * BLK)], s1_rsem).wait()

    @pl.when(c == 1)
    def _():
        bytes_of(land.at[pl.ds(0, (X * Z - 1) * BLK)], s1_rsem).wait()

    def unpack(first, owners, base):
        n = owners * BLK
        pack[pl.ds(0, n), :] = land[pl.ds(first * BLK, n), :].astype(jnp.float32)
        for r in range(OWNED):
            for a in range(chunks):
                piece = pack[pl.ds(a * OWNED + r, owners, stride=BLK), :]
                at = base + r * owners
                pool[pl.ds(pl.multiple_of(at, 16), owners), a * 128:(a + 1) * 128] = piece.astype(jnp.bfloat16)

    xz_own, xy_own = X // 2 * Z, X // 2 * Y

    def slab0(px):
        return pl.ds(pl.multiple_of(px * slab, 16), slab)

    def slab_y(py):
        return pl.ds(pl.multiple_of(py * yrows, 16), yrows)

    def slab_z(pz):
        return pl.ds(pl.multiple_of(half + pz * zrows, 16), zrows)

    @pl.when(c == 0)
    def _():
        unpack(0, Y * Z, x * slab)

        for dx in far_ring(X):
            remote(pool.at[slab0(x)], pool.at[slab0(x)], s2_ssem, s2_rsem, dev((x + dx) % X, y, z, 0)).start()
        bytes_of(pool.at[pl.ds(0, (X - 1) * slab)], s2_rsem).wait()

    @pl.when(c == 1)
    def _():
        unpack(0, xz_own, y * yrows)

        for dy in far_ring(Y):
            remote(pool.at[slab_y(y)], pool.at[slab_y(y)], s2_ssem, s2_rsem, dev(x, (y + dy) % Y, z, 1)).start()
        unpack(xz_own, xy_own, half + z * zrows)

        for dz in far_ring(Z):
            remote(pool.at[slab_z(z)], pool.at[slab_z(z)], s2_ssem, s2_rsem, dev(x, y, (z + dz) % Z, 1)).start()
        bytes_of(pool.at[pl.ds(0, (Y - 1) * yrows + (Z - 1) * zrows)], s2_rsem).wait()

    q_copy.wait()
    info_copy.wait()

    def local_row(h):
        t = info[h, pl.ds(0, 1), :].astype(jnp.int32)
        o = (t * 21846) >> 16
        r = t - o * OWNED
        w, n = o // (zlo * Y * 2), o % (zlo * Y * 2)
        tx, tc = w // ZHI, n % 2
        ty, tz = (n // 2) % Y, (w % ZHI) * zlo + n // (2 * Y)
        on0 = tx * slab + r * (Y * Z) + ty * Z + tz
        on1 = jnp.where(tx % 2 == 0, ty * yrows + r * xz_own + (tx // 2) * Z + tz,
                        half + tz * zrows + r * xy_own + (tx // 2) * Y + ty)
        return jnp.where(tc == c, jnp.where(tc == 0, on0, on1), -1)

    tile = items // 3
    step = max(8, items // 12)
    fold = functools.partial(jnp.reshape, shape=(step // 8, 8, qd))
    row_iota = lax.broadcasted_iota(jnp.int32, (step, qd), 0)
    K = SHARPNESS * LOG2E

    def first_pass(h):
        m8 = jnp.full((8, qd), -3e38, jnp.float32)
        for i in range(3):
            s = lax.dot_general(pool[pl.ds(i * tile, tile), :], q_all[h], (((1,), (1,)), ((), ())),
                                preferred_element_type=jnp.float32)
            scores[h, pl.ds(i * tile, tile), :] = s
            m8 = jnp.maximum(m8, jnp.max(s.reshape(tile // 8, 8, qd), axis=0))
        m = jnp.max(m8, axis=0, keepdims=True)
        target = local_row(h)

        def body(i, carry):
            l8, t8 = carry
            at = pl.ds(pl.multiple_of(i * step, 8), step)
            s = scores[h, at, :]
            hit = row_iota == target - i * step
            e = jnp.exp2((s - m) * K)
            scores[h, at, :] = e
            return l8 + jnp.sum(fold(e), axis=0), t8 + jnp.sum(fold(jnp.where(hit, s, 0.0)), axis=0)

        zero = jnp.zeros((8, qd), jnp.float32)
        l8, t8 = lax.fori_loop(0, items // step, body, (zero, zero))
        stat[0, h, pl.ds(0, 1), :] = m
        stat[0, h, pl.ds(1, 1), :] = jnp.sum(l8, axis=0, keepdims=True)
        stat[0, h, pl.ds(2, 1), :] = jnp.sum(t8, axis=0, keepdims=True)
        stat[0, h, pl.ds(3, 5), :] = jnp.zeros((5, qd), jnp.float32)
        remote(stat.at[0, h], stat.at[1, h], pair_ssem.at[2 + h], pair_rsem.at[2 + h], partner).start()

    first_pass(1 - c)
    first_pass(c)

    def second_pass(h):
        remote(stat.at[0, h], stat.at[1, h], pair_ssem.at[2 + h], pair_rsem.at[2 + h], partner).wait()
        m, l, t = (stat[0, h, pl.ds(k, 1), :] for k in range(3))
        m2, l2, t2 = (stat[1, h, pl.ds(k, 1), :] for k in range(3))
        top = jnp.maximum(m, m2)
        mine = jnp.exp2((m - top) * K)
        total = l * mine + l2 * jnp.exp2((m2 - top) * K)
        valid = info[h, pl.ds(1, 1), :]
        weight = SHARPNESS * valid
        factor = weight * mine / total
        target = local_row(h)

        @pl.when(h == c)
        def _():
            loss_ref[...] = valid * (SHARPNESS * (top - (t + t2)) + jnp.log(total))

        def body(i):
            at = pl.ds(pl.multiple_of(i * step, 16), step)
            hit = row_iota == target - i * step
            g = scores[h, at, :] * factor - jnp.where(hit, weight, 0.0)
            grads[h, at, :] = g.astype(jnp.bfloat16)
        loop(0, items // step, body)

    def query_part(h):
        return lax.dot_general(grads[h], pool[...], (((0,), (0,)), ((), ())), preferred_element_type=jnp.float32)

    second_pass(1 - c)
    qpart[...] = query_part(1 - c)
    part_copy = remote(qpart, qland, pair_ssem.at[4], pair_rsem.at[4], partner)
    part_copy.start()
    second_pass(c)

    per = slab // yrows
    for dx in far_ring(X) + [0]:
        px = (x + dx) % X
        at = slab0(px)
        g = jnp.dot(grads[0, at, :], q_all[0], preferred_element_type=jnp.float32)
        g = g + jnp.dot(grads[1, at, :], q_all[1], preferred_element_type=jnp.float32)
        out_items[at, :] = g.astype(jnp.bfloat16)

        if dx:
            @pl.when(c == 0)
            def _():
                remote(out_items.at[at], in_items.at[slab0(x)], r1_ssem, r1_rsem, dev(px, y, z, 0)).start()

        @pl.when(jnp.logical_and(c == 1, px < X // 2))
        def _():
            for j in range(per):
                py = px * per + j

                @pl.when(py != y)
                def _():
                    remote(out_items.at[slab_y(py)], in_items.at[slab_y(y)], r1_ssem, r1_rsem, dev(x, py, z, 1)).start()

        @pl.when(jnp.logical_and(c == 1, px >= X // 2))
        def _():
            for j in range(per):
                pz = (px - X // 2) * per + j

                @pl.when(pz != z)
                def _():
                    remote(out_items.at[slab_z(pz)], in_items.at[slab_z(z)], r1_ssem, r1_rsem, dev(x, y, pz, 1)).start()

    scores[0, pl.ds(0, qd), :] = query_part(c)

    def spread(rows_sum, owners, first):
        n = owners * BLK
        pack[pl.ds(0, n), :] = jnp.zeros((n, 128), jnp.float32)
        for r in range(OWNED):
            for a in range(chunks):
                pack[pl.ds(a * OWNED + r, owners, stride=BLK), :] = \
                    rows_sum[r * owners:(r + 1) * owners, a * 128:(a + 1) * 128]
        pieces[pl.ds(first * BLK, n), :] = pack[pl.ds(0, n), :].astype(jnp.bfloat16)

    @pl.when(c == 0)
    def _():
        bytes_of(in_items.at[pl.ds(0, (X - 1) * slab)], r1_rsem).wait()
        total = out_items[slab0(x), :].astype(jnp.float32)
        for i in range(1, X):
            total = total + in_items[slab0((x + i) % X), :].astype(jnp.float32)
        acc[pl.ds(0, slab), :] = total
        spread(acc[pl.ds(0, slab), :], Y * Z, 0)
        me = y * Z + z
        land2[rows(me), :] = pieces[rows(me), :]

        for dy, dz in yz:
            py, pz = (y + dy) % Y, (z + dz) % Z
            remote(pieces.at[rows(py * Z + pz)], land2.at[rows(me)], r2_ssem, r2_rsem, dev(x, py, pz, 0)).start()

    @pl.when(c == 1)
    def _():
        bytes_of(in_items.at[pl.ds(0, (Y - 1) * yrows + (Z - 1) * zrows)], r1_rsem).wait()
        acc[pl.ds(0, yrows), :] = out_items[slab_y(y), :].astype(jnp.float32)
        acc[pl.ds(yrows, zrows), :] = out_items[slab_z(z), :].astype(jnp.float32)

        def one(i):
            acc[pl.ds(0, yrows), :] += in_items[slab_y((y + i) % Y), :].astype(jnp.float32)
        loop(1, Y, one)

        def two(i):
            acc[pl.ds(yrows, zrows), :] += in_items[slab_z((z + i) % Z), :].astype(jnp.float32)
        loop(1, Z, two)
        spread(acc[pl.ds(0, yrows), :], xz_own, 0)
        spread(acc[pl.ds(yrows, zrows), :], xy_own, xz_own)

        @pl.when(even)
        def _():
            land2[rows(x * Z + z), :] = pieces[rows((x // 2) * Z + z), :]

        @pl.when(jnp.logical_not(even))
        def _():
            land2[rows(x * Y + y), :] = pieces[rows(xz_own + (x // 2) * Y + y), :]

        def to_xz(dx, dz):
            px, pz = (x + dx) % X, (z + dz) % Z
            remote(pieces.at[rows((px // 2) * Z + pz)], land2.at[rows(x * Z + z)],
                   r2_ssem, r2_rsem, dev(px, y, pz, 1)).start()

        def to_xy(dx, dy):
            px, py = (x + dx) % X, (y + dy) % Y
            remote(pieces.at[rows(xz_own + (px // 2) * Y + py)], land2.at[rows(x * Y + y)],
                   r2_ssem, r2_rsem, dev(px, py, z, 1)).start()

        @pl.when(even)
        def _():
            for dx, dz in xz:
                if dx % 2 == 0:
                    to_xz(dx, dz)
            for dx, dy in xy:
                if dx % 2 == 1:
                    to_xy(dx, dy)

        @pl.when(jnp.logical_not(even))
        def _():
            for dx, dz in xz:
                if dx % 2 == 1:
                    to_xz(dx, dz)
            for dx, dy in xy:
                if dx % 2 == 0:
                    to_xy(dx, dy)

    part_copy.wait()
    qg_ref[...] = (scores[0, pl.ds(0, qd), :] + qland[...]).astype(jnp.bfloat16)
    results = [pltpu.make_async_copy(a, b, out_sem.at[k])
               for k, (a, b) in enumerate([(qg_ref, qg_hbm), (loss_ref, loss_hbm), (ig_ref, ig_hbm)])]
    results[0].start()
    results[1].start()

    @pl.when(c == 0)
    def _():
        bytes_of(land2.at[pl.ds(0, (Y * Z - 1) * BLK)], r2_rsem).wait()

    @pl.when(c == 1)
    def _():
        bytes_of(land2.at[pl.ds(0, (X * Z - 1) * BLK)], r2_rsem).wait()

    def gather(n):
        def body(i, carry):
            return carry + land2[rows(i), :].astype(jnp.float32)
        pack[pl.ds(0, BLK), :] = lax.fori_loop(0, n, body, jnp.zeros((BLK, 128), jnp.float32))

    @pl.when(c == 0)
    def _():
        gather(Y * Z)

    @pl.when(c == 1)
    def _():
        gather(X * Z)
    for a in range(chunks):
        ig_ref[:, a * 128:(a + 1) * 128] = pack[pl.ds(a * OWNED, OWNED), :]

    results[2].start()

    @pl.when(c == 0)
    def _():
        bytes_of(land.at[pl.ds(0, (Y * Z - 1) * BLK)], s1_ssem).wait()
        bytes_of(pool.at[pl.ds(0, (X - 1) * slab)], s2_ssem).wait()
        bytes_of(pool.at[pl.ds(0, (X - 1) * slab)], r1_ssem).wait()
        bytes_of(land2.at[pl.ds(0, (Y * Z - 1) * BLK)], r2_ssem).wait()

    @pl.when(c == 1)
    def _():
        bytes_of(land.at[pl.ds(0, (X * Z - 1) * BLK)], s1_ssem).wait()
        bytes_of(pool.at[pl.ds(0, (Y - 1) * yrows + (Z - 1) * zrows)], s2_ssem).wait()
        bytes_of(pool.at[pl.ds(0, (Y - 1) * yrows + (Z - 1) * zrows)], r1_ssem).wait()
        bytes_of(land2.at[pl.ds(0, (X * Z - 1) * BLK)], r2_ssem).wait()
    for result in results:
        result.wait()


def leave(qg, ig, loss, qg_out, ig_out, loss_out, sem):
    copies = [pltpu.make_async_copy(a, b, sem.at[k])
              for k, (a, b) in enumerate([(qg, qg_out), (ig, ig_out), (loss, loss_out)])]
    for copy in copies:
        copy.start()
    for copy in copies:
        copy.wait()


def solution(mesh):
    X = mesh.shape["wide"] // ZHI

    def body(queries, targets, lengths, contrast_items):
        qd, width = queries.shape
        zlo = 4 if mesh.shape["narrow"] == 64 else 1
        Y = mesh.shape["narrow"] // (2 * zlo)
        Z = zlo * ZHI
        items = X * Y * Z * OWNED
        blocks = max(Y * Z, X * Z, X * Y) * BLK
        anywhere = pl.BlockSpec(memory_space=pl.ANY)
        f32, bf16 = jnp.float32, jnp.bfloat16
        outs = (
            jax.ShapeDtypeStruct((qd, width), bf16),
            jax.ShapeDtypeStruct((OWNED, width), f32),
            jax.ShapeDtypeStruct((1, qd), f32),
        )
        qg, ig, loss = pl.pallas_call(
            functools.partial(kernel, X, Y, Z),
            out_shape=outs,
            in_specs=[anywhere] * 4,
            out_specs=(anywhere,) * 3,
            scratch_shapes=[
                pltpu.VMEM((1, qd), jnp.int32),
                pltpu.SMEM(lengths.shape, jnp.int32),
                pltpu.VMEM((OWNED, width), bf16),
                *[pltpu.VMEM(o.shape, o.dtype) for o in outs],
                pltpu.VMEM((2, qd, width), bf16),
                pltpu.VMEM((2, 8, qd), f32),
                pltpu.VMEM((2, 2, 8, qd), f32),
                pltpu.VMEM((items, width), bf16),
                pltpu.VMEM((blocks, 128), f32),
                pltpu.VMEM((BLK, 128), bf16),
                pltpu.VMEM((blocks, 128), bf16),
                pltpu.VMEM((2, max(items, qd), qd), f32),
                pltpu.VMEM((2, items, qd), bf16),
                pltpu.VMEM((items, width), bf16),
                pltpu.VMEM((items, width), bf16),
                pltpu.VMEM((items // X, width), f32),
                pltpu.VMEM((blocks, 128), bf16),
                pltpu.VMEM((blocks, 128), bf16),
                pltpu.VMEM((qd, width), f32),
                pltpu.VMEM((qd, width), f32),
                pltpu.SemaphoreType.DMA,
                pltpu.SemaphoreType.DMA((3,)),
                pltpu.SemaphoreType.DMA((3,)),
                pltpu.SemaphoreType.DMA((5,)),
                pltpu.SemaphoreType.DMA((5,)),
                *[pltpu.SemaphoreType.DMA] * 8,
            ],
            compiler_params=pltpu.CompilerParams(
                collective_id=0, has_side_effects=True, vmem_limit_bytes=60 << 20),
        )(queries, targets.reshape(1, qd), lengths, contrast_items)
        qg, ig, loss = pl.pallas_call(
            leave, out_shape=outs, in_specs=[anywhere] * 3, out_specs=(anywhere,) * 3,
            scratch_shapes=[pltpu.SemaphoreType.DMA((3,))],
            compiler_params=pltpu.CompilerParams(vmem_limit_bytes=60 << 20),
        )(qg, ig, loss)
        return qg, ig, loss.reshape(qd)

    rows = P(("wide", "narrow"), None)
    flat = P(("wide", "narrow"))
    return jax.shard_map(
        body, mesh=mesh, in_specs=(rows, flat, flat, rows), out_specs=(rows, rows, flat), check_vma=False)
```

```python
import functools

import jax
import jax.numpy as jnp
from jax import lax
from jax.experimental import pallas as pl
from jax.experimental.pallas import tpu as pltpu
from jax.sharding import PartitionSpec as P

MESH = pl.DeviceIdType.MESH
SEQ_LEN = 256
SHARPNESS = 20.0
LOG2E = 1.4426950408889634
ZHI = 2
OWNED = 3
BLK = 16


def hops(d, n):
    return min(d % n, -d % n)


def far_first(A, B):
    offsets = [(a, b) for a in range(A) for b in range(B) if a or b]
    return sorted(offsets, key=lambda o: -hops(o[0], A) - hops(o[1], B))


def far_ring(n):
    return sorted(range(1, n), key=lambda d: -hops(d, n))


def kernel(X, Y, Z, q_hbm, tgt_hbm, len_hbm, it_hbm, qg_hbm, ig_hbm, loss_hbm,
           tgt_ref, len_ref, it_ref, qg_ref, ig_ref, loss_ref, q_all, info, stat, pool, pack, blk, land, scores, grads, out_items, in_items,
           acc, pieces, land2, qpart, qland,
           q_sem, in_sem, out_sem, pair_ssem, pair_rsem, s1_ssem, s1_rsem, s2_ssem, s2_rsem,
           r1_ssem, r1_rsem, r2_ssem, r2_rsem):
    zlo = Z // ZHI
    wide, narrow = lax.axis_index("wide"), lax.axis_index("narrow")
    x, c = wide // ZHI, narrow % 2
    y, z = (narrow // 2) % Y, (wide % ZHI) * zlo + narrow // (2 * Y)
    qd, width = q_hbm.shape
    chunks = width // 128
    slab = Y * Z * OWNED
    half = X * slab // 2
    yrows, zrows = half // Y, half // Z
    items = X * slab
    even = x % 2 == 0

    def dev(px, py, pz, pc):
        return (px * ZHI + pz // zlo, ((pz % zlo) * Y + py) * 2 + pc)

    yz, xz, xy = far_first(Y, Z), far_first(X, Z), far_first(X, Y)

    def remote(src, dst, ssem, rsem, to):
        return pltpu.make_async_remote_copy(
            src_ref=src, dst_ref=dst, send_sem=ssem, recv_sem=rsem, device_id=to, device_id_type=MESH)

    def bytes_of(ref, sem):
        return pltpu.make_async_copy(ref, ref, sem)

    def loop(lo, hi, f):
        def step(i, carry):
            f(i)
            return carry
        lax.fori_loop(lo, hi, step, 0)

    loads = [pltpu.make_async_copy(a, b, in_sem.at[k])
             for k, (a, b) in enumerate([(it_hbm, it_ref), (tgt_hbm, tgt_ref), (len_hbm, len_ref)])]
    load_q = pltpu.make_async_copy(q_hbm, q_all.at[c], q_sem)
    for load in loads:
        load.start()
    load_q.start()

    barrier = pltpu.get_barrier_semaphore()
    partner = dev(x, y, z, 1 - c)

    def greet(to):
        pl.semaphore_signal(barrier, inc=1, device_id=to, device_id_type=MESH)

    @pl.when(c == 0)
    def _():
        for dy, dz in yz:
            greet(dev(x, (y + dy) % Y, (z + dz) % Z, 0))
        for dx in far_ring(X):
            greet(dev((x + dx) % X, y, z, 0))

    @pl.when(c == 1)
    def _():
        for dx, dz in xz:
            greet(dev((x + dx) % X, y, (z + dz) % Z, 1))
        for dx, dy in xy:
            greet(dev((x + dx) % X, (y + dy) % Y, z, 1))

    greet(partner)

    loads[0].wait()
    own = it_ref[...].astype(jnp.float32)
    pack[pl.ds(0, BLK), :] = jnp.zeros((BLK, 128), jnp.float32)
    for a in range(chunks):
        pack[pl.ds(a * OWNED, OWNED), :] = own[:, a * 128:(a + 1) * 128]
    blk[...] = pack[pl.ds(0, BLK), :].astype(jnp.bfloat16)

    loads[1].wait()
    loads[2].wait()
    pos = lax.broadcasted_iota(jnp.int32, (1, qd), 1)
    live = jnp.where(pos < SEQ_LEN, (pos < len_ref[0]).astype(jnp.float32),
                     (pos - SEQ_LEN < len_ref[1]).astype(jnp.float32))
    info[c, pl.ds(0, 1), :] = tgt_ref[...].astype(jnp.float32)
    info[c, pl.ds(1, 1), :] = live
    info[c, pl.ds(2, 6), :] = jnp.zeros((6, qd), jnp.float32)
    load_q.wait()

    @pl.when(c == 0)
    def _():
        pl.semaphore_wait(barrier, Y * Z - 1 + X - 1 + 1)

    @pl.when(c == 1)
    def _():
        pl.semaphore_wait(barrier, X * Z - 1 + X * Y - 1 + 1)

    def rows(i):
        return pl.ds(pl.multiple_of(i * BLK, BLK), BLK)

    @pl.when(c == 0)
    def _():
        me = y * Z + z
        land[rows(me), :] = blk[...]

        for dy, dz in yz:
            remote(blk, land.at[rows(me)], s1_ssem, s1_rsem, dev(x, (y + dy) % Y, (z + dz) % Z, 0)).start()

    @pl.when(jnp.logical_and(c == 1, even))
    def _():
        me = (x // 2) * Z + z
        land[rows(me), :] = blk[...]

        for dx, dz in xz:
            remote(blk, land.at[rows(me)], s1_ssem, s1_rsem, dev((x + dx) % X, y, (z + dz) % Z, 1)).start()

    @pl.when(jnp.logical_and(c == 1, jnp.logical_not(even)))
    def _():
        me = X // 2 * Z + (x // 2) * Y + y
        land[rows(me), :] = blk[...]

        for dx, dy in xy:
            remote(blk, land.at[rows(me)], s1_ssem, s1_rsem, dev((x + dx) % X, (y + dy) % Y, z, 1)).start()

    q_copy = remote(q_all.at[c], q_all.at[c], pair_ssem.at[0], pair_rsem.at[0], partner)
    q_copy.start()
    info_copy = remote(info.at[c], info.at[c], pair_ssem.at[1], pair_rsem.at[1], partner)
    info_copy.start()

    @pl.when(c == 0)
    def _():
        bytes_of(land.at[pl.ds(0, (Y * Z - 1) * BLK)], s1_rsem).wait()

    @pl.when(c == 1)
    def _():
        bytes_of(land.at[pl.ds(0, (X * Z - 1) * BLK)], s1_rsem).wait()

    def unpack(first, owners, base):
        n = owners * BLK
        pack[pl.ds(0, n), :] = land[pl.ds(first * BLK, n), :].astype(jnp.float32)
        for r in range(OWNED):
            for a in range(chunks):
                piece = pack[pl.ds(a * OWNED + r, owners, stride=BLK), :]
                at = base + r * owners
                pool[pl.ds(pl.multiple_of(at, 16), owners), a * 128:(a + 1) * 128] = piece.astype(jnp.bfloat16)

    xz_own, xy_own = X // 2 * Z, X // 2 * Y

    def slab0(px):
        return pl.ds(pl.multiple_of(px * slab, 16), slab)

    def slab_y(py):
        return pl.ds(pl.multiple_of(py * yrows, 16), yrows)

    def slab_z(pz):
        return pl.ds(pl.multiple_of(half + pz * zrows, 16), zrows)

    @pl.when(c == 0)
    def _():
        unpack(0, Y * Z, x * slab)

        for dx in far_ring(X):
            remote(pool.at[slab0(x)], pool.at[slab0(x)], s2_ssem, s2_rsem, dev((x + dx) % X, y, z, 0)).start()
        bytes_of(pool.at[pl.ds(0, (X - 1) * slab)], s2_rsem).wait()

    @pl.when(c == 1)
    def _():
        unpack(0, xz_own, y * yrows)

        for dy in far_ring(Y):
            remote(pool.at[slab_y(y)], pool.at[slab_y(y)], s2_ssem, s2_rsem, dev(x, (y + dy) % Y, z, 1)).start()
        unpack(xz_own, xy_own, half + z * zrows)

        for dz in far_ring(Z):
            remote(pool.at[slab_z(z)], pool.at[slab_z(z)], s2_ssem, s2_rsem, dev(x, y, (z + dz) % Z, 1)).start()
        bytes_of(pool.at[pl.ds(0, (Y - 1) * yrows + (Z - 1) * zrows)], s2_rsem).wait()

    q_copy.wait()
    info_copy.wait()

    def local_row(h):
        t = info[h, pl.ds(0, 1), :].astype(jnp.int32)
        o = (t * 21846) >> 16
        r = t - o * OWNED
        w, n = o // (zlo * Y * 2), o % (zlo * Y * 2)
        tx, tc = w // ZHI, n % 2
        ty, tz = (n // 2) % Y, (w % ZHI) * zlo + n // (2 * Y)
        on0 = tx * slab + r * (Y * Z) + ty * Z + tz
        on1 = jnp.where(tx % 2 == 0, ty * yrows + r * xz_own + (tx // 2) * Z + tz,
                        half + tz * zrows + r * xy_own + (tx // 2) * Y + ty)
        return jnp.where(tc == c, jnp.where(tc == 0, on0, on1), -1)

    tile = items // 3
    step = max(8, items // 12)
    fold = functools.partial(jnp.reshape, shape=(step // 8, 8, qd))
    row_iota = lax.broadcasted_iota(jnp.int32, (step, qd), 0)
    K = SHARPNESS * LOG2E

    def first_pass(h):
        m8 = jnp.full((8, qd), -3e38, jnp.float32)
        for i in range(3):
            s = lax.dot_general(pool[pl.ds(i * tile, tile), :], q_all[h], (((1,), (1,)), ((), ())),
                                preferred_element_type=jnp.float32)
            scores[h, pl.ds(i * tile, tile), :] = s
            m8 = jnp.maximum(m8, jnp.max(s.reshape(tile // 8, 8, qd), axis=0))
        m = jnp.max(m8, axis=0, keepdims=True)
        target = local_row(h)

        def body(i, carry):
            l8, t8 = carry
            at = pl.ds(pl.multiple_of(i * step, 8), step)
            s = scores[h, at, :]
            hit = row_iota == target - i * step
            e = jnp.exp2((s - m) * K)
            scores[h, at, :] = e
            return l8 + jnp.sum(fold(e), axis=0), t8 + jnp.sum(fold(jnp.where(hit, s, 0.0)), axis=0)

        zero = jnp.zeros((8, qd), jnp.float32)
        l8, t8 = lax.fori_loop(0, items // step, body, (zero, zero))
        stat[0, h, pl.ds(0, 1), :] = m
        stat[0, h, pl.ds(1, 1), :] = jnp.sum(l8, axis=0, keepdims=True)
        stat[0, h, pl.ds(2, 1), :] = jnp.sum(t8, axis=0, keepdims=True)
        stat[0, h, pl.ds(3, 5), :] = jnp.zeros((5, qd), jnp.float32)
        remote(stat.at[0, h], stat.at[1, h], pair_ssem.at[2 + h], pair_rsem.at[2 + h], partner).start()

    first_pass(1 - c)
    first_pass(c)

    def second_pass(h):
        remote(stat.at[0, h], stat.at[1, h], pair_ssem.at[2 + h], pair_rsem.at[2 + h], partner).wait()
        m, l, t = (stat[0, h, pl.ds(k, 1), :] for k in range(3))
        m2, l2, t2 = (stat[1, h, pl.ds(k, 1), :] for k in range(3))
        top = jnp.maximum(m, m2)
        mine = jnp.exp2((m - top) * K)
        total = l * mine + l2 * jnp.exp2((m2 - top) * K)
        valid = info[h, pl.ds(1, 1), :]
        weight = SHARPNESS * valid
        factor = weight * mine / total
        target = local_row(h)

        @pl.when(h == c)
        def _():
            loss_ref[...] = valid * (SHARPNESS * (top - (t + t2)) + jnp.log(total))

        def body(i):
            at = pl.ds(pl.multiple_of(i * step, 16), step)
            hit = row_iota == target - i * step
            g = scores[h, at, :] * factor - jnp.where(hit, weight, 0.0)
            grads[h, at, :] = g.astype(jnp.bfloat16)
        loop(0, items // step, body)

    def query_part(h):
        return lax.dot_general(grads[h], pool[...], (((0,), (0,)), ((), ())), preferred_element_type=jnp.float32)

    second_pass(1 - c)
    qpart[...] = query_part(1 - c)
    part_copy = remote(qpart, qland, pair_ssem.at[4], pair_rsem.at[4], partner)
    part_copy.start()
    second_pass(c)

    per = slab // yrows
    for dx in far_ring(X) + [0]:
        px = (x + dx) % X
        at = slab0(px)
        g = jnp.dot(grads[0, at, :], q_all[0], preferred_element_type=jnp.float32)
        g = g + jnp.dot(grads[1, at, :], q_all[1], preferred_element_type=jnp.float32)
        out_items[at, :] = g.astype(jnp.bfloat16)

        if dx:
            @pl.when(c == 0)
            def _():
                remote(out_items.at[at], in_items.at[slab0(x)], r1_ssem, r1_rsem, dev(px, y, z, 0)).start()

        @pl.when(jnp.logical_and(c == 1, px < X // 2))
        def _():
            for j in range(per):
                py = px * per + j

                @pl.when(py != y)
                def _():
                    remote(out_items.at[slab_y(py)], in_items.at[slab_y(y)], r1_ssem, r1_rsem, dev(x, py, z, 1)).start()

        @pl.when(jnp.logical_and(c == 1, px >= X // 2))
        def _():
            for j in range(per):
                pz = (px - X // 2) * per + j

                @pl.when(pz != z)
                def _():
                    remote(out_items.at[slab_z(pz)], in_items.at[slab_z(z)], r1_ssem, r1_rsem, dev(x, y, pz, 1)).start()

    scores[0, pl.ds(0, qd), :] = query_part(c)

    def spread(rows_sum, owners, first):
        n = owners * BLK
        pack[pl.ds(0, n), :] = jnp.zeros((n, 128), jnp.float32)
        for r in range(OWNED):
            for a in range(chunks):
                pack[pl.ds(a * OWNED + r, owners, stride=BLK), :] = \
                    rows_sum[r * owners:(r + 1) * owners, a * 128:(a + 1) * 128]
        pieces[pl.ds(first * BLK, n), :] = pack[pl.ds(0, n), :].astype(jnp.bfloat16)

    @pl.when(c == 0)
    def _():
        bytes_of(in_items.at[pl.ds(0, (X - 1) * slab)], r1_rsem).wait()
        total = out_items[slab0(x), :].astype(jnp.float32)
        for i in range(1, X):
            total = total + in_items[slab0((x + i) % X), :].astype(jnp.float32)
        acc[pl.ds(0, slab), :] = total
        spread(acc[pl.ds(0, slab), :], Y * Z, 0)
        me = y * Z + z
        land2[rows(me), :] = pieces[rows(me), :]

        for dy, dz in yz:
            py, pz = (y + dy) % Y, (z + dz) % Z
            remote(pieces.at[rows(py * Z + pz)], land2.at[rows(me)], r2_ssem, r2_rsem, dev(x, py, pz, 0)).start()

    @pl.when(c == 1)
    def _():
        bytes_of(in_items.at[pl.ds(0, (Y - 1) * yrows + (Z - 1) * zrows)], r1_rsem).wait()
        acc[pl.ds(0, yrows), :] = out_items[slab_y(y), :].astype(jnp.float32)
        acc[pl.ds(yrows, zrows), :] = out_items[slab_z(z), :].astype(jnp.float32)

        def one(i):
            acc[pl.ds(0, yrows), :] += in_items[slab_y((y + i) % Y), :].astype(jnp.float32)
        loop(1, Y, one)

        def two(i):
            acc[pl.ds(yrows, zrows), :] += in_items[slab_z((z + i) % Z), :].astype(jnp.float32)
        loop(1, Z, two)
        spread(acc[pl.ds(0, yrows), :], xz_own, 0)
        spread(acc[pl.ds(yrows, zrows), :], xy_own, xz_own)

        @pl.when(even)
        def _():
            land2[rows(x * Z + z), :] = pieces[rows((x // 2) * Z + z), :]

        @pl.when(jnp.logical_not(even))
        def _():
            land2[rows(x * Y + y), :] = pieces[rows(xz_own + (x // 2) * Y + y), :]

        def to_xz(dx, dz):
            px, pz = (x + dx) % X, (z + dz) % Z
            remote(pieces.at[rows((px // 2) * Z + pz)], land2.at[rows(x * Z + z)],
                   r2_ssem, r2_rsem, dev(px, y, pz, 1)).start()

        def to_xy(dx, dy):
            px, py = (x + dx) % X, (y + dy) % Y
            remote(pieces.at[rows(xz_own + (px // 2) * Y + py)], land2.at[rows(x * Y + y)],
                   r2_ssem, r2_rsem, dev(px, py, z, 1)).start()

        @pl.when(even)
        def _():
            for dx, dz in xz:
                if dx % 2 == 0:
                    to_xz(dx, dz)
            for dx, dy in xy:
                if dx % 2 == 1:
                    to_xy(dx, dy)

        @pl.when(jnp.logical_not(even))
        def _():
            for dx, dz in xz:
                if dx % 2 == 1:
                    to_xz(dx, dz)
            for dx, dy in xy:
                if dx % 2 == 0:
                    to_xy(dx, dy)

    part_copy.wait()
    qg_ref[...] = (scores[0, pl.ds(0, qd), :] + qland[...]).astype(jnp.bfloat16)
    results = [pltpu.make_async_copy(a, b, out_sem.at[k])
               for k, (a, b) in enumerate([(qg_ref, qg_hbm), (loss_ref, loss_hbm), (ig_ref, ig_hbm)])]
    results[0].start()
    results[1].start()

    @pl.when(c == 0)
    def _():
        bytes_of(land2.at[pl.ds(0, (Y * Z - 1) * BLK)], r2_rsem).wait()

    @pl.when(c == 1)
    def _():
        bytes_of(land2.at[pl.ds(0, (X * Z - 1) * BLK)], r2_rsem).wait()

    def gather(n):
        def body(i, carry):
            return carry + land2[rows(i), :].astype(jnp.float32)
        pack[pl.ds(0, BLK), :] = lax.fori_loop(0, n, body, jnp.zeros((BLK, 128), jnp.float32))

    @pl.when(c == 0)
    def _():
        gather(Y * Z)

    @pl.when(c == 1)
    def _():
        gather(X * Z)
    for a in range(chunks):
        ig_ref[:, a * 128:(a + 1) * 128] = pack[pl.ds(a * OWNED, OWNED), :]

    results[2].start()

    @pl.when(c == 0)
    def _():
        bytes_of(land.at[pl.ds(0, (Y * Z - 1) * BLK)], s1_ssem).wait()
        bytes_of(pool.at[pl.ds(0, (X - 1) * slab)], s2_ssem).wait()
        bytes_of(pool.at[pl.ds(0, (X - 1) * slab)], r1_ssem).wait()
        bytes_of(land2.at[pl.ds(0, (Y * Z - 1) * BLK)], r2_ssem).wait()

    @pl.when(c == 1)
    def _():
        bytes_of(land.at[pl.ds(0, (X * Z - 1) * BLK)], s1_ssem).wait()
        bytes_of(pool.at[pl.ds(0, (Y - 1) * yrows + (Z - 1) * zrows)], s2_ssem).wait()
        bytes_of(pool.at[pl.ds(0, (Y - 1) * yrows + (Z - 1) * zrows)], r1_ssem).wait()
        bytes_of(land2.at[pl.ds(0, (X * Z - 1) * BLK)], r2_ssem).wait()
    for result in results:
        result.wait()


def leave(qg, ig, loss, qg_out, ig_out, loss_out, qg_v, ig_v, loss_v, in_sem, out_sem):
    n = qg.shape[0] // 4
    legs = [(qg.at[pl.ds(i * n, n)], qg_v.at[pl.ds(i * n, n)], qg_out.at[pl.ds(i * n, n)]) for i in range(4)]
    legs += [(ig, ig_v, ig_out), (loss, loss_v, loss_out)]
    ins = [pltpu.make_async_copy(a, b, in_sem.at[k]) for k, (a, b, _) in enumerate(legs)]
    outs = [pltpu.make_async_copy(b, d, out_sem.at[k]) for k, (_, b, d) in enumerate(legs)]
    for copy in ins:
        copy.start()
    for copy, after in zip(ins, outs):
        copy.wait()
        after.start()
    for copy in outs:
        copy.wait()


def solution(mesh):
    X = mesh.shape["wide"] // ZHI

    def body(queries, targets, lengths, contrast_items):
        qd, width = queries.shape
        zlo = 4 if mesh.shape["narrow"] == 64 else 1
        Y = mesh.shape["narrow"] // (2 * zlo)
        Z = zlo * ZHI
        items = X * Y * Z * OWNED
        blocks = max(Y * Z, X * Z, X * Y) * BLK
        anywhere = pl.BlockSpec(memory_space=pl.ANY)
        f32, bf16 = jnp.float32, jnp.bfloat16
        outs = (
            jax.ShapeDtypeStruct((qd, width), bf16),
            jax.ShapeDtypeStruct((OWNED, width), f32),
            jax.ShapeDtypeStruct((1, qd), f32),
        )
        qg, ig, loss = pl.pallas_call(
            functools.partial(kernel, X, Y, Z),
            out_shape=outs,
            in_specs=[anywhere] * 4,
            out_specs=(anywhere,) * 3,
            scratch_shapes=[
                pltpu.VMEM((1, qd), jnp.int32),
                pltpu.SMEM(lengths.shape, jnp.int32),
                pltpu.VMEM((OWNED, width), bf16),
                *[pltpu.VMEM(o.shape, o.dtype) for o in outs],
                pltpu.VMEM((2, qd, width), bf16),
                pltpu.VMEM((2, 8, qd), f32),
                pltpu.VMEM((2, 2, 8, qd), f32),
                pltpu.VMEM((items, width), bf16),
                pltpu.VMEM((blocks, 128), f32),
                pltpu.VMEM((BLK, 128), bf16),
                pltpu.VMEM((blocks, 128), bf16),
                pltpu.VMEM((2, max(items, qd), qd), f32),
                pltpu.VMEM((2, items, qd), bf16),
                pltpu.VMEM((items, width), bf16),
                pltpu.VMEM((items, width), bf16),
                pltpu.VMEM((items // X, width), f32),
                pltpu.VMEM((blocks, 128), bf16),
                pltpu.VMEM((blocks, 128), bf16),
                pltpu.VMEM((qd, width), f32),
                pltpu.VMEM((qd, width), f32),
                pltpu.SemaphoreType.DMA,
                pltpu.SemaphoreType.DMA((3,)),
                pltpu.SemaphoreType.DMA((3,)),
                pltpu.SemaphoreType.DMA((5,)),
                pltpu.SemaphoreType.DMA((5,)),
                *[pltpu.SemaphoreType.DMA] * 8,
            ],
            compiler_params=pltpu.CompilerParams(
                collective_id=0, has_side_effects=True, vmem_limit_bytes=60 << 20),
        )(queries, targets.reshape(1, qd), lengths, contrast_items)
        qg, ig, loss = pl.pallas_call(
            leave, out_shape=outs, in_specs=[anywhere] * 3, out_specs=(anywhere,) * 3,
            scratch_shapes=[
                *[pltpu.VMEM(o.shape, o.dtype) for o in outs],
                pltpu.SemaphoreType.DMA((6,)),
                pltpu.SemaphoreType.DMA((6,)),
            ],
            compiler_params=pltpu.CompilerParams(vmem_limit_bytes=60 << 20),
        )(qg, ig, loss)
        return qg, ig, loss.reshape(qd)

    rows = P(("wide", "narrow"), None)
    flat = P(("wide", "narrow"))
    return jax.shard_map(
        body, mesh=mesh, in_specs=(rows, flat, flat, rows), out_specs=(rows, rows, flat), check_vma=False)
```

```python
import functools

import jax
import jax.numpy as jnp
from jax import lax
from jax.experimental import pallas as pl
from jax.experimental.pallas import tpu as pltpu
from jax.sharding import PartitionSpec as P

MESH = pl.DeviceIdType.MESH
SEQ_LEN = 256
SHARPNESS = 20.0
LOG2E = 1.4426950408889634
ZHI = 2
OWNED = 3
BLK = 16


def hops(d, n):
    return min(d % n, -d % n)


def far_first(A, B):
    offsets = [(a, b) for a in range(A) for b in range(B) if a or b]
    return sorted(offsets, key=lambda o: -hops(o[0], A) - hops(o[1], B))


def far_ring(n):
    return sorted(range(1, n), key=lambda d: -hops(d, n))


def kernel(X, Y, Z, q_hbm, tgt_hbm, len_hbm, it_hbm, qg_hbm, loss_hbm, land2,
           tgt_ref, len_ref, it_ref, qg_ref, loss_ref, q_all, info, stat, pool, pack, blk, land, scores, grads, out_items, in_items,
           acc, pieces, qpart, qland,
           q_sem, in_sem, out_sem, pair_ssem, pair_rsem, s1_ssem, s1_rsem, s2_ssem, s2_rsem,
           r1_ssem, r1_rsem, r2_ssem, r2_rsem):
    zlo = Z // ZHI
    wide, narrow = lax.axis_index("wide"), lax.axis_index("narrow")
    x, c = wide // ZHI, narrow % 2
    y, z = (narrow // 2) % Y, (wide % ZHI) * zlo + narrow // (2 * Y)
    qd, width = q_hbm.shape
    chunks = width // 128
    slab = Y * Z * OWNED
    half = X * slab // 2
    yrows, zrows = half // Y, half // Z
    items = X * slab
    even = x % 2 == 0

    def dev(px, py, pz, pc):
        return (px * ZHI + pz // zlo, ((pz % zlo) * Y + py) * 2 + pc)

    yz, xz, xy = far_first(Y, Z), far_first(X, Z), far_first(X, Y)

    def remote(src, dst, ssem, rsem, to):
        return pltpu.make_async_remote_copy(
            src_ref=src, dst_ref=dst, send_sem=ssem, recv_sem=rsem, device_id=to, device_id_type=MESH)

    def bytes_of(ref, sem):
        return pltpu.make_async_copy(ref, ref, sem)

    def loop(lo, hi, f):
        def step(i, carry):
            f(i)
            return carry
        lax.fori_loop(lo, hi, step, 0)

    loads = [pltpu.make_async_copy(a, b, in_sem.at[k])
             for k, (a, b) in enumerate([(it_hbm, it_ref), (tgt_hbm, tgt_ref), (len_hbm, len_ref)])]
    load_q = pltpu.make_async_copy(q_hbm, q_all.at[c], q_sem)
    for load in loads:
        load.start()
    load_q.start()

    barrier = pltpu.get_barrier_semaphore()
    partner = dev(x, y, z, 1 - c)

    def greet(to):
        pl.semaphore_signal(barrier, inc=1, device_id=to, device_id_type=MESH)

    @pl.when(c == 0)
    def _():
        for dy, dz in yz:
            greet(dev(x, (y + dy) % Y, (z + dz) % Z, 0))
        for dx in far_ring(X):
            greet(dev((x + dx) % X, y, z, 0))

    @pl.when(c == 1)
    def _():
        for dx, dz in xz:
            greet(dev((x + dx) % X, y, (z + dz) % Z, 1))
        for dx, dy in xy:
            greet(dev((x + dx) % X, (y + dy) % Y, z, 1))

    greet(partner)

    loads[0].wait()
    own = it_ref[...].astype(jnp.float32)
    pack[pl.ds(0, BLK), :] = jnp.zeros((BLK, 128), jnp.float32)
    for a in range(chunks):
        pack[pl.ds(a * OWNED, OWNED), :] = own[:, a * 128:(a + 1) * 128]
    blk[...] = pack[pl.ds(0, BLK), :].astype(jnp.bfloat16)

    loads[1].wait()
    loads[2].wait()
    pos = lax.broadcasted_iota(jnp.int32, (1, qd), 1)
    live = jnp.where(pos < SEQ_LEN, (pos < len_ref[0]).astype(jnp.float32),
                     (pos - SEQ_LEN < len_ref[1]).astype(jnp.float32))
    info[c, pl.ds(0, 1), :] = tgt_ref[...].astype(jnp.float32)
    info[c, pl.ds(1, 1), :] = live
    info[c, pl.ds(2, 6), :] = jnp.zeros((6, qd), jnp.float32)
    load_q.wait()

    @pl.when(c == 0)
    def _():
        pl.semaphore_wait(barrier, Y * Z - 1 + X - 1 + 1)

    @pl.when(c == 1)
    def _():
        pl.semaphore_wait(barrier, X * Z - 1 + X * Y - 1 + 1)

    def rows(i):
        return pl.ds(pl.multiple_of(i * BLK, BLK), BLK)

    @pl.when(c == 0)
    def _():
        me = y * Z + z
        land[rows(me), :] = blk[...]

        for dy, dz in yz:
            remote(blk, land.at[rows(me)], s1_ssem, s1_rsem, dev(x, (y + dy) % Y, (z + dz) % Z, 0)).start()

    @pl.when(jnp.logical_and(c == 1, even))
    def _():
        me = (x // 2) * Z + z
        land[rows(me), :] = blk[...]

        for dx, dz in xz:
            remote(blk, land.at[rows(me)], s1_ssem, s1_rsem, dev((x + dx) % X, y, (z + dz) % Z, 1)).start()

    @pl.when(jnp.logical_and(c == 1, jnp.logical_not(even)))
    def _():
        me = X // 2 * Z + (x // 2) * Y + y
        land[rows(me), :] = blk[...]

        for dx, dy in xy:
            remote(blk, land.at[rows(me)], s1_ssem, s1_rsem, dev((x + dx) % X, (y + dy) % Y, z, 1)).start()

    q_copy = remote(q_all.at[c], q_all.at[c], pair_ssem.at[0], pair_rsem.at[0], partner)
    q_copy.start()
    info_copy = remote(info.at[c], info.at[c], pair_ssem.at[1], pair_rsem.at[1], partner)
    info_copy.start()

    @pl.when(c == 0)
    def _():
        bytes_of(land.at[pl.ds(0, (Y * Z - 1) * BLK)], s1_rsem).wait()

    @pl.when(c == 1)
    def _():
        bytes_of(land.at[pl.ds(0, (X * Z - 1) * BLK)], s1_rsem).wait()

    def unpack(first, owners, base):
        n = owners * BLK
        pack[pl.ds(0, n), :] = land[pl.ds(first * BLK, n), :].astype(jnp.float32)
        for r in range(OWNED):
            for a in range(chunks):
                piece = pack[pl.ds(a * OWNED + r, owners, stride=BLK), :]
                at = base + r * owners
                pool[pl.ds(pl.multiple_of(at, 16), owners), a * 128:(a + 1) * 128] = piece.astype(jnp.bfloat16)

    xz_own, xy_own = X // 2 * Z, X // 2 * Y

    def slab0(px):
        return pl.ds(pl.multiple_of(px * slab, 16), slab)

    def slab_y(py):
        return pl.ds(pl.multiple_of(py * yrows, 16), yrows)

    def slab_z(pz):
        return pl.ds(pl.multiple_of(half + pz * zrows, 16), zrows)

    @pl.when(c == 0)
    def _():
        unpack(0, Y * Z, x * slab)

        for dx in far_ring(X):
            remote(pool.at[slab0(x)], pool.at[slab0(x)], s2_ssem, s2_rsem, dev((x + dx) % X, y, z, 0)).start()
        bytes_of(pool.at[pl.ds(0, (X - 1) * slab)], s2_rsem).wait()

    @pl.when(c == 1)
    def _():
        unpack(0, xz_own, y * yrows)

        for dy in far_ring(Y):
            remote(pool.at[slab_y(y)], pool.at[slab_y(y)], s2_ssem, s2_rsem, dev(x, (y + dy) % Y, z, 1)).start()
        unpack(xz_own, xy_own, half + z * zrows)

        for dz in far_ring(Z):
            remote(pool.at[slab_z(z)], pool.at[slab_z(z)], s2_ssem, s2_rsem, dev(x, y, (z + dz) % Z, 1)).start()
        bytes_of(pool.at[pl.ds(0, (Y - 1) * yrows + (Z - 1) * zrows)], s2_rsem).wait()

    q_copy.wait()
    info_copy.wait()

    def local_row(h):
        t = info[h, pl.ds(0, 1), :].astype(jnp.int32)
        o = (t * 21846) >> 16
        r = t - o * OWNED
        w, n = o // (zlo * Y * 2), o % (zlo * Y * 2)
        tx, tc = w // ZHI, n % 2
        ty, tz = (n // 2) % Y, (w % ZHI) * zlo + n // (2 * Y)
        on0 = tx * slab + r * (Y * Z) + ty * Z + tz
        on1 = jnp.where(tx % 2 == 0, ty * yrows + r * xz_own + (tx // 2) * Z + tz,
                        half + tz * zrows + r * xy_own + (tx // 2) * Y + ty)
        return jnp.where(tc == c, jnp.where(tc == 0, on0, on1), -1)

    tile = items // 3
    step = max(8, items // 12)
    fold = functools.partial(jnp.reshape, shape=(step // 8, 8, qd))
    row_iota = lax.broadcasted_iota(jnp.int32, (step, qd), 0)
    K = SHARPNESS * LOG2E

    def first_pass(h):
        m8 = jnp.full((8, qd), -3e38, jnp.float32)
        for i in range(3):
            s = lax.dot_general(pool[pl.ds(i * tile, tile), :], q_all[h], (((1,), (1,)), ((), ())),
                                preferred_element_type=jnp.float32)
            scores[h, pl.ds(i * tile, tile), :] = s
            m8 = jnp.maximum(m8, jnp.max(s.reshape(tile // 8, 8, qd), axis=0))
        m = jnp.max(m8, axis=0, keepdims=True)
        target = local_row(h)

        def body(i, carry):
            l8, t8 = carry
            at = pl.ds(pl.multiple_of(i * step, 8), step)
            s = scores[h, at, :]
            hit = row_iota == target - i * step
            e = jnp.exp2((s - m) * K)
            scores[h, at, :] = e
            return l8 + jnp.sum(fold(e), axis=0), t8 + jnp.sum(fold(jnp.where(hit, s, 0.0)), axis=0)

        zero = jnp.zeros((8, qd), jnp.float32)
        l8, t8 = lax.fori_loop(0, items // step, body, (zero, zero))
        stat[0, h, pl.ds(0, 1), :] = m
        stat[0, h, pl.ds(1, 1), :] = jnp.sum(l8, axis=0, keepdims=True)
        stat[0, h, pl.ds(2, 1), :] = jnp.sum(t8, axis=0, keepdims=True)
        stat[0, h, pl.ds(3, 5), :] = jnp.zeros((5, qd), jnp.float32)
        remote(stat.at[0, h], stat.at[1, h], pair_ssem.at[2 + h], pair_rsem.at[2 + h], partner).start()

    first_pass(1 - c)
    first_pass(c)

    def second_pass(h):
        remote(stat.at[0, h], stat.at[1, h], pair_ssem.at[2 + h], pair_rsem.at[2 + h], partner).wait()
        m, l, t = (stat[0, h, pl.ds(k, 1), :] for k in range(3))
        m2, l2, t2 = (stat[1, h, pl.ds(k, 1), :] for k in range(3))
        top = jnp.maximum(m, m2)
        mine = jnp.exp2((m - top) * K)
        total = l * mine + l2 * jnp.exp2((m2 - top) * K)
        valid = info[h, pl.ds(1, 1), :]
        weight = SHARPNESS * valid
        factor = weight * mine / total
        target = local_row(h)

        @pl.when(h == c)
        def _():
            loss_ref[...] = valid * (SHARPNESS * (top - (t + t2)) + jnp.log(total))

        def body(i):
            at = pl.ds(pl.multiple_of(i * step, 16), step)
            hit = row_iota == target - i * step
            g = scores[h, at, :] * factor - jnp.where(hit, weight, 0.0)
            grads[h, at, :] = g.astype(jnp.bfloat16)
        loop(0, items // step, body)

    def query_part(h):
        return lax.dot_general(grads[h], pool[...], (((0,), (0,)), ((), ())), preferred_element_type=jnp.float32)

    per, tiles = slab // yrows, X // 2
    order0 = [(x + dx) % X for dx in far_ring(X) + [0]]
    order1 = [p for k in range(1, tiles + 1)
              for p in ((y // per + k) % tiles, tiles + (z // per + k) % tiles)]
    order = [jnp.where(c == 0, p, q) for p, q in zip(order0, order1)]

    second_pass(1 - c)
    for px in order:
        at = slab0(px)
        scores[1 - c, at, :] = jnp.dot(grads[1 - c, at, :], q_all[1 - c], preferred_element_type=jnp.float32)
    second_pass(c)
    for k, px in enumerate(order):
        at = slab0(px)
        g = jnp.dot(grads[c, at, :], q_all[c], preferred_element_type=jnp.float32) + scores[1 - c, at, :]
        out_items[at, :] = g.astype(jnp.bfloat16)

        if k < X - 1:
            @pl.when(c == 0)
            def _():
                remote(out_items.at[at], in_items.at[slab0(x)], r1_ssem, r1_rsem, dev(px, y, z, 0)).start()

        @pl.when(c == 1)
        def _():
            for j in range(per):
                if k % 2 == 0:
                    py = px * per + j

                    @pl.when(py != y)
                    def _():
                        remote(out_items.at[slab_y(py)], in_items.at[slab_y(y)], r1_ssem, r1_rsem, dev(x, py, z, 1)).start()
                else:
                    pz = (px - tiles) * per + j

                    @pl.when(pz != z)
                    def _():
                        remote(out_items.at[slab_z(pz)], in_items.at[slab_z(z)], r1_ssem, r1_rsem, dev(x, y, pz, 1)).start()

    def query_part(h):
        return lax.dot_general(grads[h], pool[...], (((0,), (0,)), ((), ())), preferred_element_type=jnp.float32)

    qpart[...] = query_part(1 - c)
    part_copy = remote(qpart, qland, pair_ssem.at[4], pair_rsem.at[4], partner)
    part_copy.start()
    scores[0, pl.ds(0, qd), :] = query_part(c)

    def spread(rows_sum, owners, first):
        n = owners * BLK
        pack[pl.ds(0, n), :] = jnp.zeros((n, 128), jnp.float32)
        for r in range(OWNED):
            for a in range(chunks):
                pack[pl.ds(a * OWNED + r, owners, stride=BLK), :] = \
                    rows_sum[r * owners:(r + 1) * owners, a * 128:(a + 1) * 128]
        pieces[pl.ds(first * BLK, n), :] = pack[pl.ds(0, n), :].astype(jnp.bfloat16)

    @pl.when(c == 0)
    def _():
        bytes_of(in_items.at[pl.ds(0, (X - 1) * slab)], r1_rsem).wait()
        total = out_items[slab0(x), :].astype(jnp.float32)
        for i in range(1, X):
            total = total + in_items[slab0((x + i) % X), :].astype(jnp.float32)
        acc[pl.ds(0, slab), :] = total
        spread(acc[pl.ds(0, slab), :], Y * Z, 0)
        me = y * Z + z
        pltpu.make_async_copy(pieces.at[rows(me)], land2.at[rows(me)], out_sem.at[2]).start()

        for dy, dz in yz:
            py, pz = (y + dy) % Y, (z + dz) % Z
            remote(pieces.at[rows(py * Z + pz)], land2.at[rows(me)], r2_ssem, r2_rsem, dev(x, py, pz, 0)).start()

    @pl.when(c == 1)
    def _():
        bytes_of(in_items.at[pl.ds(0, (Y - 1) * yrows + (Z - 1) * zrows)], r1_rsem).wait()
        acc[pl.ds(0, yrows), :] = out_items[slab_y(y), :].astype(jnp.float32)
        acc[pl.ds(yrows, zrows), :] = out_items[slab_z(z), :].astype(jnp.float32)

        def one(i):
            acc[pl.ds(0, yrows), :] += in_items[slab_y((y + i) % Y), :].astype(jnp.float32)
        loop(1, Y, one)

        def two(i):
            acc[pl.ds(yrows, zrows), :] += in_items[slab_z((z + i) % Z), :].astype(jnp.float32)
        loop(1, Z, two)
        spread(acc[pl.ds(0, yrows), :], xz_own, 0)
        spread(acc[pl.ds(yrows, zrows), :], xy_own, xz_own)

        @pl.when(even)
        def _():
            pltpu.make_async_copy(pieces.at[rows((x // 2) * Z + z)], land2.at[rows(x * Z + z)], out_sem.at[2]).start()

        @pl.when(jnp.logical_not(even))
        def _():
            pltpu.make_async_copy(pieces.at[rows(xz_own + (x // 2) * Y + y)], land2.at[rows(x * Y + y)],
                                  out_sem.at[2]).start()

        def to_xz(dx, dz):
            px, pz = (x + dx) % X, (z + dz) % Z
            remote(pieces.at[rows((px // 2) * Z + pz)], land2.at[rows(x * Z + z)],
                   r2_ssem, r2_rsem, dev(px, y, pz, 1)).start()

        def to_xy(dx, dy):
            px, py = (x + dx) % X, (y + dy) % Y
            remote(pieces.at[rows(xz_own + (px // 2) * Y + py)], land2.at[rows(x * Y + y)],
                   r2_ssem, r2_rsem, dev(px, py, z, 1)).start()

        @pl.when(even)
        def _():
            for dx, dz in xz:
                if dx % 2 == 0:
                    to_xz(dx, dz)
            for dx, dy in xy:
                if dx % 2 == 1:
                    to_xy(dx, dy)

        @pl.when(jnp.logical_not(even))
        def _():
            for dx, dz in xz:
                if dx % 2 == 1:
                    to_xz(dx, dz)
            for dx, dy in xy:
                if dx % 2 == 0:
                    to_xy(dx, dy)

    part_copy.wait()
    qg_ref[...] = (scores[0, pl.ds(0, qd), :] + qland[...]).astype(jnp.bfloat16)
    results = [pltpu.make_async_copy(a, b, out_sem.at[k])
               for k, (a, b) in enumerate([(qg_ref, qg_hbm), (loss_ref, loss_hbm)])]
    for result in results:
        result.start()

    @pl.when(c == 0)
    def _():
        bytes_of(land2.at[pl.ds(0, (Y * Z - 1) * BLK)], r2_rsem).wait()

    @pl.when(c == 1)
    def _():
        bytes_of(land2.at[pl.ds(0, (X * Z - 1) * BLK)], r2_rsem).wait()

    @pl.when(c == 0)
    def _():
        bytes_of(land.at[pl.ds(0, (Y * Z - 1) * BLK)], s1_ssem).wait()
        bytes_of(pool.at[pl.ds(0, (X - 1) * slab)], s2_ssem).wait()
        bytes_of(pool.at[pl.ds(0, (X - 1) * slab)], r1_ssem).wait()
        bytes_of(land2.at[pl.ds(0, (Y * Z - 1) * BLK)], r2_ssem).wait()

    @pl.when(c == 1)
    def _():
        bytes_of(land.at[pl.ds(0, (X * Z - 1) * BLK)], s1_ssem).wait()
        bytes_of(pool.at[pl.ds(0, (Y - 1) * yrows + (Z - 1) * zrows)], s2_ssem).wait()
        bytes_of(pool.at[pl.ds(0, (Y - 1) * yrows + (Z - 1) * zrows)], r1_ssem).wait()
        bytes_of(land2.at[pl.ds(0, (X * Z - 1) * BLK)], r2_ssem).wait()
    bytes_of(pieces.at[pl.ds(0, BLK)], out_sem.at[2]).wait()
    for result in results:
        result.wait()


def finish(n0, n1, qg, loss, land2, qg_out, ig_out, loss_out, qg_v, ig_v, loss_v, land_v, total, in_sem, out_sem):
    n = qg.shape[0] // 4
    legs = [(qg.at[pl.ds(i * n, n)], qg_v.at[pl.ds(i * n, n)], qg_out.at[pl.ds(i * n, n)]) for i in range(4)]
    legs += [(loss, loss_v, loss_out)]
    land_in = pltpu.make_async_copy(land2, land_v, in_sem.at[5])
    land_in.start()
    ins = [pltpu.make_async_copy(a, b, in_sem.at[k]) for k, (a, b, _) in enumerate(legs)]
    outs = [pltpu.make_async_copy(b, d, out_sem.at[k]) for k, (_, b, d) in enumerate(legs)]
    for copy in ins:
        copy.start()
    land_in.wait()
    group = min(n0, n1, 8)

    def body(i, carry):
        part = land_v[pl.ds(pl.multiple_of(i * group * BLK, BLK), group * BLK), :].astype(jnp.float32)
        return carry + jnp.sum(part.reshape(group, BLK, 128), axis=0)

    count = jnp.where(lax.axis_index("narrow") % 2 == 0, n0 // group, n1 // group)
    total[...] = lax.fori_loop(0, count, body, jnp.zeros((BLK, 128), jnp.float32))
    for a in range(ig_v.shape[1] // 128):
        ig_v[:, a * 128:(a + 1) * 128] = total[pl.ds(a * OWNED, OWNED), :]
    ig_copy = pltpu.make_async_copy(ig_v, ig_out, out_sem.at[5])
    ig_copy.start()
    for copy, after in zip(ins, outs):
        copy.wait()
        after.start()
    for copy in outs:
        copy.wait()
    ig_copy.wait()


def solution(mesh):
    X = mesh.shape["wide"] // ZHI

    def body(queries, targets, lengths, contrast_items):
        qd, width = queries.shape
        zlo = 4 if mesh.shape["narrow"] == 64 else 1
        Y = mesh.shape["narrow"] // (2 * zlo)
        Z = zlo * ZHI
        items = X * Y * Z * OWNED
        blocks = max(Y * Z, X * Z, X * Y) * BLK
        anywhere = pl.BlockSpec(memory_space=pl.ANY)
        f32, bf16 = jnp.float32, jnp.bfloat16
        outs = (
            jax.ShapeDtypeStruct((qd, width), bf16),
            jax.ShapeDtypeStruct((OWNED, width), f32),
            jax.ShapeDtypeStruct((1, qd), f32),
        )
        qg, loss, land2 = pl.pallas_call(
            functools.partial(kernel, X, Y, Z),
            out_shape=(outs[0], outs[2], jax.ShapeDtypeStruct((blocks, 128), bf16)),
            in_specs=[anywhere] * 4,
            out_specs=(anywhere,) * 3,
            scratch_shapes=[
                pltpu.VMEM((1, qd), jnp.int32),
                pltpu.SMEM(lengths.shape, jnp.int32),
                pltpu.VMEM((OWNED, width), bf16),
                pltpu.VMEM((qd, width), bf16),
                pltpu.VMEM((1, qd), f32),
                pltpu.VMEM((2, qd, width), bf16),
                pltpu.VMEM((2, 8, qd), f32),
                pltpu.VMEM((2, 2, 8, qd), f32),
                pltpu.VMEM((items, width), bf16),
                pltpu.VMEM((blocks, 128), f32),
                pltpu.VMEM((BLK, 128), bf16),
                pltpu.VMEM((blocks, 128), bf16),
                pltpu.VMEM((2, max(items, qd), qd), f32),
                pltpu.VMEM((2, items, qd), bf16),
                pltpu.VMEM((items, width), bf16),
                pltpu.VMEM((items, width), bf16),
                pltpu.VMEM((items // X, width), f32),
                pltpu.VMEM((blocks, 128), bf16),
                pltpu.VMEM((qd, width), f32),
                pltpu.VMEM((qd, width), f32),
                pltpu.SemaphoreType.DMA,
                pltpu.SemaphoreType.DMA((3,)),
                pltpu.SemaphoreType.DMA((3,)),
                pltpu.SemaphoreType.DMA((5,)),
                pltpu.SemaphoreType.DMA((5,)),
                *[pltpu.SemaphoreType.DMA] * 8,
            ],
            compiler_params=pltpu.CompilerParams(
                collective_id=0, has_side_effects=True, vmem_limit_bytes=60 << 20),
        )(queries, targets.reshape(1, qd), lengths, contrast_items)
        qg, ig, loss = pl.pallas_call(
            functools.partial(finish, Y * Z, X * Z), out_shape=outs, in_specs=[anywhere] * 3, out_specs=(anywhere,) * 3,
            scratch_shapes=[
                *[pltpu.VMEM(o.shape, o.dtype) for o in outs],
                pltpu.VMEM((blocks, 128), bf16),
                pltpu.VMEM((BLK, 128), f32),
                pltpu.SemaphoreType.DMA((6,)),
                pltpu.SemaphoreType.DMA((6,)),
            ],
            compiler_params=pltpu.CompilerParams(vmem_limit_bytes=60 << 20),
        )(qg, loss, land2)
        return qg, ig, loss.reshape(qd)

    rows = P(("wide", "narrow"), None)
    flat = P(("wide", "narrow"))
    return jax.shard_map(
        body, mesh=mesh, in_specs=(rows, flat, flat, rows), out_specs=(rows, rows, flat), check_vma=False)
```

```python
import functools

import jax
import jax.numpy as jnp
from jax import lax
from jax.experimental import pallas as pl
from jax.experimental.pallas import tpu as pltpu
from jax.sharding import PartitionSpec as P

MESH = pl.DeviceIdType.MESH
SEQ_LEN = 256
SHARPNESS = 20.0
LOG2E = 1.4426950408889634
ZHI = 2
OWNED = 3
BLK = 16


def hops(d, n):
    return min(d % n, -d % n)


def far_first(A, B):
    offsets = [(a, b) for a in range(A) for b in range(B) if a or b]
    return sorted(offsets, key=lambda o: -hops(o[0], A) - hops(o[1], B))


def far_ring(n):
    return sorted(range(1, n), key=lambda d: -hops(d, n))


def kernel(X, Y, Z, q_hbm, tgt_hbm, len_hbm, it_hbm, qg_hbm, loss_hbm, land2,
           tgt_ref, len_ref, it_ref, qg_ref, loss_ref, q_all, info, stat, pool, pack, blk, land, scores, grads, out_items, in_items,
           pieces, qpart, qland,
           q_sem, in_sem, out_sem, pair_ssem, pair_rsem, s1_ssem, s1_rsem, s2_ssem, s2_rsem,
           r1_ssem, r1_rsem, r2_ssem, r2_rsem):
    zlo = Z // ZHI
    wide, narrow = lax.axis_index("wide"), lax.axis_index("narrow")
    x, c = wide // ZHI, narrow % 2
    y, z = (narrow // 2) % Y, (wide % ZHI) * zlo + narrow // (2 * Y)
    qd, width = q_hbm.shape
    chunks = width // 128
    slab = Y * Z * OWNED
    half = X * slab // 2
    yrows, zrows = half // Y, half // Z
    items = X * slab
    groups, members = Z // 2, 2 * Y
    grows = members * OWNED
    tile = X * grows
    last = Z - 1
    even = x % 2 == 0

    def dev(px, py, pz, pc):
        return (px * ZHI + pz // zlo, ((pz % zlo) * Y + py) * 2 + pc)

    yz, xz, xy = far_first(Y, Z), far_first(X, Z), far_first(X, Y)

    def remote(src, dst, ssem, rsem, to):
        return pltpu.make_async_remote_copy(
            src_ref=src, dst_ref=dst, send_sem=ssem, recv_sem=rsem, device_id=to, device_id_type=MESH)

    def bytes_of(ref, sem):
        return pltpu.make_async_copy(ref, ref, sem)

    def loop(lo, hi, f):
        def step(i, carry):
            f(i)
            return carry
        lax.fori_loop(lo, hi, step, 0)

    loads = [pltpu.make_async_copy(a, b, in_sem.at[k])
             for k, (a, b) in enumerate([(it_hbm, it_ref), (tgt_hbm, tgt_ref), (len_hbm, len_ref)])]
    load_q = pltpu.make_async_copy(q_hbm, q_all.at[c], q_sem)
    for load in loads:
        load.start()
    load_q.start()

    barrier = pltpu.get_barrier_semaphore()
    partner = dev(x, y, z, 1 - c)

    def greet(to):
        pl.semaphore_signal(barrier, inc=1, device_id=to, device_id_type=MESH)

    @pl.when(c == 0)
    def _():
        for dy, dz in yz:
            greet(dev(x, (y + dy) % Y, (z + dz) % Z, 0))
        for dx in far_ring(X):
            greet(dev((x + dx) % X, y, z, 0))

    @pl.when(c == 1)
    def _():
        for dx, dz in xz:
            greet(dev((x + dx) % X, y, (z + dz) % Z, 1))
        for dx, dy in xy:
            greet(dev((x + dx) % X, (y + dy) % Y, z, 1))

    greet(partner)

    loads[0].wait()
    own = it_ref[...].astype(jnp.float32)
    pack[pl.ds(0, BLK), :] = jnp.zeros((BLK, 128), jnp.float32)
    for a in range(chunks):
        pack[pl.ds(a * OWNED, OWNED), :] = own[:, a * 128:(a + 1) * 128]
    blk[...] = pack[pl.ds(0, BLK), :].astype(jnp.bfloat16)

    loads[1].wait()
    loads[2].wait()
    pos = lax.broadcasted_iota(jnp.int32, (1, qd), 1)
    live = jnp.where(pos < SEQ_LEN, (pos < len_ref[0]).astype(jnp.float32),
                     (pos - SEQ_LEN < len_ref[1]).astype(jnp.float32))
    info[c, pl.ds(0, 1), :] = tgt_ref[...].astype(jnp.float32)
    info[c, pl.ds(1, 1), :] = live
    info[c, pl.ds(2, 6), :] = jnp.zeros((6, qd), jnp.float32)
    load_q.wait()

    @pl.when(c == 0)
    def _():
        pl.semaphore_wait(barrier, Y * Z - 1 + X - 1 + 1)

    @pl.when(c == 1)
    def _():
        pl.semaphore_wait(barrier, X * Z - 1 + X * Y - 1 + 1)

    def rows(i):
        return pl.ds(pl.multiple_of(i * BLK, BLK), BLK)

    @pl.when(c == 0)
    def _():
        me = z * Y + y
        land[rows(me), :] = blk[...]

        def send(py, pz):
            remote(blk, land.at[rows(me)], s1_ssem, s1_rsem, dev(x, py, pz, 0)).start()

        for dy in far_ring(Y):
            send((y + dy) % Y, last)
        pl.when(z != last)(functools.partial(send, y, last))
        for dy, dz in yz:
            pz = (z + dz) % Z
            pl.when(pz != last)(functools.partial(send, (y + dy) % Y, pz))

    @pl.when(jnp.logical_and(c == 1, even))
    def _():
        me = (x // 2) * Z + z
        land[rows(me), :] = blk[...]

        def send(px, pz):
            remote(blk, land.at[rows(me)], s1_ssem, s1_rsem, dev(px, y, pz, 1)).start()

        for dx in far_ring(X):
            send((x + dx) % X, last)
        pl.when(z != last)(functools.partial(send, x, last))
        for dx, dz in xz:
            pz = (z + dz) % Z
            pl.when(pz != last)(functools.partial(send, (x + dx) % X, pz))

    @pl.when(jnp.logical_and(c == 1, jnp.logical_not(even)))
    def _():
        me = X // 2 * Z + (x // 2) * Y + y
        land[rows(me), :] = blk[...]

        for dx, dy in xy:
            remote(blk, land.at[rows(me)], s1_ssem, s1_rsem, dev((x + dx) % X, (y + dy) % Y, z, 1)).start()

    q_copy = remote(q_all.at[c], q_all.at[c], pair_ssem.at[0], pair_rsem.at[0], partner)
    q_copy.start()
    info_copy = remote(info.at[c], info.at[c], pair_ssem.at[1], pair_rsem.at[1], partner)
    info_copy.start()

    @pl.when(c == 0)
    def _():
        bytes_of(land.at[pl.ds(0, (Y * Z - 1) * BLK)], s1_rsem).wait()

    @pl.when(c == 1)
    def _():
        bytes_of(land.at[pl.ds(0, (X * Z - 1) * BLK)], s1_rsem).wait()

    def unpack(first, owners, base):
        n = owners * BLK
        pack[pl.ds(0, n), :] = land[pl.ds(first * BLK, n), :].astype(jnp.float32)
        for r in range(OWNED):
            for a in range(chunks):
                piece = pack[pl.ds(a * OWNED + r, owners, stride=BLK), :]
                at = base + r * owners
                pool[pl.ds(pl.multiple_of(at, 16), owners), a * 128:(a + 1) * 128] = piece.astype(jnp.bfloat16)

    xz_own, xy_own = X // 2 * Z, X // 2 * Y

    def piece(g, px):
        return pl.ds(pl.multiple_of(g * tile + px * grows, 16), grows)

    def y_at(py):
        return half // 2 + py * yrows

    def z_at(pz):
        return pz * zrows + jnp.where(pz >= Z // 2, half, 0)

    def slab_y(py):
        return pl.ds(pl.multiple_of(y_at(py), 16), yrows)

    def slab_z(pz):
        return pl.ds(pl.multiple_of(z_at(pz), 16), zrows)

    @pl.when(c == 0)
    def _():
        for g in range(groups):
            unpack(g * members, members, g * tile + x * grows)
            for dx in far_ring(X):
                remote(pool.at[piece(g, x)], pool.at[piece(g, x)], s2_ssem, s2_rsem, dev((x + dx) % X, y, z, 0)).start()
        bytes_of(pool.at[pl.ds(0, (X - 1) * slab)], s2_rsem).wait()

    @pl.when(c == 1)
    def _():
        unpack(xz_own, xy_own, z_at(z))

        def send(pz):
            remote(pool.at[slab_z(z)], pool.at[slab_z(z)], s2_ssem, s2_rsem, dev(x, y, pz, 1)).start()

        pl.when(z != last)(functools.partial(send, last))
        for dz in far_ring(Z):
            pz = (z + dz) % Z
            pl.when(pz != last)(functools.partial(send, pz))
        unpack(0, xz_own, y_at(y))
        for dy in far_ring(Y):
            remote(pool.at[slab_y(y)], pool.at[slab_y(y)], s2_ssem, s2_rsem, dev(x, (y + dy) % Y, z, 1)).start()
        bytes_of(pool.at[pl.ds(0, (Y - 1) * yrows + (Z - 1) * zrows)], s2_rsem).wait()

    q_copy.wait()
    info_copy.wait()

    def local_row(h):
        t = info[h, pl.ds(0, 1), :].astype(jnp.int32)
        o = (t * 21846) >> 16
        r = t - o * OWNED
        w, n = o // (zlo * Y * 2), o % (zlo * Y * 2)
        tx, tc = w // ZHI, n % 2
        ty, tz = (n // 2) % Y, (w % ZHI) * zlo + n // (2 * Y)
        on0 = (tz // 2) * tile + tx * grows + r * members + (tz % 2) * Y + ty
        on1 = jnp.where(tx % 2 == 0, y_at(ty) + r * xz_own + (tx // 2) * Z + tz,
                        z_at(tz) + r * xy_own + (tx // 2) * Y + ty)
        return jnp.where(tc == c, jnp.where(tc == 0, on0, on1), -1)

    third = items // 3
    step = max(8, items // 12)
    fold = functools.partial(jnp.reshape, shape=(step // 8, 8, qd))
    row_iota = lax.broadcasted_iota(jnp.int32, (step, qd), 0)
    K = SHARPNESS * LOG2E

    def first_pass(h):
        m8 = jnp.full((8, qd), -3e38, jnp.float32)
        for i in range(3):
            s = lax.dot_general(pool[pl.ds(i * third, third), :], q_all[h], (((1,), (1,)), ((), ())),
                                preferred_element_type=jnp.float32)
            scores[h, pl.ds(i * third, third), :] = s
            m8 = jnp.maximum(m8, jnp.max(s.reshape(third // 8, 8, qd), axis=0))
        m = jnp.max(m8, axis=0, keepdims=True)
        target = local_row(h)

        def body(i, carry):
            l8, t8 = carry
            at = pl.ds(pl.multiple_of(i * step, 8), step)
            s = scores[h, at, :]
            hit = row_iota == target - i * step
            e = jnp.exp2((s - m) * K)
            scores[h, at, :] = e
            return l8 + jnp.sum(fold(e), axis=0), t8 + jnp.sum(fold(jnp.where(hit, s, 0.0)), axis=0)

        zero = jnp.zeros((8, qd), jnp.float32)
        l8, t8 = lax.fori_loop(0, items // step, body, (zero, zero))
        stat[0, h, pl.ds(0, 1), :] = m
        stat[0, h, pl.ds(1, 1), :] = jnp.sum(l8, axis=0, keepdims=True)
        stat[0, h, pl.ds(2, 1), :] = jnp.sum(t8, axis=0, keepdims=True)
        stat[0, h, pl.ds(3, 5), :] = jnp.zeros((5, qd), jnp.float32)
        remote(stat.at[0, h], stat.at[1, h], pair_ssem.at[2 + h], pair_rsem.at[2 + h], partner).start()

    first_pass(1 - c)
    first_pass(c)

    def second_pass(h):
        remote(stat.at[0, h], stat.at[1, h], pair_ssem.at[2 + h], pair_rsem.at[2 + h], partner).wait()
        m, l, t = (stat[0, h, pl.ds(k, 1), :] for k in range(3))
        m2, l2, t2 = (stat[1, h, pl.ds(k, 1), :] for k in range(3))
        top = jnp.maximum(m, m2)
        mine = jnp.exp2((m - top) * K)
        total = l * mine + l2 * jnp.exp2((m2 - top) * K)
        valid = info[h, pl.ds(1, 1), :]
        weight = SHARPNESS * valid
        factor = weight * mine / total
        target = local_row(h)

        @pl.when(h == c)
        def _():
            loss_ref[...] = valid * (SHARPNESS * (top - (t + t2)) + jnp.log(total))

        def body(i):
            at = pl.ds(pl.multiple_of(i * step, 16), step)
            hit = row_iota == target - i * step
            g = scores[h, at, :] * factor - jnp.where(hit, weight, 0.0)
            grads[h, at, :] = g.astype(jnp.bfloat16)
        loop(0, items // step, body)

    second_pass(1 - c)
    for g in range(groups):
        at = pl.ds(g * tile, tile)
        scores[1 - c, at, :] = jnp.dot(grads[1 - c, at, :], q_all[1 - c], preferred_element_type=jnp.float32)
    second_pass(c)

    slabs = [(0, i) for i in range(Z // 2)] + [(1, i) for i in range(Y)] + [(0, i) for i in range(Z // 2, Z)]
    per = len(slabs) // groups
    for g in range(groups):
        at = pl.ds(g * tile, tile)
        total = jnp.dot(grads[c, at, :], q_all[c], preferred_element_type=jnp.float32) + scores[1 - c, at, :]
        out_items[at, :] = total.astype(jnp.bfloat16)

        @pl.when(c == 0)
        def _():
            for dx in far_ring(X):
                px = (x + dx) % X
                remote(out_items.at[piece(g, px)], in_items.at[piece(g, x)],
                       r1_ssem, r1_rsem.at[g], dev(px, y, z, 0)).start()

        @pl.when(c == 1)
        def _():
            for kind, i in slabs[g * per:(g + 1) * per]:
                if kind == 0:
                    @pl.when(z != i)
                    def _():
                        remote(out_items.at[slab_z(i)], in_items.at[slab_z(z)],
                               r1_ssem, r1_rsem.at[0], dev(x, y, i, 1)).start()
                else:
                    @pl.when(y != i)
                    def _():
                        remote(out_items.at[slab_y(i)], in_items.at[slab_y(y)],
                               r1_ssem, r1_rsem.at[1], dev(x, i, z, 1)).start()

    def query_part(h):
        return lax.dot_general(grads[h], pool[...], (((0,), (0,)), ((), ())), preferred_element_type=jnp.float32)

    qpart[...] = query_part(1 - c)
    part_copy = remote(qpart, qland, pair_ssem.at[4], pair_rsem.at[4], partner)
    part_copy.start()
    scores[0, pl.ds(0, qd), :] = query_part(c)

    def spread(rows_sum, owners, first):
        n = owners * BLK
        pack[pl.ds(0, n), :] = jnp.zeros((n, 128), jnp.float32)
        for r in range(OWNED):
            for a in range(chunks):
                pack[pl.ds(a * OWNED + r, owners, stride=BLK), :] = \
                    rows_sum[r * owners:(r + 1) * owners, a * 128:(a + 1) * 128]
        pieces[pl.ds(first * BLK, n), :] = pack[pl.ds(0, n), :].astype(jnp.bfloat16)

    def keep(block, slot):
        pltpu.make_async_copy(pieces.at[rows(block)], land2.at[rows(slot)], out_sem.at[2]).start()

    def deliver(block, slot, to):
        remote(pieces.at[rows(block)], land2.at[rows(slot)], r2_ssem, r2_rsem, to).start()

    @pl.when(c == 0)
    def _():
        me = z * Y + y
        for g in range(groups):
            bytes_of(in_items.at[pl.ds(0, (X - 1) * grows)], r1_rsem.at[g]).wait()
            total = out_items[piece(g, x), :].astype(jnp.float32)
            for i in range(1, X):
                total = total + in_items[piece(g, (x + i) % X), :].astype(jnp.float32)
            spread(total, members, g * members)
            for pz in (2 * g, 2 * g + 1):
                for dy in far_ring(Y):
                    py = (y + dy) % Y
                    deliver(pz * Y + py, me, dev(x, py, pz, 0))
                pl.when(z != pz)(functools.partial(deliver, pz * Y + y, me, dev(x, y, pz, 0)))
            pl.when(z // 2 == g)(functools.partial(keep, me, me))

    @pl.when(c == 1)
    def _():
        def of_kind(k):
            @pl.when(k == 0)
            def _():
                bytes_of(in_items.at[pl.ds(0, (Z - 1) * zrows)], r1_rsem.at[0]).wait()
                total = out_items[slab_z(z), :].astype(jnp.float32)
                for i in range(1, Z):
                    total = total + in_items[slab_z((z + i) % Z), :].astype(jnp.float32)
                spread(total, xy_own, xz_own)
                me = x * Y + y
                for py in range(Y):
                    for px in range(1, X, 2):
                        block = xz_own + (px // 2) * Y + py
                        here = jnp.logical_and(px == x, py == y)
                        pl.when(jnp.logical_not(here))(functools.partial(deliver, block, me, dev(px, py, z, 1)))
                        pl.when(here)(functools.partial(keep, block, me))

            @pl.when(k == 1)
            def _():
                bytes_of(in_items.at[pl.ds(0, (Y - 1) * yrows)], r1_rsem.at[1]).wait()
                total = out_items[slab_y(y), :].astype(jnp.float32)
                for i in range(1, Y):
                    total = total + in_items[slab_y((y + i) % Y), :].astype(jnp.float32)
                spread(total, xz_own, 0)
                me = x * Z + z
                for pz in range(Z):
                    for px in range(0, X, 2):
                        block = (px // 2) * Z + pz
                        here = jnp.logical_and(px == x, pz == z)
                        pl.when(jnp.logical_not(here))(functools.partial(deliver, block, me, dev(px, y, pz, 1)))
                        pl.when(here)(functools.partial(keep, block, me))

        loop(0, 2, lambda i: of_kind(jnp.where(z < Z // 2, i, 1 - i)))

    part_copy.wait()
    qg_ref[...] = (scores[0, pl.ds(0, qd), :] + qland[...]).astype(jnp.bfloat16)
    results = [pltpu.make_async_copy(a, b, out_sem.at[k])
               for k, (a, b) in enumerate([(qg_ref, qg_hbm), (loss_ref, loss_hbm)])]
    for result in results:
        result.start()

    @pl.when(c == 0)
    def _():
        bytes_of(land2.at[pl.ds(0, (Y * Z - 1) * BLK)], r2_rsem).wait()

    @pl.when(c == 1)
    def _():
        bytes_of(land2.at[pl.ds(0, (X * Z - 1) * BLK)], r2_rsem).wait()

    @pl.when(c == 0)
    def _():
        bytes_of(land.at[pl.ds(0, (Y * Z - 1) * BLK)], s1_ssem).wait()
        bytes_of(pool.at[pl.ds(0, (X - 1) * slab)], s2_ssem).wait()
        bytes_of(pool.at[pl.ds(0, (X - 1) * slab)], r1_ssem).wait()
        bytes_of(land2.at[pl.ds(0, (Y * Z - 1) * BLK)], r2_ssem).wait()

    @pl.when(c == 1)
    def _():
        bytes_of(land.at[pl.ds(0, (X * Z - 1) * BLK)], s1_ssem).wait()
        bytes_of(pool.at[pl.ds(0, (Y - 1) * yrows + (Z - 1) * zrows)], s2_ssem).wait()
        bytes_of(pool.at[pl.ds(0, (Y - 1) * yrows + (Z - 1) * zrows)], r1_ssem).wait()
        bytes_of(land2.at[pl.ds(0, (X * Z - 1) * BLK)], r2_ssem).wait()
    bytes_of(pieces.at[pl.ds(0, BLK)], out_sem.at[2]).wait()
    for result in results:
        result.wait()


def finish(n0, n1, qg, loss, land2, qg_out, ig_out, loss_out, qg_v, ig_v, loss_v, land_v, total, in_sem, out_sem):
    n = qg.shape[0] // 4
    legs = [(qg.at[pl.ds(i * n, n)], qg_v.at[pl.ds(i * n, n)], qg_out.at[pl.ds(i * n, n)]) for i in range(4)]
    legs += [(loss, loss_v, loss_out)]
    land_in = pltpu.make_async_copy(land2, land_v, in_sem.at[5])
    land_in.start()
    ins = [pltpu.make_async_copy(a, b, in_sem.at[k]) for k, (a, b, _) in enumerate(legs)]
    outs = [pltpu.make_async_copy(b, d, out_sem.at[k]) for k, (_, b, d) in enumerate(legs)]
    for copy in ins:
        copy.start()
    land_in.wait()
    group = min(n0, n1, 8)

    def body(i, carry):
        part = land_v[pl.ds(pl.multiple_of(i * group * BLK, BLK), group * BLK), :].astype(jnp.float32)
        return carry + jnp.sum(part.reshape(group, BLK, 128), axis=0)

    count = jnp.where(lax.axis_index("narrow") % 2 == 0, n0 // group, n1 // group)
    total[...] = lax.fori_loop(0, count, body, jnp.zeros((BLK, 128), jnp.float32))
    for a in range(ig_v.shape[1] // 128):
        ig_v[:, a * 128:(a + 1) * 128] = total[pl.ds(a * OWNED, OWNED), :]
    ig_copy = pltpu.make_async_copy(ig_v, ig_out, out_sem.at[5])
    ig_copy.start()
    for copy, after in zip(ins, outs):
        copy.wait()
        after.start()
    for copy in outs:
        copy.wait()
    ig_copy.wait()


def solution(mesh):
    X = mesh.shape["wide"] // ZHI

    def body(queries, targets, lengths, contrast_items):
        qd, width = queries.shape
        zlo = 4 if mesh.shape["narrow"] == 64 else 1
        Y = mesh.shape["narrow"] // (2 * zlo)
        Z = zlo * ZHI
        items = X * Y * Z * OWNED
        blocks = max(Y * Z, X * Z, X * Y) * BLK
        anywhere = pl.BlockSpec(memory_space=pl.ANY)
        f32, bf16 = jnp.float32, jnp.bfloat16
        outs = (
            jax.ShapeDtypeStruct((qd, width), bf16),
            jax.ShapeDtypeStruct((OWNED, width), f32),
            jax.ShapeDtypeStruct((1, qd), f32),
        )
        qg, loss, land2 = pl.pallas_call(
            functools.partial(kernel, X, Y, Z),
            out_shape=(outs[0], outs[2], jax.ShapeDtypeStruct((blocks, 128), bf16)),
            in_specs=[anywhere] * 4,
            out_specs=(anywhere,) * 3,
            scratch_shapes=[
                pltpu.VMEM((1, qd), jnp.int32),
                pltpu.SMEM(lengths.shape, jnp.int32),
                pltpu.VMEM((OWNED, width), bf16),
                pltpu.VMEM((qd, width), bf16),
                pltpu.VMEM((1, qd), f32),
                pltpu.VMEM((2, qd, width), bf16),
                pltpu.VMEM((2, 8, qd), f32),
                pltpu.VMEM((2, 2, 8, qd), f32),
                pltpu.VMEM((items, width), bf16),
                pltpu.VMEM((blocks, 128), f32),
                pltpu.VMEM((BLK, 128), bf16),
                pltpu.VMEM((blocks, 128), bf16),
                pltpu.VMEM((2, max(items, qd), qd), f32),
                pltpu.VMEM((2, items, qd), bf16),
                pltpu.VMEM((items, width), bf16),
                pltpu.VMEM((items, width), bf16),
                pltpu.VMEM((blocks, 128), bf16),
                pltpu.VMEM((qd, width), f32),
                pltpu.VMEM((qd, width), f32),
                pltpu.SemaphoreType.DMA,
                pltpu.SemaphoreType.DMA((3,)),
                pltpu.SemaphoreType.DMA((3,)),
                pltpu.SemaphoreType.DMA((5,)),
                pltpu.SemaphoreType.DMA((5,)),
                *[pltpu.SemaphoreType.DMA] * 5,
                pltpu.SemaphoreType.DMA((max(Z // 2, 2),)),
                *[pltpu.SemaphoreType.DMA] * 2,
            ],
            compiler_params=pltpu.CompilerParams(
                collective_id=0, has_side_effects=True, vmem_limit_bytes=60 << 20),
        )(queries, targets.reshape(1, qd), lengths, contrast_items)
        qg, ig, loss = pl.pallas_call(
            functools.partial(finish, Y * Z, X * Z), out_shape=outs, in_specs=[anywhere] * 3, out_specs=(anywhere,) * 3,
            scratch_shapes=[
                *[pltpu.VMEM(o.shape, o.dtype) for o in outs],
                pltpu.VMEM((blocks, 128), bf16),
                pltpu.VMEM((BLK, 128), f32),
                pltpu.SemaphoreType.DMA((6,)),
                pltpu.SemaphoreType.DMA((6,)),
            ],
            compiler_params=pltpu.CompilerParams(vmem_limit_bytes=60 << 20),
        )(qg, loss, land2)
        return qg, ig, loss.reshape(qd)

    rows = P(("wide", "narrow"), None)
    flat = P(("wide", "narrow"))
    return jax.shard_map(
        body, mesh=mesh, in_specs=(rows, flat, flat, rows), out_specs=(rows, rows, flat), check_vma=False)
```

```python
import functools

import jax
import jax.numpy as jnp
from jax import lax
from jax.experimental import pallas as pl
from jax.experimental.pallas import tpu as pltpu
from jax.sharding import PartitionSpec as P

MESH = pl.DeviceIdType.MESH
SEQ_LEN = 256
SHARPNESS = 20.0
LOG2E = 1.4426950408889634
ZHI = 2
OWNED = 3
BLK = 16


def hops(d, n):
    return min(d % n, -d % n)


def far_first(A, B):
    offsets = [(a, b) for a in range(A) for b in range(B) if a or b]
    return sorted(offsets, key=lambda o: -hops(o[0], A) - hops(o[1], B))


def far_ring(n):
    return sorted(range(1, n), key=lambda d: -hops(d, n))


def kernel(X, Y, Z, q_hbm, tgt_hbm, len_hbm, it_hbm, qg_hbm, loss_hbm, land2,
           tgt_ref, len_ref, it_ref, qg_ref, loss_ref, q_all, info, stat, pool, pack, blk, land, scores, grads, out_items, in_items,
           pieces, qpart, qland,
           q_sem, in_sem, out_sem, pair_ssem, pair_rsem, s1_ssem, s1_rsem, s2_ssem, s2_rsem,
           r1_ssem, r1_rsem, r2_ssem, r2_rsem):
    zlo = Z // ZHI
    wide, narrow = lax.axis_index("wide"), lax.axis_index("narrow")
    x, c = wide // ZHI, narrow % 2
    y, z = (narrow // 2) % Y, (wide % ZHI) * zlo + narrow // (2 * Y)
    qd, width = q_hbm.shape
    chunks = width // 128
    slab = Y * Z * OWNED
    half = X * slab // 2
    yrows, zrows = half // Y, half // Z
    items = X * slab
    groups, members = Z // 2, 2 * Y
    grows = members * OWNED
    tile = X * grows
    last = Z - 1
    near = sorted(range(groups), key=lambda k: hops(k, groups))
    even = x % 2 == 0

    def dev(px, py, pz, pc):
        return (px * ZHI + pz // zlo, ((pz % zlo) * Y + py) * 2 + pc)

    yz, xz, xy = far_first(Y, Z), far_first(X, Z), far_first(X, Y)

    def remote(src, dst, ssem, rsem, to):
        return pltpu.make_async_remote_copy(
            src_ref=src, dst_ref=dst, send_sem=ssem, recv_sem=rsem, device_id=to, device_id_type=MESH)

    def bytes_of(ref, sem):
        return pltpu.make_async_copy(ref, ref, sem)

    def loop(lo, hi, f):
        def step(i, carry):
            f(i)
            return carry
        lax.fori_loop(lo, hi, step, 0)

    loads = [pltpu.make_async_copy(a, b, in_sem.at[k])
             for k, (a, b) in enumerate([(it_hbm, it_ref), (tgt_hbm, tgt_ref), (len_hbm, len_ref)])]
    load_q = pltpu.make_async_copy(q_hbm, q_all.at[c], q_sem)
    for load in loads:
        load.start()
    load_q.start()

    barrier = pltpu.get_barrier_semaphore()
    partner = dev(x, y, z, 1 - c)

    def greet(to):
        pl.semaphore_signal(barrier, inc=1, device_id=to, device_id_type=MESH)

    @pl.when(c == 0)
    def _():
        for dy, dz in yz:
            greet(dev(x, (y + dy) % Y, (z + dz) % Z, 0))
        for dx in far_ring(X):
            greet(dev((x + dx) % X, y, z, 0))

    @pl.when(c == 1)
    def _():
        for dx, dz in xz:
            greet(dev((x + dx) % X, y, (z + dz) % Z, 1))
        for dx, dy in xy:
            greet(dev((x + dx) % X, (y + dy) % Y, z, 1))

    greet(partner)

    loads[0].wait()
    own = it_ref[...].astype(jnp.float32)
    pack[pl.ds(0, BLK), :] = jnp.zeros((BLK, 128), jnp.float32)
    for a in range(chunks):
        pack[pl.ds(a * OWNED, OWNED), :] = own[:, a * 128:(a + 1) * 128]
    blk[...] = pack[pl.ds(0, BLK), :].astype(jnp.bfloat16)

    loads[1].wait()
    loads[2].wait()
    pos = lax.broadcasted_iota(jnp.int32, (1, qd), 1)
    live = jnp.where(pos < SEQ_LEN, (pos < len_ref[0]).astype(jnp.float32),
                     (pos - SEQ_LEN < len_ref[1]).astype(jnp.float32))
    info[c, pl.ds(0, 1), :] = tgt_ref[...].astype(jnp.float32)
    info[c, pl.ds(1, 1), :] = live
    info[c, pl.ds(2, 6), :] = jnp.zeros((6, qd), jnp.float32)
    load_q.wait()

    @pl.when(c == 0)
    def _():
        pl.semaphore_wait(barrier, Y * Z - 1 + X - 1 + 1)

    @pl.when(c == 1)
    def _():
        pl.semaphore_wait(barrier, X * Z - 1 + X * Y - 1 + 1)

    def rows(i):
        return pl.ds(pl.multiple_of(i * BLK, BLK), BLK)

    @pl.when(c == 0)
    def _():
        me = z * Y + y
        land[rows(me), :] = blk[...]

        def send(py, pz):
            remote(blk, land.at[rows(me)], s1_ssem, s1_rsem.at[z // 2], dev(x, py, pz, 0)).start()

        for dy in far_ring(Y):
            send((y + dy) % Y, last)
        pl.when(z != last)(functools.partial(send, y, last))
        for dy, dz in yz:
            pz = (z + dz) % Z
            pl.when(pz != last)(functools.partial(send, (y + dy) % Y, pz))

    @pl.when(jnp.logical_and(c == 1, even))
    def _():
        me = (x // 2) * Z + z
        land[rows(me), :] = blk[...]

        def send(px, pz):
            remote(blk, land.at[rows(me)], s1_ssem, s1_rsem.at[1], dev(px, y, pz, 1)).start()

        for dx in far_ring(X):
            send((x + dx) % X, last)
        pl.when(z != last)(functools.partial(send, x, last))
        for dx, dz in xz:
            pz = (z + dz) % Z
            pl.when(pz != last)(functools.partial(send, (x + dx) % X, pz))

    @pl.when(jnp.logical_and(c == 1, jnp.logical_not(even)))
    def _():
        me = X // 2 * Z + (x // 2) * Y + y
        land[rows(me), :] = blk[...]

        for dx, dy in xy:
            remote(blk, land.at[rows(me)], s1_ssem, s1_rsem.at[0], dev((x + dx) % X, (y + dy) % Y, z, 1)).start()

    q_copy = remote(q_all.at[c], q_all.at[c], pair_ssem.at[0], pair_rsem.at[0], partner)
    q_copy.start()
    info_copy = remote(info.at[c], info.at[c], pair_ssem.at[1], pair_rsem.at[1], partner)
    info_copy.start()

    def landed(count, k):
        bytes_of(land.at[pl.ds(0, count * BLK)], s1_rsem.at[k]).wait()

    def unpack(first, owners, base):
        n = owners * BLK
        pack[pl.ds(0, n), :] = land[pl.ds(pl.multiple_of(first * BLK, BLK), n), :].astype(jnp.float32)
        for r in range(OWNED):
            for a in range(chunks):
                piece = pack[pl.ds(a * OWNED + r, owners, stride=BLK), :]
                at = base + r * owners
                pool[pl.ds(pl.multiple_of(at, 16), owners), a * 128:(a + 1) * 128] = piece.astype(jnp.bfloat16)

    xz_own, xy_own = X // 2 * Z, X // 2 * Y

    def piece(g, px):
        return pl.ds(pl.multiple_of(g * tile + px * grows, 16), grows)

    def y_at(py):
        return half // 2 + py * yrows

    def z_at(pz):
        return pz * zrows + jnp.where(pz >= Z // 2, half, 0)

    def slab_y(py):
        return pl.ds(pl.multiple_of(y_at(py), 16), yrows)

    def slab_z(pz):
        return pl.ds(pl.multiple_of(z_at(pz), 16), zrows)

    @pl.when(c == 0)
    def _():
        for k in near:
            g = (z // 2 + k) % groups
            landed(members - (k == 0), g)
            unpack(g * members, members, g * tile + x * grows)
            for dx in far_ring(X):
                remote(pool.at[piece(g, x)], pool.at[piece(g, x)],
                       s2_ssem, s2_rsem.at[g], dev((x + dx) % X, y, z, 0)).start()

    @pl.when(c == 1)
    def _():
        pl.when(even)(functools.partial(landed, xy_own, 0))
        pl.when(jnp.logical_not(even))(functools.partial(landed, xy_own - 1, 0))
        unpack(xz_own, xy_own, z_at(z))

        def send(pz):
            remote(pool.at[slab_z(z)], pool.at[slab_z(z)], s2_ssem, s2_rsem.at[0], dev(x, y, pz, 1)).start()

        pl.when(z != last)(functools.partial(send, last))
        for dz in far_ring(Z):
            pz = (z + dz) % Z
            pl.when(pz != last)(functools.partial(send, pz))

        pl.when(even)(functools.partial(landed, xz_own - 1, 1))
        pl.when(jnp.logical_not(even))(functools.partial(landed, xz_own, 1))
        unpack(0, xz_own, y_at(y))
        for dy in far_ring(Y):
            remote(pool.at[slab_y(y)], pool.at[slab_y(y)],
                   s2_ssem, s2_rsem.at[1], dev(x, (y + dy) % Y, z, 1)).start()

    q_copy.wait()
    info_copy.wait()

    def local_row(h):
        t = info[h, pl.ds(0, 1), :].astype(jnp.int32)
        o = (t * 21846) >> 16
        r = t - o * OWNED
        w, n = o // (zlo * Y * 2), o % (zlo * Y * 2)
        tx, tc = w // ZHI, n % 2
        ty, tz = (n // 2) % Y, (w % ZHI) * zlo + n // (2 * Y)
        on0 = (tz // 2) * tile + tx * grows + r * members + (tz % 2) * Y + ty
        on1 = jnp.where(tx % 2 == 0, y_at(ty) + r * xz_own + (tx // 2) * Z + tz,
                        z_at(tz) + r * xy_own + (tx // 2) * Y + ty)
        return jnp.where(tc == c, jnp.where(tc == 0, on0, on1), -1)

    step = max(8, items // 12)
    fold = functools.partial(jnp.reshape, shape=(step // 8, 8, qd))
    row_iota = lax.broadcasted_iota(jnp.int32, (step, qd), 0)
    K = SHARPNESS * LOG2E

    halves = (1 - c, c)
    tops = [jnp.full((8, qd), -3e38, jnp.float32)] * 2
    for k in range(groups):
        g = jnp.where(c == 0, (z // 2 + near[k]) % groups, k)

        @pl.when(c == 0)
        def _():
            bytes_of(pool.at[pl.ds(0, (X - 1) * grows)], s2_rsem.at[g]).wait()

        @pl.when(c == 1)
        def _():
            if k == 0:
                bytes_of(pool.at[pl.ds(0, (Z - 1) * zrows)], s2_rsem.at[0]).wait()
            if k == min(1, groups - 1):
                bytes_of(pool.at[pl.ds(0, (Y - 1) * yrows)], s2_rsem.at[1]).wait()

        at = pl.ds(pl.multiple_of(g * tile, 16), tile)
        for i, h in enumerate(halves):
            s = lax.dot_general(pool[at, :], q_all[h], (((1,), (1,)), ((), ())), preferred_element_type=jnp.float32)
            scores[h, at, :] = s
            tops[i] = jnp.maximum(tops[i], jnp.max(s.reshape(tile // 8, 8, qd), axis=0))

    def first_pass(h, m8):
        m = jnp.max(m8, axis=0, keepdims=True)
        target = local_row(h)

        def body(i, carry):
            l8, t8 = carry
            at = pl.ds(pl.multiple_of(i * step, 8), step)
            s = scores[h, at, :]
            hit = row_iota == target - i * step
            e = jnp.exp2((s - m) * K)
            scores[h, at, :] = e
            return l8 + jnp.sum(fold(e), axis=0), t8 + jnp.sum(fold(jnp.where(hit, s, 0.0)), axis=0)

        zero = jnp.zeros((8, qd), jnp.float32)
        l8, t8 = lax.fori_loop(0, items // step, body, (zero, zero))
        stat[0, h, pl.ds(0, 1), :] = m
        stat[0, h, pl.ds(1, 1), :] = jnp.sum(l8, axis=0, keepdims=True)
        stat[0, h, pl.ds(2, 1), :] = jnp.sum(t8, axis=0, keepdims=True)
        stat[0, h, pl.ds(3, 5), :] = jnp.zeros((5, qd), jnp.float32)
        remote(stat.at[0, h], stat.at[1, h], pair_ssem.at[2 + h], pair_rsem.at[2 + h], partner).start()

    for h, m8 in zip(halves, tops):
        first_pass(h, m8)

    def second_pass(h):
        remote(stat.at[0, h], stat.at[1, h], pair_ssem.at[2 + h], pair_rsem.at[2 + h], partner).wait()
        m, l, t = (stat[0, h, pl.ds(k, 1), :] for k in range(3))
        m2, l2, t2 = (stat[1, h, pl.ds(k, 1), :] for k in range(3))
        top = jnp.maximum(m, m2)
        mine = jnp.exp2((m - top) * K)
        total = l * mine + l2 * jnp.exp2((m2 - top) * K)
        valid = info[h, pl.ds(1, 1), :]
        weight = SHARPNESS * valid
        factor = weight * mine / total
        target = local_row(h)

        @pl.when(h == c)
        def _():
            loss_ref[...] = valid * (SHARPNESS * (top - (t + t2)) + jnp.log(total))

        def body(i):
            at = pl.ds(pl.multiple_of(i * step, 16), step)
            hit = row_iota == target - i * step
            g = scores[h, at, :] * factor - jnp.where(hit, weight, 0.0)
            grads[h, at, :] = g.astype(jnp.bfloat16)
        loop(0, items // step, body)

    second_pass(1 - c)
    for g in range(groups):
        at = pl.ds(g * tile, tile)
        scores[1 - c, at, :] = jnp.dot(grads[1 - c, at, :], q_all[1 - c], preferred_element_type=jnp.float32)
    second_pass(c)

    slabs = [(0, i) for i in range(Z // 2)] + [(1, i) for i in range(Y)] + [(0, i) for i in range(Z // 2, Z)]
    per = len(slabs) // groups
    for g in range(groups):
        at = pl.ds(g * tile, tile)
        total = jnp.dot(grads[c, at, :], q_all[c], preferred_element_type=jnp.float32) + scores[1 - c, at, :]
        out_items[at, :] = total.astype(jnp.bfloat16)

        @pl.when(c == 0)
        def _():
            for dx in far_ring(X):
                px = (x + dx) % X
                remote(out_items.at[piece(g, px)], in_items.at[piece(g, x)],
                       r1_ssem, r1_rsem.at[g], dev(px, y, z, 0)).start()

        @pl.when(c == 1)
        def _():
            for kind, i in slabs[g * per:(g + 1) * per]:
                if kind == 0:
                    @pl.when(z != i)
                    def _():
                        remote(out_items.at[slab_z(i)], in_items.at[slab_z(z)],
                               r1_ssem, r1_rsem.at[0], dev(x, y, i, 1)).start()
                else:
                    @pl.when(y != i)
                    def _():
                        remote(out_items.at[slab_y(i)], in_items.at[slab_y(y)],
                               r1_ssem, r1_rsem.at[1], dev(x, i, z, 1)).start()

    def query_part(h):
        return lax.dot_general(grads[h], pool[...], (((0,), (0,)), ((), ())), preferred_element_type=jnp.float32)

    qpart[...] = query_part(1 - c)
    part_copy = remote(qpart, qland, pair_ssem.at[4], pair_rsem.at[4], partner)
    part_copy.start()
    scores[0, pl.ds(0, qd), :] = query_part(c)

    def spread(rows_sum, owners, first):
        n = owners * BLK
        pack[pl.ds(0, n), :] = jnp.zeros((n, 128), jnp.float32)
        for r in range(OWNED):
            for a in range(chunks):
                pack[pl.ds(a * OWNED + r, owners, stride=BLK), :] = \
                    rows_sum[r * owners:(r + 1) * owners, a * 128:(a + 1) * 128]
        pieces[pl.ds(first * BLK, n), :] = pack[pl.ds(0, n), :].astype(jnp.bfloat16)

    def keep(block, slot):
        pltpu.make_async_copy(pieces.at[rows(block)], land2.at[rows(slot)], out_sem.at[2]).start()

    def deliver(block, slot, to):
        remote(pieces.at[rows(block)], land2.at[rows(slot)], r2_ssem, r2_rsem, to).start()

    @pl.when(c == 0)
    def _():
        me = z * Y + y
        for g in range(groups):
            bytes_of(in_items.at[pl.ds(0, (X - 1) * grows)], r1_rsem.at[g]).wait()
            total = out_items[piece(g, x), :].astype(jnp.float32)
            for i in range(1, X):
                total = total + in_items[piece(g, (x + i) % X), :].astype(jnp.float32)
            spread(total, members, g * members)
            for pz in (2 * g, 2 * g + 1):
                for dy in far_ring(Y):
                    py = (y + dy) % Y
                    deliver(pz * Y + py, me, dev(x, py, pz, 0))
                pl.when(z != pz)(functools.partial(deliver, pz * Y + y, me, dev(x, y, pz, 0)))
            pl.when(z // 2 == g)(functools.partial(keep, me, me))

    @pl.when(c == 1)
    def _():
        def of_kind(k):
            @pl.when(k == 0)
            def _():
                bytes_of(in_items.at[pl.ds(0, (Z - 1) * zrows)], r1_rsem.at[0]).wait()
                total = out_items[slab_z(z), :].astype(jnp.float32)
                for i in range(1, Z):
                    total = total + in_items[slab_z((z + i) % Z), :].astype(jnp.float32)
                spread(total, xy_own, xz_own)
                me = x * Y + y
                for py in range(Y):
                    for px in range(1, X, 2):
                        block = xz_own + (px // 2) * Y + py
                        here = jnp.logical_and(px == x, py == y)
                        pl.when(jnp.logical_not(here))(functools.partial(deliver, block, me, dev(px, py, z, 1)))
                        pl.when(here)(functools.partial(keep, block, me))

            @pl.when(k == 1)
            def _():
                bytes_of(in_items.at[pl.ds(0, (Y - 1) * yrows)], r1_rsem.at[1]).wait()
                total = out_items[slab_y(y), :].astype(jnp.float32)
                for i in range(1, Y):
                    total = total + in_items[slab_y((y + i) % Y), :].astype(jnp.float32)
                spread(total, xz_own, 0)
                me = x * Z + z
                for pz in range(Z):
                    for px in range(0, X, 2):
                        block = (px // 2) * Z + pz
                        here = jnp.logical_and(px == x, pz == z)
                        pl.when(jnp.logical_not(here))(functools.partial(deliver, block, me, dev(px, y, pz, 1)))
                        pl.when(here)(functools.partial(keep, block, me))

        loop(0, 2, lambda i: of_kind(jnp.where(z < Z // 2, i, 1 - i)))

    part_copy.wait()
    qg_ref[...] = (scores[0, pl.ds(0, qd), :] + qland[...]).astype(jnp.bfloat16)
    results = [pltpu.make_async_copy(a, b, out_sem.at[k])
               for k, (a, b) in enumerate([(qg_ref, qg_hbm), (loss_ref, loss_hbm)])]
    for result in results:
        result.start()

    @pl.when(c == 0)
    def _():
        bytes_of(land2.at[pl.ds(0, (Y * Z - 1) * BLK)], r2_rsem).wait()

    @pl.when(c == 1)
    def _():
        bytes_of(land2.at[pl.ds(0, (X * Z - 1) * BLK)], r2_rsem).wait()

    @pl.when(c == 0)
    def _():
        bytes_of(land.at[pl.ds(0, (Y * Z - 1) * BLK)], s1_ssem).wait()
        bytes_of(pool.at[pl.ds(0, (X - 1) * slab)], s2_ssem).wait()
        bytes_of(pool.at[pl.ds(0, (X - 1) * slab)], r1_ssem).wait()
        bytes_of(land2.at[pl.ds(0, (Y * Z - 1) * BLK)], r2_ssem).wait()

    @pl.when(c == 1)
    def _():
        bytes_of(land.at[pl.ds(0, (X * Z - 1) * BLK)], s1_ssem).wait()
        bytes_of(pool.at[pl.ds(0, (Y - 1) * yrows + (Z - 1) * zrows)], s2_ssem).wait()
        bytes_of(pool.at[pl.ds(0, (Y - 1) * yrows + (Z - 1) * zrows)], r1_ssem).wait()
        bytes_of(land2.at[pl.ds(0, (X * Z - 1) * BLK)], r2_ssem).wait()
    bytes_of(pieces.at[pl.ds(0, BLK)], out_sem.at[2]).wait()
    for result in results:
        result.wait()


def finish(n0, n1, qg, loss, land2, qg_out, ig_out, loss_out, qg_v, ig_v, loss_v, land_v, total, in_sem, out_sem):
    n = qg.shape[0] // 4
    legs = [(qg.at[pl.ds(i * n, n)], qg_v.at[pl.ds(i * n, n)], qg_out.at[pl.ds(i * n, n)]) for i in range(4)]
    legs += [(loss, loss_v, loss_out)]
    land_in = pltpu.make_async_copy(land2, land_v, in_sem.at[5])
    land_in.start()
    ins = [pltpu.make_async_copy(a, b, in_sem.at[k]) for k, (a, b, _) in enumerate(legs)]
    outs = [pltpu.make_async_copy(b, d, out_sem.at[k]) for k, (_, b, d) in enumerate(legs)]
    for copy in ins:
        copy.start()
    land_in.wait()
    group = min(n0, n1, 8)

    def body(i, carry):
        part = land_v[pl.ds(pl.multiple_of(i * group * BLK, BLK), group * BLK), :].astype(jnp.float32)
        return carry + jnp.sum(part.reshape(group, BLK, 128), axis=0)

    count = jnp.where(lax.axis_index("narrow") % 2 == 0, n0 // group, n1 // group)
    total[...] = lax.fori_loop(0, count, body, jnp.zeros((BLK, 128), jnp.float32))
    for a in range(ig_v.shape[1] // 128):
        ig_v[:, a * 128:(a + 1) * 128] = total[pl.ds(a * OWNED, OWNED), :]
    ig_copy = pltpu.make_async_copy(ig_v, ig_out, out_sem.at[5])
    ig_copy.start()
    for copy, after in zip(ins, outs):
        copy.wait()
        after.start()
    for copy in outs:
        copy.wait()
    ig_copy.wait()


def solution(mesh):
    X = mesh.shape["wide"] // ZHI

    def body(queries, targets, lengths, contrast_items):
        qd, width = queries.shape
        zlo = 4 if mesh.shape["narrow"] == 64 else 1
        Y = mesh.shape["narrow"] // (2 * zlo)
        Z = zlo * ZHI
        items = X * Y * Z * OWNED
        blocks = max(Y * Z, X * Z, X * Y) * BLK
        anywhere = pl.BlockSpec(memory_space=pl.ANY)
        f32, bf16 = jnp.float32, jnp.bfloat16
        outs = (
            jax.ShapeDtypeStruct((qd, width), bf16),
            jax.ShapeDtypeStruct((OWNED, width), f32),
            jax.ShapeDtypeStruct((1, qd), f32),
        )
        qg, loss, land2 = pl.pallas_call(
            functools.partial(kernel, X, Y, Z),
            out_shape=(outs[0], outs[2], jax.ShapeDtypeStruct((blocks, 128), bf16)),
            in_specs=[anywhere] * 4,
            out_specs=(anywhere,) * 3,
            scratch_shapes=[
                pltpu.VMEM((1, qd), jnp.int32),
                pltpu.SMEM(lengths.shape, jnp.int32),
                pltpu.VMEM((OWNED, width), bf16),
                pltpu.VMEM((qd, width), bf16),
                pltpu.VMEM((1, qd), f32),
                pltpu.VMEM((2, qd, width), bf16),
                pltpu.VMEM((2, 8, qd), f32),
                pltpu.VMEM((2, 2, 8, qd), f32),
                pltpu.VMEM((items, width), bf16),
                pltpu.VMEM((blocks, 128), f32),
                pltpu.VMEM((BLK, 128), bf16),
                pltpu.VMEM((blocks, 128), bf16),
                pltpu.VMEM((2, max(items, qd), qd), f32),
                pltpu.VMEM((2, items, qd), bf16),
                pltpu.VMEM((items, width), bf16),
                pltpu.VMEM((items, width), bf16),
                pltpu.VMEM((blocks, 128), bf16),
                pltpu.VMEM((qd, width), f32),
                pltpu.VMEM((qd, width), f32),
                pltpu.SemaphoreType.DMA,
                pltpu.SemaphoreType.DMA((3,)),
                pltpu.SemaphoreType.DMA((3,)),
                pltpu.SemaphoreType.DMA((5,)),
                pltpu.SemaphoreType.DMA((5,)),
                *[pltpu.SemaphoreType.DMA, pltpu.SemaphoreType.DMA((max(Z // 2, 2),))] * 3,
                *[pltpu.SemaphoreType.DMA] * 2,
            ],
            compiler_params=pltpu.CompilerParams(
                collective_id=0, has_side_effects=True, vmem_limit_bytes=60 << 20),
        )(queries, targets.reshape(1, qd), lengths, contrast_items)
        qg, ig, loss = pl.pallas_call(
            functools.partial(finish, Y * Z, X * Z), out_shape=outs, in_specs=[anywhere] * 3, out_specs=(anywhere,) * 3,
            scratch_shapes=[
                *[pltpu.VMEM(o.shape, o.dtype) for o in outs],
                pltpu.VMEM((blocks, 128), bf16),
                pltpu.VMEM((BLK, 128), f32),
                pltpu.SemaphoreType.DMA((6,)),
                pltpu.SemaphoreType.DMA((6,)),
            ],
            compiler_params=pltpu.CompilerParams(vmem_limit_bytes=60 << 20),
        )(qg, loss, land2)
        return qg, ig, loss.reshape(qd)

    rows = P(("wide", "narrow"), None)
    flat = P(("wide", "narrow"))
    return jax.shard_map(
        body, mesh=mesh, in_specs=(rows, flat, flat, rows), out_specs=(rows, rows, flat), check_vma=False)
```

```python
import functools

import jax
import jax.numpy as jnp
from jax import lax
from jax.experimental import pallas as pl
from jax.experimental.pallas import tpu as pltpu
from jax.sharding import PartitionSpec as P

MESH = pl.DeviceIdType.MESH
SEQ_LEN = 256
SHARPNESS = 20.0
LOG2E = 1.4426950408889634
ZHI = 2
OWNED = 3
BLK = 16


def hops(d, n):
    return min(d % n, -d % n)


def far_first(A, B):
    offsets = [(a, b) for a in range(A) for b in range(B) if a or b]
    return sorted(offsets, key=lambda o: -hops(o[0], A) - hops(o[1], B))


def far_ring(n):
    return sorted(range(1, n), key=lambda d: -hops(d, n))


def kernel(X, Y, Z, q_hbm, tgt_hbm, len_hbm, it_hbm, qg_hbm, loss_hbm, land2,
           tgt_ref, len_ref, it_ref, qg_ref, loss_ref, q_all, info, stat, pool, pack, blk, land, scores, tops, grads, out_items, in_items,
           pieces, qpart, qland,
           q_sem, in_sem, out_sem, pair_ssem, pair_rsem, s1_ssem, s1_rsem, s2_ssem, s2_rsem,
           r1_ssem, r1_rsem, r2_ssem, r2_rsem):
    zlo = Z // ZHI
    wide, narrow = lax.axis_index("wide"), lax.axis_index("narrow")
    x, c = wide // ZHI, narrow % 2
    y, z = (narrow // 2) % Y, (wide % ZHI) * zlo + narrow // (2 * Y)
    qd, width = q_hbm.shape
    chunks = width // 128
    slab = Y * Z * OWNED
    half = X * slab // 2
    yrows, zrows = half // Y, half // Z
    items = X * slab
    groups, members = Z // 2, 2 * Y
    grows = members * OWNED
    tile = X * grows
    last = Z - 1
    near = sorted(range(groups), key=lambda k: hops(k, groups))
    even = x % 2 == 0

    def dev(px, py, pz, pc):
        return (px * ZHI + pz // zlo, ((pz % zlo) * Y + py) * 2 + pc)

    yz, xz, xy = far_first(Y, Z), far_first(X, Z), far_first(X, Y)

    def remote(src, dst, ssem, rsem, to):
        return pltpu.make_async_remote_copy(
            src_ref=src, dst_ref=dst, send_sem=ssem, recv_sem=rsem, device_id=to, device_id_type=MESH)

    def bytes_of(ref, sem):
        return pltpu.make_async_copy(ref, ref, sem)

    def loop(lo, hi, f):
        def step(i, carry):
            f(i)
            return carry
        lax.fori_loop(lo, hi, step, 0)

    loads = [pltpu.make_async_copy(a, b, in_sem.at[k])
             for k, (a, b) in enumerate([(it_hbm, it_ref), (tgt_hbm, tgt_ref), (len_hbm, len_ref)])]
    load_q = pltpu.make_async_copy(q_hbm, q_all.at[c], q_sem)
    for load in loads:
        load.start()
    load_q.start()

    barrier = pltpu.get_barrier_semaphore()
    partner = dev(x, y, z, 1 - c)

    def greet(to):
        pl.semaphore_signal(barrier, inc=1, device_id=to, device_id_type=MESH)

    @pl.when(c == 0)
    def _():
        for dy, dz in yz:
            greet(dev(x, (y + dy) % Y, (z + dz) % Z, 0))
        for dx in far_ring(X):
            greet(dev((x + dx) % X, y, z, 0))

    @pl.when(c == 1)
    def _():
        for dx, dz in xz:
            greet(dev((x + dx) % X, y, (z + dz) % Z, 1))
        for dx, dy in xy:
            greet(dev((x + dx) % X, (y + dy) % Y, z, 1))

    greet(partner)

    loads[0].wait()
    own = it_ref[...].astype(jnp.float32)
    pack[pl.ds(0, BLK), :] = jnp.zeros((BLK, 128), jnp.float32)
    for a in range(chunks):
        pack[pl.ds(a * OWNED, OWNED), :] = own[:, a * 128:(a + 1) * 128]
    blk[...] = pack[pl.ds(0, BLK), :].astype(jnp.bfloat16)

    loads[1].wait()
    loads[2].wait()
    pos = lax.broadcasted_iota(jnp.int32, (1, qd), 1)
    live = jnp.where(pos < SEQ_LEN, (pos < len_ref[0]).astype(jnp.float32),
                     (pos - SEQ_LEN < len_ref[1]).astype(jnp.float32))
    info[c, pl.ds(0, 1), :] = tgt_ref[...].astype(jnp.float32)
    info[c, pl.ds(1, 1), :] = live
    info[c, pl.ds(2, 6), :] = jnp.zeros((6, qd), jnp.float32)
    load_q.wait()

    @pl.when(c == 0)
    def _():
        pl.semaphore_wait(barrier, Y * Z - 1 + X - 1 + 1)

    @pl.when(c == 1)
    def _():
        pl.semaphore_wait(barrier, X * Z - 1 + X * Y - 1 + 1)

    def rows(i):
        return pl.ds(pl.multiple_of(i * BLK, BLK), BLK)

    @pl.when(c == 0)
    def _():
        me = z * Y + y
        land[rows(me), :] = blk[...]

        def send(py, pz):
            remote(blk, land.at[rows(me)], s1_ssem, s1_rsem.at[z // 2], dev(x, py, pz, 0)).start()

        for dy in far_ring(Y):
            send((y + dy) % Y, last)
        pl.when(z != last)(functools.partial(send, y, last))
        for dy, dz in yz:
            pz = (z + dz) % Z
            pl.when(pz != last)(functools.partial(send, (y + dy) % Y, pz))

    @pl.when(jnp.logical_and(c == 1, even))
    def _():
        me = (x // 2) * Z + z
        land[rows(me), :] = blk[...]

        def send(px, pz):
            remote(blk, land.at[rows(me)], s1_ssem, s1_rsem.at[1], dev(px, y, pz, 1)).start()

        for dx in far_ring(X):
            send((x + dx) % X, last)
        pl.when(z != last)(functools.partial(send, x, last))
        for dx, dz in xz:
            pz = (z + dz) % Z
            pl.when(pz != last)(functools.partial(send, (x + dx) % X, pz))

    @pl.when(jnp.logical_and(c == 1, jnp.logical_not(even)))
    def _():
        me = X // 2 * Z + (x // 2) * Y + y
        land[rows(me), :] = blk[...]

        for dx, dy in xy:
            remote(blk, land.at[rows(me)], s1_ssem, s1_rsem.at[0], dev((x + dx) % X, (y + dy) % Y, z, 1)).start()

    q_copy = remote(q_all.at[c], q_all.at[c], pair_ssem.at[0], pair_rsem.at[0], partner)
    q_copy.start()
    info_copy = remote(info.at[c], info.at[c], pair_ssem.at[1], pair_rsem.at[1], partner)
    info_copy.start()

    def landed(count, k):
        bytes_of(land.at[pl.ds(0, count * BLK)], s1_rsem.at[k]).wait()

    def unpack(first, owners, base):
        n = owners * BLK
        pack[pl.ds(0, n), :] = land[pl.ds(pl.multiple_of(first * BLK, BLK), n), :].astype(jnp.float32)
        for r in range(OWNED):
            for a in range(chunks):
                piece = pack[pl.ds(a * OWNED + r, owners, stride=BLK), :]
                at = base + r * owners
                pool[pl.ds(pl.multiple_of(at, 16), owners), a * 128:(a + 1) * 128] = piece.astype(jnp.bfloat16)

    xz_own, xy_own = X // 2 * Z, X // 2 * Y

    def piece(g, px):
        return pl.ds(pl.multiple_of(g * tile + px * grows, 16), grows)

    def y_at(py):
        return py * yrows

    def z_at(pz):
        return half + pz * zrows

    def slab_y(py):
        return pl.ds(pl.multiple_of(y_at(py), 16), yrows)

    def slab_z(pz):
        return pl.ds(pl.multiple_of(z_at(pz), 16), zrows)

    @pl.when(c == 0)
    def _():
        for k in near:
            g = (z // 2 + k) % groups
            landed(members - (k == 0), g)
            unpack(g * members, members, g * tile + x * grows)
            for dx in far_ring(X):
                remote(pool.at[piece(g, x)], pool.at[piece(g, x)],
                       s2_ssem, s2_rsem.at[g], dev((x + dx) % X, y, z, 0)).start()

    @pl.when(c == 1)
    def _():
        pl.when(even)(functools.partial(landed, xy_own, 0))
        pl.when(jnp.logical_not(even))(functools.partial(landed, xy_own - 1, 0))
        unpack(xz_own, xy_own, z_at(z))

        def send(pz):
            remote(pool.at[slab_z(z)], pool.at[slab_z(z)], s2_ssem, s2_rsem.at[0], dev(x, y, pz, 1)).start()

        pl.when(z != last)(functools.partial(send, last))
        for dz in far_ring(Z):
            pz = (z + dz) % Z
            pl.when(pz != last)(functools.partial(send, pz))

        pl.when(even)(functools.partial(landed, xz_own - 1, 1))
        pl.when(jnp.logical_not(even))(functools.partial(landed, xz_own, 1))
        unpack(0, xz_own, y_at(y))
        for dy in far_ring(Y):
            remote(pool.at[slab_y(y)], pool.at[slab_y(y)],
                   s2_ssem, s2_rsem.at[1], dev(x, (y + dy) % Y, z, 1)).start()

    q_copy.wait()
    info_copy.wait()

    def local_row(h):
        t = info[h, pl.ds(0, 1), :].astype(jnp.int32)
        o = (t * 21846) >> 16
        r = t - o * OWNED
        w, n = o // (zlo * Y * 2), o % (zlo * Y * 2)
        tx, tc = w // ZHI, n % 2
        ty, tz = (n // 2) % Y, (w % ZHI) * zlo + n // (2 * Y)
        on0 = (tz // 2) * tile + tx * grows + r * members + (tz % 2) * Y + ty
        on1 = jnp.where(tx % 2 == 0, y_at(ty) + r * xz_own + (tx // 2) * Z + tz,
                        z_at(tz) + r * xy_own + (tx // 2) * Y + ty)
        return jnp.where(tc == c, jnp.where(tc == 0, on0, on1), -1)

    step = max(8, items // 12)
    fold = functools.partial(jnp.reshape, shape=(step // 8, 8, qd))
    row_iota = lax.broadcasted_iota(jnp.int32, (step, qd), 0)
    K = SHARPNESS * LOG2E

    halves = (1 - c, c)
    targets = [local_row(h) for h in halves]
    zero = jnp.zeros((8, qd), jnp.float32)
    found = [zero, zero]
    for k in range(groups):
        g = jnp.where(c == 0, (z // 2 + near[k]) % groups, (groups // 2 + k) % groups)

        @pl.when(c == 0)
        def _():
            bytes_of(pool.at[pl.ds(0, (X - 1) * grows)], s2_rsem.at[g]).wait()

        @pl.when(c == 1)
        def _():
            if k == 0:
                bytes_of(pool.at[pl.ds(0, (Z - 1) * zrows)], s2_rsem.at[0]).wait()
            if k == groups // 2:
                bytes_of(pool.at[pl.ds(0, (Y - 1) * yrows)], s2_rsem.at[1]).wait()

        at = pl.ds(pl.multiple_of(g * tile, 16), tile)
        for i, h in enumerate(halves):
            s = lax.dot_general(pool[at, :], q_all[h], (((1,), (1,)), ((), ())), preferred_element_type=jnp.float32)
            scores[h, at, :] = s
            m = jnp.max(jnp.max(s.reshape(tile // 8, 8, qd), axis=0), axis=0, keepdims=True)

            def body(j, carry, g=g, h=h, m=m, target=targets[i]):
                l8, t8 = carry
                first = pl.multiple_of(g * tile + j * step, 8)
                at = pl.ds(first, step)
                s = scores[h, at, :]
                e = jnp.exp2((s - m) * K)
                scores[h, at, :] = e
                hit = row_iota == target - first
                return l8 + jnp.sum(fold(e), axis=0), t8 + jnp.sum(fold(jnp.where(hit, s, 0.0)), axis=0)

            l8, found[i] = lax.fori_loop(0, tile // step, body, (zero, found[i]))
            tops[g, h, pl.ds(0, 1), :] = m
            tops[g, h, pl.ds(1, 1), :] = jnp.sum(l8, axis=0, keepdims=True)

    for i, h in enumerate(halves):
        m = tops[0, h, pl.ds(0, 1), :]
        for g in range(1, groups):
            m = jnp.maximum(m, tops[g, h, pl.ds(0, 1), :])
        l = jnp.zeros((1, qd), jnp.float32)
        for g in range(groups):
            l = l + tops[g, h, pl.ds(1, 1), :] * jnp.exp2((tops[g, h, pl.ds(0, 1), :] - m) * K)
        stat[0, h, pl.ds(0, 1), :] = m
        stat[0, h, pl.ds(1, 1), :] = l
        stat[0, h, pl.ds(2, 1), :] = jnp.sum(found[i], axis=0, keepdims=True)
        stat[0, h, pl.ds(3, 5), :] = jnp.zeros((5, qd), jnp.float32)
        remote(stat.at[0, h], stat.at[1, h], pair_ssem.at[2 + h], pair_rsem.at[2 + h], partner).start()

    def second_pass(h, target):
        remote(stat.at[0, h], stat.at[1, h], pair_ssem.at[2 + h], pair_rsem.at[2 + h], partner).wait()
        m, l, t = (stat[0, h, pl.ds(k, 1), :] for k in range(3))
        m2, l2, t2 = (stat[1, h, pl.ds(k, 1), :] for k in range(3))
        top = jnp.maximum(m, m2)
        total = l * jnp.exp2((m - top) * K) + l2 * jnp.exp2((m2 - top) * K)
        valid = info[h, pl.ds(1, 1), :]
        weight = SHARPNESS * valid
        share = weight / total

        @pl.when(h == c)
        def _():
            loss_ref[...] = valid * (SHARPNESS * (top - (t + t2)) + jnp.log(total))

        def of_tile(g):
            factor = share * jnp.exp2((tops[g, h, pl.ds(0, 1), :] - top) * K)

            def body(j):
                first = pl.multiple_of(g * tile + j * step, 16)
                at = pl.ds(first, step)
                hit = row_iota == target - first
                grad = scores[h, at, :] * factor - jnp.where(hit, weight, 0.0)
                grads[h, at, :] = grad.astype(jnp.bfloat16)
            loop(0, tile // step, body)
        loop(0, groups, of_tile)

    second_pass(1 - c, targets[0])
    for g in range(groups):
        at = pl.ds(g * tile, tile)
        scores[1 - c, at, :] = jnp.dot(grads[1 - c, at, :], q_all[1 - c], preferred_element_type=jnp.float32)
    second_pass(c, targets[1])

    slabs = [(1, i) for i in range(Y)] + [(0, i) for i in range(Z)]
    per = len(slabs) // groups
    for g in range(groups):
        at = pl.ds(g * tile, tile)
        total = jnp.dot(grads[c, at, :], q_all[c], preferred_element_type=jnp.float32) + scores[1 - c, at, :]
        out_items[at, :] = total.astype(jnp.bfloat16)

        @pl.when(c == 0)
        def _():
            for dx in far_ring(X):
                px = (x + dx) % X
                remote(out_items.at[piece(g, px)], in_items.at[piece(g, x)],
                       r1_ssem, r1_rsem.at[g], dev(px, y, z, 0)).start()

        @pl.when(c == 1)
        def _():
            for kind, i in slabs[g * per:(g + 1) * per]:
                if kind == 0:
                    @pl.when(z != i)
                    def _():
                        remote(out_items.at[slab_z(i)], in_items.at[slab_z(z)],
                               r1_ssem, r1_rsem.at[0], dev(x, y, i, 1)).start()
                else:
                    @pl.when(y != i)
                    def _():
                        remote(out_items.at[slab_y(i)], in_items.at[slab_y(y)],
                               r1_ssem, r1_rsem.at[1], dev(x, i, z, 1)).start()

    def query_part(h):
        return lax.dot_general(grads[h], pool[...], (((0,), (0,)), ((), ())), preferred_element_type=jnp.float32)

    qpart[...] = query_part(1 - c)
    part_copy = remote(qpart, qland, pair_ssem.at[4], pair_rsem.at[4], partner)
    part_copy.start()
    scores[0, pl.ds(0, qd), :] = query_part(c)

    def spread(rows_sum, owners, first):
        n = owners * BLK
        pack[pl.ds(0, n), :] = jnp.zeros((n, 128), jnp.float32)
        for r in range(OWNED):
            for a in range(chunks):
                pack[pl.ds(a * OWNED + r, owners, stride=BLK), :] = \
                    rows_sum[r * owners:(r + 1) * owners, a * 128:(a + 1) * 128]
        pieces[pl.ds(first * BLK, n), :] = pack[pl.ds(0, n), :].astype(jnp.bfloat16)

    def keep(block, slot):
        pltpu.make_async_copy(pieces.at[rows(block)], land2.at[rows(slot)], out_sem.at[2]).start()

    def deliver(block, slot, to):
        remote(pieces.at[rows(block)], land2.at[rows(slot)], r2_ssem, r2_rsem, to).start()

    @pl.when(c == 0)
    def _():
        me = z * Y + y
        for g in range(groups):
            bytes_of(in_items.at[pl.ds(0, (X - 1) * grows)], r1_rsem.at[g]).wait()
            total = out_items[piece(g, x), :].astype(jnp.float32)
            for i in range(1, X):
                total = total + in_items[piece(g, (x + i) % X), :].astype(jnp.float32)
            spread(total, members, g * members)
            for pz in (2 * g, 2 * g + 1):
                for dy in far_ring(Y):
                    py = (y + dy) % Y
                    deliver(pz * Y + py, me, dev(x, py, pz, 0))
                pl.when(z != pz)(functools.partial(deliver, pz * Y + y, me, dev(x, y, pz, 0)))
            pl.when(z // 2 == g)(functools.partial(keep, me, me))

    @pl.when(c == 1)
    def _():
        def deliver_all(rows_of, n, me, k, first, dests):
            bytes_of(in_items.at[pl.ds(0, (n - 1) * yrows)], r1_rsem.at[k]).wait()
            total = out_items[rows_of(me), :].astype(jnp.float32)
            for i in range(1, n):
                total = total + in_items[rows_of((me + i) % n), :].astype(jnp.float32)
            spread(total, len(dests), first)
            for i, (px, py, pz, slot) in enumerate(dests):
                here = jnp.logical_and(px == x, jnp.logical_and(py == y, pz == z))
                pl.when(jnp.logical_not(here))(functools.partial(deliver, first + i, slot, dev(px, py, pz, 1)))
                pl.when(here)(functools.partial(keep, first + i, slot))

        deliver_all(slab_y, Y, y, 1, 0,
                    [(px, y, pz, x * Z + z) for px in range(0, X, 2) for pz in range(Z)])
        deliver_all(slab_z, Z, z, 0, xz_own,
                    [(px, py, z, x * Y + y) for px in range(1, X, 2) for py in range(Y)])

    part_copy.wait()
    qg_ref[...] = (scores[0, pl.ds(0, qd), :] + qland[...]).astype(jnp.bfloat16)
    results = [pltpu.make_async_copy(a, b, out_sem.at[k])
               for k, (a, b) in enumerate([(qg_ref, qg_hbm), (loss_ref, loss_hbm)])]
    for result in results:
        result.start()

    @pl.when(c == 0)
    def _():
        bytes_of(land2.at[pl.ds(0, (Y * Z - 1) * BLK)], r2_rsem).wait()

    @pl.when(c == 1)
    def _():
        bytes_of(land2.at[pl.ds(0, (X * Z - 1) * BLK)], r2_rsem).wait()

    @pl.when(c == 0)
    def _():
        bytes_of(land.at[pl.ds(0, (Y * Z - 1) * BLK)], s1_ssem).wait()
        bytes_of(pool.at[pl.ds(0, (X - 1) * slab)], s2_ssem).wait()
        bytes_of(pool.at[pl.ds(0, (X - 1) * slab)], r1_ssem).wait()
        bytes_of(land2.at[pl.ds(0, (Y * Z - 1) * BLK)], r2_ssem).wait()

    @pl.when(c == 1)
    def _():
        bytes_of(land.at[pl.ds(0, (X * Z - 1) * BLK)], s1_ssem).wait()
        bytes_of(pool.at[pl.ds(0, (Y - 1) * yrows + (Z - 1) * zrows)], s2_ssem).wait()
        bytes_of(pool.at[pl.ds(0, (Y - 1) * yrows + (Z - 1) * zrows)], r1_ssem).wait()
        bytes_of(land2.at[pl.ds(0, (X * Z - 1) * BLK)], r2_ssem).wait()
    bytes_of(pieces.at[pl.ds(0, BLK)], out_sem.at[2]).wait()
    for result in results:
        result.wait()


def finish(n0, n1, qg, loss, land2, qg_out, ig_out, loss_out, qg_v, ig_v, loss_v, land_v, total, in_sem, out_sem):
    n = qg.shape[0] // 4
    legs = [(qg.at[pl.ds(i * n, n)], qg_v.at[pl.ds(i * n, n)], qg_out.at[pl.ds(i * n, n)]) for i in range(4)]
    legs += [(loss, loss_v, loss_out)]
    land_in = pltpu.make_async_copy(land2, land_v, in_sem.at[5])
    land_in.start()
    ins = [pltpu.make_async_copy(a, b, in_sem.at[k]) for k, (a, b, _) in enumerate(legs)]
    outs = [pltpu.make_async_copy(b, d, out_sem.at[k]) for k, (_, b, d) in enumerate(legs)]
    for copy in ins:
        copy.start()
    land_in.wait()
    group = min(n0, n1, 8)

    def body(i, carry):
        part = land_v[pl.ds(pl.multiple_of(i * group * BLK, BLK), group * BLK), :].astype(jnp.float32)
        return carry + jnp.sum(part.reshape(group, BLK, 128), axis=0)

    count = jnp.where(lax.axis_index("narrow") % 2 == 0, n0 // group, n1 // group)
    total[...] = lax.fori_loop(0, count, body, jnp.zeros((BLK, 128), jnp.float32))
    for a in range(ig_v.shape[1] // 128):
        ig_v[:, a * 128:(a + 1) * 128] = total[pl.ds(a * OWNED, OWNED), :]
    ig_copy = pltpu.make_async_copy(ig_v, ig_out, out_sem.at[5])
    ig_copy.start()
    for copy, after in zip(ins, outs):
        copy.wait()
        after.start()
    for copy in outs:
        copy.wait()
    ig_copy.wait()


def solution(mesh):
    X = mesh.shape["wide"] // ZHI

    def body(queries, targets, lengths, contrast_items):
        qd, width = queries.shape
        zlo = 4 if mesh.shape["narrow"] == 64 else 1
        Y = mesh.shape["narrow"] // (2 * zlo)
        Z = zlo * ZHI
        items = X * Y * Z * OWNED
        blocks = max(Y * Z, X * Z, X * Y) * BLK
        anywhere = pl.BlockSpec(memory_space=pl.ANY)
        f32, bf16 = jnp.float32, jnp.bfloat16
        outs = (
            jax.ShapeDtypeStruct((qd, width), bf16),
            jax.ShapeDtypeStruct((OWNED, width), f32),
            jax.ShapeDtypeStruct((1, qd), f32),
        )
        qg, loss, land2 = pl.pallas_call(
            functools.partial(kernel, X, Y, Z),
            out_shape=(outs[0], outs[2], jax.ShapeDtypeStruct((blocks, 128), bf16)),
            in_specs=[anywhere] * 4,
            out_specs=(anywhere,) * 3,
            scratch_shapes=[
                pltpu.VMEM((1, qd), jnp.int32),
                pltpu.SMEM(lengths.shape, jnp.int32),
                pltpu.VMEM((OWNED, width), bf16),
                pltpu.VMEM((qd, width), bf16),
                pltpu.VMEM((1, qd), f32),
                pltpu.VMEM((2, qd, width), bf16),
                pltpu.VMEM((2, 8, qd), f32),
                pltpu.VMEM((2, 2, 8, qd), f32),
                pltpu.VMEM((items, width), bf16),
                pltpu.VMEM((blocks, 128), f32),
                pltpu.VMEM((BLK, 128), bf16),
                pltpu.VMEM((blocks, 128), bf16),
                pltpu.VMEM((2, max(items, qd), qd), f32),
                pltpu.VMEM((Z // 2, 2, 8, qd), f32),
                pltpu.VMEM((2, items, qd), bf16),
                pltpu.VMEM((items, width), bf16),
                pltpu.VMEM((items, width), bf16),
                pltpu.VMEM((blocks, 128), bf16),
                pltpu.VMEM((qd, width), f32),
                pltpu.VMEM((qd, width), f32),
                pltpu.SemaphoreType.DMA,
                pltpu.SemaphoreType.DMA((3,)),
                pltpu.SemaphoreType.DMA((3,)),
                pltpu.SemaphoreType.DMA((5,)),
                pltpu.SemaphoreType.DMA((5,)),
                *[pltpu.SemaphoreType.DMA, pltpu.SemaphoreType.DMA((max(Z // 2, 2),))] * 3,
                *[pltpu.SemaphoreType.DMA] * 2,
            ],
            compiler_params=pltpu.CompilerParams(
                collective_id=0, has_side_effects=True, vmem_limit_bytes=60 << 20),
        )(queries, targets.reshape(1, qd), lengths, contrast_items)
        qg, ig, loss = pl.pallas_call(
            functools.partial(finish, Y * Z, X * Z), out_shape=outs, in_specs=[anywhere] * 3, out_specs=(anywhere,) * 3,
            scratch_shapes=[
                *[pltpu.VMEM(o.shape, o.dtype) for o in outs],
                pltpu.VMEM((blocks, 128), bf16),
                pltpu.VMEM((BLK, 128), f32),
                pltpu.SemaphoreType.DMA((6,)),
                pltpu.SemaphoreType.DMA((6,)),
            ],
            compiler_params=pltpu.CompilerParams(vmem_limit_bytes=60 << 20),
        )(qg, loss, land2)
        return qg, ig, loss.reshape(qd)

    rows = P(("wide", "narrow"), None)
    flat = P(("wide", "narrow"))
    return jax.shard_map(
        body, mesh=mesh, in_specs=(rows, flat, flat, rows), out_specs=(rows, rows, flat), check_vma=False)
```

```python
import functools

import jax
import jax.numpy as jnp
from jax import lax
from jax.experimental import pallas as pl
from jax.experimental.pallas import tpu as pltpu
from jax.sharding import PartitionSpec as P

MESH = pl.DeviceIdType.MESH
SEQ_LEN = 256
SHARPNESS = 20.0
LOG2E = 1.4426950408889634
ZHI = 2
OWNED = 3
BLK = 16


def hops(d, n):
    return min(d % n, -d % n)


def far_first(A, B):
    offsets = [(a, b) for a in range(A) for b in range(B) if a or b]
    return sorted(offsets, key=lambda o: -hops(o[0], A) - hops(o[1], B))


def far_ring(n):
    return sorted(range(1, n), key=lambda d: -hops(d, n))


def kernel(X, Y, Z, q_hbm, tgt_hbm, len_hbm, it_hbm, qg_hbm, loss_hbm, land2,
           tgt_ref, len_ref, it_ref, qg_ref, loss_ref, q_all, info, stat, pool, pack, blk, land, scores, tops, grads, out_items, in_items,
           pieces, qpart, qland,
           q_sem, in_sem, out_sem, pair_ssem, pair_rsem, s1_ssem, s1_rsem, s2_ssem, s2_rsem,
           r1_ssem, r1_rsem, r2_ssem, r2_rsem):
    zlo = Z // ZHI
    wide, narrow = lax.axis_index("wide"), lax.axis_index("narrow")
    x, c = wide // ZHI, narrow % 2
    y, z = (narrow // 2) % Y, (wide % ZHI) * zlo + narrow // (2 * Y)
    qd, width = q_hbm.shape
    chunks = width // 128
    slab = Y * Z * OWNED
    half = X * slab // 2
    yrows, zrows = half // Y, half // Z
    items = X * slab
    groups, members = Z // 2, 2 * Y
    grows = members * OWNED
    tile = X * grows
    last = Z - 1
    near = sorted(range(groups), key=lambda k: hops(k, groups))
    even = x % 2 == 0

    def dev(px, py, pz, pc):
        return (px * ZHI + pz // zlo, ((pz % zlo) * Y + py) * 2 + pc)

    yz, xz, xy = far_first(Y, Z), far_first(X, Z), far_first(X, Y)

    def remote(src, dst, ssem, rsem, to):
        return pltpu.make_async_remote_copy(
            src_ref=src, dst_ref=dst, send_sem=ssem, recv_sem=rsem, device_id=to, device_id_type=MESH)

    def bytes_of(ref, sem):
        return pltpu.make_async_copy(ref, ref, sem)

    def loop(lo, hi, f):
        def step(i, carry):
            f(i)
            return carry
        lax.fori_loop(lo, hi, step, 0)

    loads = [pltpu.make_async_copy(a, b, in_sem.at[k])
             for k, (a, b) in enumerate([(it_hbm, it_ref), (tgt_hbm, tgt_ref), (len_hbm, len_ref)])]
    load_q = pltpu.make_async_copy(q_hbm, q_all.at[c], q_sem)
    loads[0].start()

    barrier = pltpu.get_barrier_semaphore()
    partner = dev(x, y, z, 1 - c)

    def greet(to):
        pl.semaphore_signal(barrier, inc=1, device_id=to, device_id_type=MESH)

    @pl.when(c == 0)
    def _():
        for dy, dz in yz:
            greet(dev(x, (y + dy) % Y, (z + dz) % Z, 0))
        for dx in far_ring(X):
            greet(dev((x + dx) % X, y, z, 0))

    @pl.when(c == 1)
    def _():
        for dx, dz in xz:
            greet(dev((x + dx) % X, y, (z + dz) % Z, 1))
        for dx, dy in xy:
            greet(dev((x + dx) % X, (y + dy) % Y, z, 1))

    greet(partner)
    loads[1].start()
    loads[2].start()
    load_q.start()

    loads[0].wait()
    own = it_ref[...].astype(jnp.float32)
    pack[pl.ds(0, BLK), :] = jnp.zeros((BLK, 128), jnp.float32)
    for a in range(chunks):
        pack[pl.ds(a * OWNED, OWNED), :] = own[:, a * 128:(a + 1) * 128]
    blk[...] = pack[pl.ds(0, BLK), :].astype(jnp.bfloat16)

    @pl.when(c == 0)
    def _():
        pl.semaphore_wait(barrier, Y * Z - 1 + X - 1 + 1)

    @pl.when(c == 1)
    def _():
        pl.semaphore_wait(barrier, X * Z - 1 + X * Y - 1 + 1)

    def rows(i):
        return pl.ds(pl.multiple_of(i * BLK, BLK), BLK)

    @pl.when(c == 0)
    def _():
        me = z * Y + y
        land[rows(me), :] = blk[...]

        def send(py, pz):
            remote(blk, land.at[rows(me)], s1_ssem, s1_rsem.at[z // 2], dev(x, py, pz, 0)).start()

        for dy in far_ring(Y):
            send((y + dy) % Y, last)
        pl.when(z != last)(functools.partial(send, y, last))
        for dy, dz in yz:
            pz = (z + dz) % Z
            pl.when(pz != last)(functools.partial(send, (y + dy) % Y, pz))

    @pl.when(jnp.logical_and(c == 1, even))
    def _():
        me = (x // 2) * Z + z
        land[rows(me), :] = blk[...]

        def send(px, pz):
            remote(blk, land.at[rows(me)], s1_ssem, s1_rsem.at[1], dev(px, y, pz, 1)).start()

        for dx in far_ring(X):
            send((x + dx) % X, last)
        pl.when(z != last)(functools.partial(send, x, last))
        for dx, dz in xz:
            pz = (z + dz) % Z
            pl.when(pz != last)(functools.partial(send, (x + dx) % X, pz))

    @pl.when(jnp.logical_and(c == 1, jnp.logical_not(even)))
    def _():
        me = X // 2 * Z + (x // 2) * Y + y
        land[rows(me), :] = blk[...]

        for dx, dy in xy:
            remote(blk, land.at[rows(me)], s1_ssem, s1_rsem.at[0], dev((x + dx) % X, (y + dy) % Y, z, 1)).start()

    loads[1].wait()
    loads[2].wait()
    pos = lax.broadcasted_iota(jnp.int32, (1, qd), 1)
    live = jnp.where(pos < SEQ_LEN, (pos < len_ref[0]).astype(jnp.float32),
                     (pos - SEQ_LEN < len_ref[1]).astype(jnp.float32))
    info[c, pl.ds(0, 1), :] = tgt_ref[...].astype(jnp.float32)
    info[c, pl.ds(1, 1), :] = live
    info[c, pl.ds(2, 6), :] = jnp.zeros((6, qd), jnp.float32)
    load_q.wait()

    q_copy = remote(q_all.at[c], q_all.at[c], pair_ssem.at[0], pair_rsem.at[0], partner)
    q_copy.start()
    info_copy = remote(info.at[c], info.at[c], pair_ssem.at[1], pair_rsem.at[1], partner)
    info_copy.start()

    def landed(count, k):
        bytes_of(land.at[pl.ds(0, count * BLK)], s1_rsem.at[k]).wait()

    def unpack(first, owners, base):
        n = owners * BLK
        pack[pl.ds(0, n), :] = land[pl.ds(pl.multiple_of(first * BLK, BLK), n), :].astype(jnp.float32)
        for r in range(OWNED):
            for a in range(chunks):
                piece = pack[pl.ds(a * OWNED + r, owners, stride=BLK), :]
                at = base + r * owners
                pool[pl.ds(pl.multiple_of(at, 16), owners), a * 128:(a + 1) * 128] = piece.astype(jnp.bfloat16)

    xz_own, xy_own = X // 2 * Z, X // 2 * Y

    def piece(g, px):
        return pl.ds(pl.multiple_of(g * tile + px * grows, 16), grows)

    def y_at(py):
        return py * yrows

    def z_at(pz):
        return half + pz * zrows

    def slab_y(py):
        return pl.ds(pl.multiple_of(y_at(py), 16), yrows)

    def slab_z(pz):
        return pl.ds(pl.multiple_of(z_at(pz), 16), zrows)

    @pl.when(c == 0)
    def _():
        for k in near:
            g = (z // 2 + k) % groups
            landed(members - (k == 0), g)
            unpack(g * members, members, g * tile + x * grows)
            for dx in far_ring(X):
                remote(pool.at[piece(g, x)], pool.at[piece(g, x)],
                       s2_ssem, s2_rsem.at[g], dev((x + dx) % X, y, z, 0)).start()

    @pl.when(c == 1)
    def _():
        pl.when(even)(functools.partial(landed, xy_own, 0))
        pl.when(jnp.logical_not(even))(functools.partial(landed, xy_own - 1, 0))
        unpack(xz_own, xy_own, z_at(z))

        def send(pz):
            remote(pool.at[slab_z(z)], pool.at[slab_z(z)], s2_ssem, s2_rsem.at[0], dev(x, y, pz, 1)).start()

        pl.when(z != last)(functools.partial(send, last))
        for dz in far_ring(Z):
            pz = (z + dz) % Z
            pl.when(pz != last)(functools.partial(send, pz))

        pl.when(even)(functools.partial(landed, xz_own - 1, 1))
        pl.when(jnp.logical_not(even))(functools.partial(landed, xz_own, 1))
        unpack(0, xz_own, y_at(y))
        for dy in far_ring(Y):
            remote(pool.at[slab_y(y)], pool.at[slab_y(y)],
                   s2_ssem, s2_rsem.at[1], dev(x, (y + dy) % Y, z, 1)).start()

    q_copy.wait()
    info_copy.wait()

    def local_row(h):
        t = info[h, pl.ds(0, 1), :].astype(jnp.int32)
        o = (t * 21846) >> 16
        r = t - o * OWNED
        w, n = o // (zlo * Y * 2), o % (zlo * Y * 2)
        tx, tc = w // ZHI, n % 2
        ty, tz = (n // 2) % Y, (w % ZHI) * zlo + n // (2 * Y)
        on0 = (tz // 2) * tile + tx * grows + r * members + (tz % 2) * Y + ty
        on1 = jnp.where(tx % 2 == 0, y_at(ty) + r * xz_own + (tx // 2) * Z + tz,
                        z_at(tz) + r * xy_own + (tx // 2) * Y + ty)
        return jnp.where(tc == c, jnp.where(tc == 0, on0, on1), -1)

    step = max(8, items // 12)
    fold = functools.partial(jnp.reshape, shape=(step // 8, 8, qd))
    row_iota = lax.broadcasted_iota(jnp.int32, (step, qd), 0)
    K = SHARPNESS * LOG2E

    halves = (1 - c, c)
    targets = [local_row(h) for h in halves]
    zero = jnp.zeros((8, qd), jnp.float32)
    found = [zero, zero]
    def join(h, t8):
        m = tops[0, h, pl.ds(0, 1), :]
        for g in range(1, groups):
            m = jnp.maximum(m, tops[g, h, pl.ds(0, 1), :])
        l = jnp.zeros((1, qd), jnp.float32)
        for g in range(groups):
            l = l + tops[g, h, pl.ds(1, 1), :] * jnp.exp2((tops[g, h, pl.ds(0, 1), :] - m) * K)
        stat[0, h, pl.ds(0, 1), :] = m
        stat[0, h, pl.ds(1, 1), :] = l
        stat[0, h, pl.ds(2, 1), :] = jnp.sum(t8, axis=0, keepdims=True)
        stat[0, h, pl.ds(3, 5), :] = jnp.zeros((5, qd), jnp.float32)
        remote(stat.at[0, h], stat.at[1, h], pair_ssem.at[2 + h], pair_rsem.at[2 + h], partner).start()

    for k in range(groups):
        g = jnp.where(c == 0, (z // 2 + near[k]) % groups, (groups // 2 + k) % groups)

        @pl.when(c == 0)
        def _():
            bytes_of(pool.at[pl.ds(0, (X - 1) * grows)], s2_rsem.at[g]).wait()

        @pl.when(c == 1)
        def _():
            if k == 0:
                bytes_of(pool.at[pl.ds(0, (Z - 1) * zrows)], s2_rsem.at[0]).wait()
            if k == groups // 2:
                bytes_of(pool.at[pl.ds(0, (Y - 1) * yrows)], s2_rsem.at[1]).wait()

        at = pl.ds(pl.multiple_of(g * tile, 16), tile)
        for i, h in enumerate(halves):
            s = lax.dot_general(pool[at, :], q_all[h], (((1,), (1,)), ((), ())), preferred_element_type=jnp.float32)
            scores[h, at, :] = s
            m = jnp.max(jnp.max(s.reshape(tile // 8, 8, qd), axis=0), axis=0, keepdims=True)

            def body(j, carry, g=g, h=h, m=m, target=targets[i]):
                l8, t8 = carry
                first = pl.multiple_of(g * tile + j * step, 8)
                at = pl.ds(first, step)
                s = scores[h, at, :]
                e = jnp.exp2((s - m) * K)
                scores[h, at, :] = e
                hit = row_iota == target - first
                return l8 + jnp.sum(fold(e), axis=0), t8 + jnp.sum(fold(jnp.where(hit, s, 0.0)), axis=0)

            l8, found[i] = lax.fori_loop(0, tile // step, body, (zero, found[i]))
            tops[g, h, pl.ds(0, 1), :] = m
            tops[g, h, pl.ds(1, 1), :] = jnp.sum(l8, axis=0, keepdims=True)
            if k == groups - 1:
                join(h, found[i])

    def shares(h):
        remote(stat.at[0, h], stat.at[1, h], pair_ssem.at[2 + h], pair_rsem.at[2 + h], partner).wait()
        m, l, t = (stat[0, h, pl.ds(k, 1), :] for k in range(3))
        m2, l2, t2 = (stat[1, h, pl.ds(k, 1), :] for k in range(3))
        top = jnp.maximum(m, m2)
        total = l * jnp.exp2((m - top) * K) + l2 * jnp.exp2((m2 - top) * K)
        valid = info[h, pl.ds(1, 1), :]
        return top, total, valid, t + t2

    sums = [shares(h) for h in halves]

    def gradients(g, i):
        top, total, valid, _ = sums[i]
        h, target, weight = halves[i], targets[i], SHARPNESS * valid
        factor = weight / total * jnp.exp2((tops[g, h, pl.ds(0, 1), :] - top) * K)

        def body(j):
            first = pl.multiple_of(g * tile + j * step, 16)
            at = pl.ds(first, step)
            hit = row_iota == target - first
            grad = scores[h, at, :] * factor - jnp.where(hit, weight, 0.0)
            grads[h, at, :] = grad.astype(jnp.bfloat16)
        loop(0, tile // step, body)

    slabs = [(1, i) for i in range(Y)] + [(0, i) for i in range(Z)]
    per = len(slabs) // groups
    for g in range(groups):
        at = pl.ds(g * tile, tile)
        for i in range(2):
            gradients(g, i)
        total = jnp.dot(grads[0, at, :], q_all[0], preferred_element_type=jnp.float32)
        total = total + jnp.dot(grads[1, at, :], q_all[1], preferred_element_type=jnp.float32)
        out_items[at, :] = total.astype(jnp.bfloat16)

        @pl.when(c == 0)
        def _():
            for dx in far_ring(X):
                px = (x + dx) % X
                remote(out_items.at[piece(g, px)], in_items.at[piece(g, x)],
                       r1_ssem, r1_rsem.at[g], dev(px, y, z, 0)).start()

        @pl.when(c == 1)
        def _():
            for kind, i in slabs[g * per:(g + 1) * per]:
                if kind == 0:
                    @pl.when(z != i)
                    def _():
                        remote(out_items.at[slab_z(i)], in_items.at[slab_z(z)],
                               r1_ssem, r1_rsem.at[0], dev(x, y, i, 1)).start()
                else:
                    @pl.when(y != i)
                    def _():
                        remote(out_items.at[slab_y(i)], in_items.at[slab_y(y)],
                               r1_ssem, r1_rsem.at[1], dev(x, i, z, 1)).start()

    top, total, valid, found_score = sums[1]
    loss_ref[...] = valid * (SHARPNESS * (top - found_score) + jnp.log(total))

    def query_part(h):
        return lax.dot_general(grads[h], pool[...], (((0,), (0,)), ((), ())), preferred_element_type=jnp.float32)

    qpart[...] = query_part(1 - c)
    part_copy = remote(qpart, qland, pair_ssem.at[4], pair_rsem.at[4], partner)
    part_copy.start()
    scores[0, pl.ds(0, qd), :] = query_part(c)

    def spread(rows_sum, owners, first):
        n = owners * BLK
        pack[pl.ds(0, n), :] = jnp.zeros((n, 128), jnp.float32)
        for r in range(OWNED):
            for a in range(chunks):
                pack[pl.ds(a * OWNED + r, owners, stride=BLK), :] = \
                    rows_sum[r * owners:(r + 1) * owners, a * 128:(a + 1) * 128]
        pieces[pl.ds(first * BLK, n), :] = pack[pl.ds(0, n), :].astype(jnp.bfloat16)

    def keep(block, slot):
        pltpu.make_async_copy(pieces.at[rows(block)], land2.at[rows(slot)], out_sem.at[2]).start()

    def deliver(block, slot, to):
        remote(pieces.at[rows(block)], land2.at[rows(slot)], r2_ssem, r2_rsem, to).start()

    @pl.when(c == 0)
    def _():
        me = z * Y + y
        for g in range(groups):
            bytes_of(in_items.at[pl.ds(0, (X - 1) * grows)], r1_rsem.at[g]).wait()
            total = out_items[piece(g, x), :].astype(jnp.float32)
            for i in range(1, X):
                total = total + in_items[piece(g, (x + i) % X), :].astype(jnp.float32)
            spread(total, members, g * members)
            for pz in (2 * g, 2 * g + 1):
                for dy in far_ring(Y):
                    py = (y + dy) % Y
                    deliver(pz * Y + py, me, dev(x, py, pz, 0))
                pl.when(z != pz)(functools.partial(deliver, pz * Y + y, me, dev(x, y, pz, 0)))
            pl.when(z // 2 == g)(functools.partial(keep, me, me))

    @pl.when(c == 1)
    def _():
        def deliver_all(rows_of, n, me, k, first, dests):
            bytes_of(in_items.at[pl.ds(0, (n - 1) * yrows)], r1_rsem.at[k]).wait()
            total = out_items[rows_of(me), :].astype(jnp.float32)
            for i in range(1, n):
                total = total + in_items[rows_of((me + i) % n), :].astype(jnp.float32)
            spread(total, len(dests), first)
            for i, (px, py, pz, slot) in enumerate(dests):
                here = jnp.logical_and(px == x, jnp.logical_and(py == y, pz == z))
                pl.when(jnp.logical_not(here))(functools.partial(deliver, first + i, slot, dev(px, py, pz, 1)))
                pl.when(here)(functools.partial(keep, first + i, slot))

        deliver_all(slab_y, Y, y, 1, 0,
                    [(px, y, pz, x * Z + z) for px in range(0, X, 2) for pz in range(Z)])
        deliver_all(slab_z, Z, z, 0, xz_own,
                    [(px, py, z, x * Y + y) for px in range(1, X, 2) for py in range(Y)])

    part_copy.wait()
    qg_ref[...] = (scores[0, pl.ds(0, qd), :] + qland[...]).astype(jnp.bfloat16)
    results = [pltpu.make_async_copy(a, b, out_sem.at[k])
               for k, (a, b) in enumerate([(qg_ref, qg_hbm), (loss_ref, loss_hbm)])]
    for result in results:
        result.start()

    @pl.when(c == 0)
    def _():
        bytes_of(land2.at[pl.ds(0, (Y * Z - 1) * BLK)], r2_rsem).wait()

    @pl.when(c == 1)
    def _():
        bytes_of(land2.at[pl.ds(0, (X * Z - 1) * BLK)], r2_rsem).wait()

    @pl.when(c == 0)
    def _():
        bytes_of(land.at[pl.ds(0, (Y * Z - 1) * BLK)], s1_ssem).wait()
        bytes_of(pool.at[pl.ds(0, (X - 1) * slab)], s2_ssem).wait()
        bytes_of(pool.at[pl.ds(0, (X - 1) * slab)], r1_ssem).wait()
        bytes_of(land2.at[pl.ds(0, (Y * Z - 1) * BLK)], r2_ssem).wait()

    @pl.when(c == 1)
    def _():
        bytes_of(land.at[pl.ds(0, (X * Z - 1) * BLK)], s1_ssem).wait()
        bytes_of(pool.at[pl.ds(0, (Y - 1) * yrows + (Z - 1) * zrows)], s2_ssem).wait()
        bytes_of(pool.at[pl.ds(0, (Y - 1) * yrows + (Z - 1) * zrows)], r1_ssem).wait()
        bytes_of(land2.at[pl.ds(0, (X * Z - 1) * BLK)], r2_ssem).wait()
    bytes_of(pieces.at[pl.ds(0, BLK)], out_sem.at[2]).wait()
    for result in results:
        result.wait()


def finish(n0, n1, qg, loss, land2, qg_out, ig_out, loss_out, qg_v, ig_v, loss_v, land_v, total, in_sem, out_sem):
    n = qg.shape[0] // 4
    legs = [(qg.at[pl.ds(i * n, n)], qg_v.at[pl.ds(i * n, n)], qg_out.at[pl.ds(i * n, n)]) for i in range(4)]
    legs += [(loss, loss_v, loss_out)]
    core = lax.axis_index("narrow") % 2
    counts = (n0, n1)

    def land_in(k):
        part = pl.ds(0, counts[k] * BLK)
        return pltpu.make_async_copy(land2.at[part], land_v.at[part], in_sem.at[5])

    for k in range(2):
        pl.when(core == k)(land_in(k).start)
    ins = [pltpu.make_async_copy(a, b, in_sem.at[k]) for k, (a, b, _) in enumerate(legs)]
    outs = [pltpu.make_async_copy(b, d, out_sem.at[k]) for k, (_, b, d) in enumerate(legs)]
    for copy in ins:
        copy.start()
    for k in range(2):
        pl.when(core == k)(land_in(k).wait)
    group = min(n0, n1, 8)

    def body(i, carry):
        part = land_v[pl.ds(pl.multiple_of(i * group * BLK, BLK), group * BLK), :].astype(jnp.float32)
        return carry + jnp.sum(part.reshape(group, BLK, 128), axis=0)

    count = jnp.where(core == 0, n0 // group, n1 // group)
    total[...] = lax.fori_loop(0, count, body, jnp.zeros((BLK, 128), jnp.float32))
    for a in range(ig_v.shape[1] // 128):
        ig_v[:, a * 128:(a + 1) * 128] = total[pl.ds(a * OWNED, OWNED), :]
    ig_copy = pltpu.make_async_copy(ig_v, ig_out, out_sem.at[5])
    ig_copy.start()
    for copy, after in zip(ins, outs):
        copy.wait()
        after.start()
    for copy in outs:
        copy.wait()
    ig_copy.wait()


def solution(mesh):
    X = mesh.shape["wide"] // ZHI

    def body(queries, targets, lengths, contrast_items):
        qd, width = queries.shape
        zlo = 4 if mesh.shape["narrow"] == 64 else 1
        Y = mesh.shape["narrow"] // (2 * zlo)
        Z = zlo * ZHI
        items = X * Y * Z * OWNED
        blocks = max(Y * Z, X * Z, X * Y) * BLK
        anywhere = pl.BlockSpec(memory_space=pl.ANY)
        f32, bf16 = jnp.float32, jnp.bfloat16
        outs = (
            jax.ShapeDtypeStruct((qd, width), bf16),
            jax.ShapeDtypeStruct((OWNED, width), f32),
            jax.ShapeDtypeStruct((1, qd), f32),
        )
        qg, loss, land2 = pl.pallas_call(
            functools.partial(kernel, X, Y, Z),
            out_shape=(outs[0], outs[2], jax.ShapeDtypeStruct((blocks, 128), bf16)),
            in_specs=[anywhere] * 4,
            out_specs=(anywhere,) * 3,
            scratch_shapes=[
                pltpu.VMEM((1, qd), jnp.int32),
                pltpu.SMEM(lengths.shape, jnp.int32),
                pltpu.VMEM((OWNED, width), bf16),
                pltpu.VMEM((qd, width), bf16),
                pltpu.VMEM((1, qd), f32),
                pltpu.VMEM((2, qd, width), bf16),
                pltpu.VMEM((2, 8, qd), f32),
                pltpu.VMEM((2, 2, 8, qd), f32),
                pltpu.VMEM((items, width), bf16),
                pltpu.VMEM((blocks, 128), f32),
                pltpu.VMEM((BLK, 128), bf16),
                pltpu.VMEM((blocks, 128), bf16),
                pltpu.VMEM((2, max(items, qd), qd), f32),
                pltpu.VMEM((Z // 2, 2, 8, qd), f32),
                pltpu.VMEM((2, items, qd), bf16),
                pltpu.VMEM((items, width), bf16),
                pltpu.VMEM((items, width), bf16),
                pltpu.VMEM((blocks, 128), bf16),
                pltpu.VMEM((qd, width), f32),
                pltpu.VMEM((qd, width), f32),
                pltpu.SemaphoreType.DMA,
                pltpu.SemaphoreType.DMA((3,)),
                pltpu.SemaphoreType.DMA((3,)),
                pltpu.SemaphoreType.DMA((5,)),
                pltpu.SemaphoreType.DMA((5,)),
                *[pltpu.SemaphoreType.DMA, pltpu.SemaphoreType.DMA((max(Z // 2, 2),))] * 3,
                *[pltpu.SemaphoreType.DMA] * 2,
            ],
            compiler_params=pltpu.CompilerParams(
                collective_id=0, has_side_effects=True, vmem_limit_bytes=60 << 20),
        )(queries, targets.reshape(1, qd), lengths, contrast_items)
        qg, ig, loss = pl.pallas_call(
            functools.partial(finish, Y * Z, X * Z), out_shape=outs, in_specs=[anywhere] * 3, out_specs=(anywhere,) * 3,
            scratch_shapes=[
                *[pltpu.VMEM(o.shape, o.dtype) for o in outs],
                pltpu.VMEM((blocks, 128), bf16),
                pltpu.VMEM((BLK, 128), f32),
                pltpu.SemaphoreType.DMA((6,)),
                pltpu.SemaphoreType.DMA((6,)),
            ],
            compiler_params=pltpu.CompilerParams(vmem_limit_bytes=60 << 20),
        )(qg, loss, land2)
        return qg, ig, loss.reshape(qd)

    rows = P(("wide", "narrow"), None)
    flat = P(("wide", "narrow"))
    return jax.shard_map(
        body, mesh=mesh, in_specs=(rows, flat, flat, rows), out_specs=(rows, rows, flat), check_vma=False)
```

```python
import functools

import jax
import jax.numpy as jnp
from jax import lax
from jax.experimental import pallas as pl
from jax.experimental.pallas import tpu as pltpu
from jax.sharding import PartitionSpec as P

MESH = pl.DeviceIdType.MESH
SEQ_LEN = 256
SHARPNESS = 20.0
LOG2E = 1.4426950408889634
ZHI = 2
OWNED = 3
BLK = 16


def hops(d, n):
    return min(d % n, -d % n)


def far_first(A, B):
    offsets = [(a, b) for a in range(A) for b in range(B) if a or b]
    return sorted(offsets, key=lambda o: -hops(o[0], A) - hops(o[1], B))


def far_ring(n):
    return sorted(range(1, n), key=lambda d: -hops(d, n))


def kernel(X, Y, Z, q_hbm, tgt_hbm, len_hbm, it_hbm, qg_hbm, loss_hbm, land2,
           tgt_ref, len_ref, it_ref, qg_ref, loss_ref, q_all, info, stat, pool, pack, blk, land, scores, tops, grads, out_items, in_items,
           pieces, qpart, qland,
           q_sem, in_sem, out_sem, pair_ssem, pair_rsem, s1_ssem, s1_rsem, s2_ssem, s2_rsem,
           r1_ssem, r1_rsem, r2_ssem, r2_rsem):
    zlo = Z // ZHI
    wide, narrow = lax.axis_index("wide"), lax.axis_index("narrow")
    x, c = wide // ZHI, narrow % 2
    y, z = (narrow // 2) % Y, (wide % ZHI) * zlo + narrow // (2 * Y)
    qd, width = q_hbm.shape
    chunks = width // 128
    slab = Y * Z * OWNED
    half = X * slab // 2
    yrows, zrows = half // Y, half // Z
    items = X * slab
    groups, members = Z // 2, 2 * Y
    grows = members * OWNED
    tile = X * grows
    last = Z - 1
    near = sorted(range(groups), key=lambda k: hops(k, groups))
    even = x % 2 == 0

    def dev(px, py, pz, pc):
        return (px * ZHI + pz // zlo, ((pz % zlo) * Y + py) * 2 + pc)

    yz, xz, xy = far_first(Y, Z), far_first(X, Z), far_first(X, Y)

    def remote(src, dst, ssem, rsem, to):
        return pltpu.make_async_remote_copy(
            src_ref=src, dst_ref=dst, send_sem=ssem, recv_sem=rsem, device_id=to, device_id_type=MESH)

    def bytes_of(ref, sem):
        return pltpu.make_async_copy(ref, ref, sem)

    def loop(lo, hi, f):
        def step(i, carry):
            f(i)
            return carry
        lax.fori_loop(lo, hi, step, 0)

    loads = [pltpu.make_async_copy(a, b, in_sem.at[k])
             for k, (a, b) in enumerate([(it_hbm, it_ref), (tgt_hbm, tgt_ref), (len_hbm, len_ref)])]
    load_q = pltpu.make_async_copy(q_hbm, q_all.at[c], q_sem)
    loads[0].start()

    barrier = pltpu.get_barrier_semaphore()
    partner = dev(x, y, z, 1 - c)

    def greet(to):
        pl.semaphore_signal(barrier, inc=1, device_id=to, device_id_type=MESH)

    @pl.when(c == 0)
    def _():
        for dy, dz in yz:
            greet(dev(x, (y + dy) % Y, (z + dz) % Z, 0))
        for dx in far_ring(X):
            greet(dev((x + dx) % X, y, z, 0))

    @pl.when(c == 1)
    def _():
        for dx, dz in xz:
            greet(dev((x + dx) % X, y, (z + dz) % Z, 1))
        for dx, dy in xy:
            greet(dev((x + dx) % X, (y + dy) % Y, z, 1))

    greet(partner)
    loads[1].start()
    loads[2].start()
    load_q.start()

    loads[0].wait()
    own = it_ref[...].astype(jnp.float32)
    pack[pl.ds(0, BLK), :] = jnp.zeros((BLK, 128), jnp.float32)
    for a in range(chunks):
        pack[pl.ds(a * OWNED, OWNED), :] = own[:, a * 128:(a + 1) * 128]
    blk[...] = pack[pl.ds(0, BLK), :].astype(jnp.bfloat16)

    @pl.when(c == 0)
    def _():
        pl.semaphore_wait(barrier, Y * Z - 1 + X - 1 + 1)

    @pl.when(c == 1)
    def _():
        pl.semaphore_wait(barrier, X * Z - 1 + X * Y - 1 + 1)

    def rows(i):
        return pl.ds(pl.multiple_of(i * BLK, BLK), BLK)

    @pl.when(c == 0)
    def _():
        me = z * Y + y
        land[rows(me), :] = blk[...]

        def send(py, pz):
            remote(blk, land.at[rows(me)], s1_ssem, s1_rsem.at[z // 2], dev(x, py, pz, 0)).start()

        for dy in far_ring(Y):
            send((y + dy) % Y, last)
        pl.when(z != last)(functools.partial(send, y, last))
        for dy, dz in yz:
            pz = (z + dz) % Z
            pl.when(pz != last)(functools.partial(send, (y + dy) % Y, pz))

    @pl.when(jnp.logical_and(c == 1, even))
    def _():
        me = (x // 2) * Z + z
        land[rows(me), :] = blk[...]

        def send(px, pz):
            remote(blk, land.at[rows(me)], s1_ssem, s1_rsem.at[1], dev(px, y, pz, 1)).start()

        for dx in far_ring(X):
            send((x + dx) % X, last)
        pl.when(z != last)(functools.partial(send, x, last))
        for dx, dz in xz:
            pz = (z + dz) % Z
            pl.when(pz != last)(functools.partial(send, (x + dx) % X, pz))

    @pl.when(jnp.logical_and(c == 1, jnp.logical_not(even)))
    def _():
        me = X // 2 * Z + (x // 2) * Y + y
        land[rows(me), :] = blk[...]

        for dx, dy in xy:
            remote(blk, land.at[rows(me)], s1_ssem, s1_rsem.at[0], dev((x + dx) % X, (y + dy) % Y, z, 1)).start()

    loads[1].wait()
    loads[2].wait()
    pos = lax.broadcasted_iota(jnp.int32, (1, qd), 1)
    live = jnp.where(pos < SEQ_LEN, (pos < len_ref[0]).astype(jnp.float32),
                     (pos - SEQ_LEN < len_ref[1]).astype(jnp.float32))
    info[c, pl.ds(0, 1), :] = tgt_ref[...].astype(jnp.float32)
    info[c, pl.ds(1, 1), :] = live
    info[c, pl.ds(2, 6), :] = jnp.zeros((6, qd), jnp.float32)
    load_q.wait()

    q_copy = remote(q_all.at[c], q_all.at[c], pair_ssem.at[0], pair_rsem.at[0], partner)
    q_copy.start()
    info_copy = remote(info.at[c], info.at[c], pair_ssem.at[1], pair_rsem.at[1], partner)
    info_copy.start()

    def landed(count, k):
        bytes_of(land.at[pl.ds(0, count * BLK)], s1_rsem.at[k]).wait()

    def unpack(first, owners, base):
        n = owners * BLK
        pack[pl.ds(0, n), :] = land[pl.ds(pl.multiple_of(first * BLK, BLK), n), :].astype(jnp.float32)
        for r in range(OWNED):
            for a in range(chunks):
                piece = pack[pl.ds(a * OWNED + r, owners, stride=BLK), :]
                at = base + r * owners
                pool[pl.ds(pl.multiple_of(at, 16), owners), a * 128:(a + 1) * 128] = piece.astype(jnp.bfloat16)

    xz_own, xy_own = X // 2 * Z, X // 2 * Y

    def piece(g, px):
        return pl.ds(pl.multiple_of(g * tile + px * grows, 16), grows)

    def y_at(py):
        return py * yrows

    def z_at(pz):
        return half + pz * zrows

    def slab_y(py):
        return pl.ds(pl.multiple_of(y_at(py), 16), yrows)

    def slab_z(pz):
        return pl.ds(pl.multiple_of(z_at(pz), 16), zrows)

    @pl.when(c == 0)
    def _():
        for k in near:
            g = (z // 2 + k) % groups
            landed(members - (k == 0), g)
            unpack(g * members, members, g * tile + x * grows)
            for dx in far_ring(X):
                remote(pool.at[piece(g, x)], pool.at[piece(g, x)],
                       s2_ssem, s2_rsem.at[g], dev((x + dx) % X, y, z, 0)).start()

    @pl.when(c == 1)
    def _():
        pl.when(even)(functools.partial(landed, xy_own, 0))
        pl.when(jnp.logical_not(even))(functools.partial(landed, xy_own - 1, 0))
        unpack(xz_own, xy_own, z_at(z))

        def send(pz):
            remote(pool.at[slab_z(z)], pool.at[slab_z(z)], s2_ssem, s2_rsem.at[0], dev(x, y, pz, 1)).start()

        pl.when(z != last)(functools.partial(send, last))
        for dz in far_ring(Z):
            pz = (z + dz) % Z
            pl.when(pz != last)(functools.partial(send, pz))

        pl.when(even)(functools.partial(landed, xz_own - 1, 1))
        pl.when(jnp.logical_not(even))(functools.partial(landed, xz_own, 1))
        unpack(0, xz_own, y_at(y))
        for dy in far_ring(Y):
            remote(pool.at[slab_y(y)], pool.at[slab_y(y)],
                   s2_ssem, s2_rsem.at[1], dev(x, (y + dy) % Y, z, 1)).start()

    q_copy.wait()
    info_copy.wait()

    def local_row(h):
        t = info[h, pl.ds(0, 1), :].astype(jnp.int32)
        o = (t * 21846) >> 16
        r = t - o * OWNED
        w, n = o // (zlo * Y * 2), o % (zlo * Y * 2)
        tx, tc = w // ZHI, n % 2
        ty, tz = (n // 2) % Y, (w % ZHI) * zlo + n // (2 * Y)
        on0 = (tz // 2) * tile + tx * grows + r * members + (tz % 2) * Y + ty
        on1 = jnp.where(tx % 2 == 0, y_at(ty) + r * xz_own + (tx // 2) * Z + tz,
                        z_at(tz) + r * xy_own + (tx // 2) * Y + ty)
        return jnp.where(tc == c, jnp.where(tc == 0, on0, on1), -1)

    step = max(8, items // 12)
    fold = functools.partial(jnp.reshape, shape=(step // 8, 8, qd))
    row_iota = lax.broadcasted_iota(jnp.int32, (step, qd), 0)
    K = SHARPNESS * LOG2E

    halves = (1 - c, c)
    targets = [local_row(h) for h in halves]
    zero = jnp.zeros((8, qd), jnp.float32)
    found = [zero, zero]
    def join(h, t8):
        m = tops[0, h, pl.ds(0, 1), :]
        for g in range(1, groups):
            m = jnp.maximum(m, tops[g, h, pl.ds(0, 1), :])
        l = jnp.zeros((1, qd), jnp.float32)
        for g in range(groups):
            l = l + tops[g, h, pl.ds(1, 1), :] * jnp.exp2((tops[g, h, pl.ds(0, 1), :] - m) * K)
        stat[0, h, pl.ds(0, 1), :] = m
        stat[0, h, pl.ds(1, 1), :] = l
        stat[0, h, pl.ds(2, 1), :] = jnp.sum(t8, axis=0, keepdims=True)
        stat[0, h, pl.ds(3, 5), :] = jnp.zeros((5, qd), jnp.float32)
        remote(stat.at[0, h], stat.at[1, h], pair_ssem.at[2 + h], pair_rsem.at[2 + h], partner).start()

    for k in range(groups):
        g = jnp.where(c == 0, (z // 2 + near[k]) % groups, (groups // 2 + k) % groups)

        @pl.when(c == 0)
        def _():
            bytes_of(pool.at[pl.ds(0, (X - 1) * grows)], s2_rsem.at[g]).wait()

        @pl.when(c == 1)
        def _():
            if k == 0:
                bytes_of(pool.at[pl.ds(0, (Z - 1) * zrows)], s2_rsem.at[0]).wait()
            if k == groups // 2:
                bytes_of(pool.at[pl.ds(0, (Y - 1) * yrows)], s2_rsem.at[1]).wait()

        at = pl.ds(pl.multiple_of(g * tile, 16), tile)
        for i, h in enumerate(halves):
            s = lax.dot_general(pool[at, :], q_all[h], (((1,), (1,)), ((), ())), preferred_element_type=jnp.float32)
            scores[h, at, :] = s
            m = jnp.max(jnp.max(s.reshape(tile // 8, 8, qd), axis=0), axis=0, keepdims=True)

            def body(j, carry, g=g, h=h, m=m, target=targets[i]):
                l8, t8 = carry
                first = pl.multiple_of(g * tile + j * step, 8)
                at = pl.ds(first, step)
                s = scores[h, at, :]
                e = jnp.exp2((s - m) * K)
                scores[h, at, :] = e
                hit = row_iota == target - first
                return l8 + jnp.sum(fold(e), axis=0), t8 + jnp.sum(fold(jnp.where(hit, s, 0.0)), axis=0)

            l8 = zero
            for j in range(tile // step):
                l8, found[i] = body(j, (l8, found[i]))
            tops[g, h, pl.ds(0, 1), :] = m
            tops[g, h, pl.ds(1, 1), :] = jnp.sum(l8, axis=0, keepdims=True)
            if k == groups - 1:
                join(h, found[i])

    def shares(h):
        remote(stat.at[0, h], stat.at[1, h], pair_ssem.at[2 + h], pair_rsem.at[2 + h], partner).wait()
        m, l, t = (stat[0, h, pl.ds(k, 1), :] for k in range(3))
        m2, l2, t2 = (stat[1, h, pl.ds(k, 1), :] for k in range(3))
        top = jnp.maximum(m, m2)
        total = l * jnp.exp2((m - top) * K) + l2 * jnp.exp2((m2 - top) * K)
        valid = info[h, pl.ds(1, 1), :]
        return top, total, valid, t + t2

    sums = [shares(h) for h in halves]

    def gradients(g, i):
        top, total, valid, _ = sums[i]
        h, target, weight = halves[i], targets[i], SHARPNESS * valid
        factor = weight / total * jnp.exp2((tops[g, h, pl.ds(0, 1), :] - top) * K)

        def body(j):
            first = pl.multiple_of(g * tile + j * step, 16)
            at = pl.ds(first, step)
            hit = row_iota == target - first
            grad = scores[h, at, :] * factor - jnp.where(hit, weight, 0.0)
            grads[h, at, :] = grad.astype(jnp.bfloat16)
        for j in range(tile // step):
            body(j)

    slabs = [(1, i) for i in range(Y)] + [(0, i) for i in range(Z)]
    per = len(slabs) // groups
    for g in range(groups):
        at = pl.ds(g * tile, tile)
        for i in range(2):
            gradients(g, i)
        total = jnp.dot(grads[0, at, :], q_all[0], preferred_element_type=jnp.float32)
        total = total + jnp.dot(grads[1, at, :], q_all[1], preferred_element_type=jnp.float32)
        out_items[at, :] = total.astype(jnp.bfloat16)

        @pl.when(c == 0)
        def _():
            for dx in far_ring(X):
                px = (x + dx) % X
                remote(out_items.at[piece(g, px)], in_items.at[piece(g, x)],
                       r1_ssem, r1_rsem.at[g], dev(px, y, z, 0)).start()

        @pl.when(c == 1)
        def _():
            for kind, i in slabs[g * per:(g + 1) * per]:
                if kind == 0:
                    @pl.when(z != i)
                    def _():
                        remote(out_items.at[slab_z(i)], in_items.at[slab_z(z)],
                               r1_ssem, r1_rsem.at[0], dev(x, y, i, 1)).start()
                else:
                    @pl.when(y != i)
                    def _():
                        remote(out_items.at[slab_y(i)], in_items.at[slab_y(y)],
                               r1_ssem, r1_rsem.at[1], dev(x, i, z, 1)).start()

    top, total, valid, found_score = sums[1]
    loss_ref[...] = valid * (SHARPNESS * (top - found_score) + jnp.log(total))

    def query_part(h):
        return lax.dot_general(grads[h], pool[...], (((0,), (0,)), ((), ())), preferred_element_type=jnp.float32)

    qpart[...] = query_part(1 - c)
    part_copy = remote(qpart, qland, pair_ssem.at[4], pair_rsem.at[4], partner)
    part_copy.start()
    scores[0, pl.ds(0, qd), :] = query_part(c)

    def spread(rows_sum, owners, first):
        n = owners * BLK
        pack[pl.ds(0, n), :] = jnp.zeros((n, 128), jnp.float32)
        for r in range(OWNED):
            for a in range(chunks):
                pack[pl.ds(a * OWNED + r, owners, stride=BLK), :] = \
                    rows_sum[r * owners:(r + 1) * owners, a * 128:(a + 1) * 128]
        pieces[pl.ds(first * BLK, n), :] = pack[pl.ds(0, n), :].astype(jnp.bfloat16)

    def keep(block, slot):
        pltpu.make_async_copy(pieces.at[rows(block)], land2.at[rows(slot)], out_sem.at[2]).start()

    def deliver(block, slot, to):
        remote(pieces.at[rows(block)], land2.at[rows(slot)], r2_ssem, r2_rsem, to).start()

    @pl.when(c == 0)
    def _():
        me = z * Y + y
        for g in range(groups):
            bytes_of(in_items.at[pl.ds(0, (X - 1) * grows)], r1_rsem.at[g]).wait()
            total = out_items[piece(g, x), :].astype(jnp.float32)
            for i in range(1, X):
                total = total + in_items[piece(g, (x + i) % X), :].astype(jnp.float32)
            spread(total, members, g * members)
            for pz in (2 * g, 2 * g + 1):
                for dy in far_ring(Y):
                    py = (y + dy) % Y
                    deliver(pz * Y + py, me, dev(x, py, pz, 0))
                pl.when(z != pz)(functools.partial(deliver, pz * Y + y, me, dev(x, y, pz, 0)))
            pl.when(z // 2 == g)(functools.partial(keep, me, me))

    @pl.when(c == 1)
    def _():
        def deliver_all(rows_of, n, me, k, first, dests):
            bytes_of(in_items.at[pl.ds(0, (n - 1) * yrows)], r1_rsem.at[k]).wait()
            total = out_items[rows_of(me), :].astype(jnp.float32)
            for i in range(1, n):
                total = total + in_items[rows_of((me + i) % n), :].astype(jnp.float32)
            spread(total, len(dests), first)
            for i, px, py, pz, slot in dests:
                here = jnp.logical_and(px == x, jnp.logical_and(py == y, pz == z))
                pl.when(jnp.logical_not(here))(functools.partial(deliver, first + i, slot, dev(px, py, pz, 1)))
                pl.when(here)(functools.partial(keep, first + i, slot))

        deliver_all(slab_y, Y, y, 1, 0,
                    [(px // 2 * Z + pz, px, y, pz, x * Z + z) for pz in range(Z) for px in range(0, X, 2)])
        deliver_all(slab_z, Z, z, 0, xz_own,
                    [(px // 2 * Y + py, px, py, z, x * Y + y) for py in range(Y) for px in range(1, X, 2)])

    part_copy.wait()
    qg_ref[...] = (scores[0, pl.ds(0, qd), :] + qland[...]).astype(jnp.bfloat16)
    results = [pltpu.make_async_copy(a, b, out_sem.at[k])
               for k, (a, b) in enumerate([(qg_ref, qg_hbm), (loss_ref, loss_hbm)])]
    for result in results:
        result.start()

    @pl.when(c == 0)
    def _():
        bytes_of(land2.at[pl.ds(0, (Y * Z - 1) * BLK)], r2_rsem).wait()

    @pl.when(c == 1)
    def _():
        bytes_of(land2.at[pl.ds(0, (X * Z - 1) * BLK)], r2_rsem).wait()

    @pl.when(c == 0)
    def _():
        bytes_of(land.at[pl.ds(0, (Y * Z - 1) * BLK)], s1_ssem).wait()
        bytes_of(pool.at[pl.ds(0, (X - 1) * slab)], s2_ssem).wait()
        bytes_of(pool.at[pl.ds(0, (X - 1) * slab)], r1_ssem).wait()
        bytes_of(land2.at[pl.ds(0, (Y * Z - 1) * BLK)], r2_ssem).wait()

    @pl.when(c == 1)
    def _():
        bytes_of(land.at[pl.ds(0, (X * Z - 1) * BLK)], s1_ssem).wait()
        bytes_of(pool.at[pl.ds(0, (Y - 1) * yrows + (Z - 1) * zrows)], s2_ssem).wait()
        bytes_of(pool.at[pl.ds(0, (Y - 1) * yrows + (Z - 1) * zrows)], r1_ssem).wait()
        bytes_of(land2.at[pl.ds(0, (X * Z - 1) * BLK)], r2_ssem).wait()
    bytes_of(pieces.at[pl.ds(0, BLK)], out_sem.at[2]).wait()
    for result in results:
        result.wait()


def finish(n0, n1, qg, loss, land2, qg_out, ig_out, loss_out, qg_v, ig_v, loss_v, land_v, total, in_sem, out_sem):
    n = qg.shape[0] // 4
    legs = [(qg.at[pl.ds(i * n, n)], qg_v.at[pl.ds(i * n, n)], qg_out.at[pl.ds(i * n, n)]) for i in range(4)]
    legs += [(loss, loss_v, loss_out)]
    core = lax.axis_index("narrow") % 2
    counts = (n0, n1)

    def land_in(k):
        part = pl.ds(0, counts[k] * BLK)
        return pltpu.make_async_copy(land2.at[part], land_v.at[part], in_sem.at[5])

    for k in range(2):
        pl.when(core == k)(land_in(k).start)
    ins = [pltpu.make_async_copy(a, b, in_sem.at[k]) for k, (a, b, _) in enumerate(legs)]
    outs = [pltpu.make_async_copy(b, d, out_sem.at[k]) for k, (_, b, d) in enumerate(legs)]
    for copy in ins:
        copy.start()
    for k in range(2):
        pl.when(core == k)(land_in(k).wait)
    group = min(n0, n1, 8)

    def body(i, carry):
        part = land_v[pl.ds(pl.multiple_of(i * group * BLK, BLK), group * BLK), :].astype(jnp.float32)
        return carry + jnp.sum(part.reshape(group, BLK, 128), axis=0)

    count = jnp.where(core == 0, n0 // group, n1 // group)
    total[...] = lax.fori_loop(0, count, body, jnp.zeros((BLK, 128), jnp.float32))
    for a in range(ig_v.shape[1] // 128):
        ig_v[:, a * 128:(a + 1) * 128] = total[pl.ds(a * OWNED, OWNED), :]
    ig_copy = pltpu.make_async_copy(ig_v, ig_out, out_sem.at[5])
    ig_copy.start()
    for copy, after in zip(ins, outs):
        copy.wait()
        after.start()
    for copy in outs:
        copy.wait()
    ig_copy.wait()


def solution(mesh):
    X = mesh.shape["wide"] // ZHI

    def body(queries, targets, lengths, contrast_items):
        qd, width = queries.shape
        zlo = 4 if mesh.shape["narrow"] == 64 else 1
        Y = mesh.shape["narrow"] // (2 * zlo)
        Z = zlo * ZHI
        items = X * Y * Z * OWNED
        blocks = max(Y * Z, X * Z, X * Y) * BLK
        anywhere = pl.BlockSpec(memory_space=pl.ANY)
        f32, bf16 = jnp.float32, jnp.bfloat16
        outs = (
            jax.ShapeDtypeStruct((qd, width), bf16),
            jax.ShapeDtypeStruct((OWNED, width), f32),
            jax.ShapeDtypeStruct((1, qd), f32),
        )
        qg, loss, land2 = pl.pallas_call(
            functools.partial(kernel, X, Y, Z),
            out_shape=(outs[0], outs[2], jax.ShapeDtypeStruct((blocks, 128), bf16)),
            in_specs=[anywhere] * 4,
            out_specs=(anywhere,) * 3,
            scratch_shapes=[
                pltpu.VMEM((1, qd), jnp.int32),
                pltpu.SMEM(lengths.shape, jnp.int32),
                pltpu.VMEM((OWNED, width), bf16),
                pltpu.VMEM((qd, width), bf16),
                pltpu.VMEM((1, qd), f32),
                pltpu.VMEM((2, qd, width), bf16),
                pltpu.VMEM((2, 8, qd), f32),
                pltpu.VMEM((2, 2, 8, qd), f32),
                pltpu.VMEM((items, width), bf16),
                pltpu.VMEM((blocks, 128), f32),
                pltpu.VMEM((BLK, 128), bf16),
                pltpu.VMEM((blocks, 128), bf16),
                pltpu.VMEM((2, max(items, qd), qd), f32),
                pltpu.VMEM((Z // 2, 2, 8, qd), f32),
                pltpu.VMEM((2, items, qd), bf16),
                pltpu.VMEM((items, width), bf16),
                pltpu.VMEM((items, width), bf16),
                pltpu.VMEM((blocks, 128), bf16),
                pltpu.VMEM((qd, width), f32),
                pltpu.VMEM((qd, width), f32),
                pltpu.SemaphoreType.DMA,
                pltpu.SemaphoreType.DMA((3,)),
                pltpu.SemaphoreType.DMA((3,)),
                pltpu.SemaphoreType.DMA((5,)),
                pltpu.SemaphoreType.DMA((5,)),
                *[pltpu.SemaphoreType.DMA, pltpu.SemaphoreType.DMA((max(Z // 2, 2),))] * 3,
                *[pltpu.SemaphoreType.DMA] * 2,
            ],
            compiler_params=pltpu.CompilerParams(
                collective_id=0, has_side_effects=True, vmem_limit_bytes=60 << 20),
        )(queries, targets.reshape(1, qd), lengths, contrast_items)
        qg, ig, loss = pl.pallas_call(
            functools.partial(finish, Y * Z, X * Z), out_shape=outs, in_specs=[anywhere] * 3, out_specs=(anywhere,) * 3,
            scratch_shapes=[
                *[pltpu.VMEM(o.shape, o.dtype) for o in outs],
                pltpu.VMEM((blocks, 128), bf16),
                pltpu.VMEM((BLK, 128), f32),
                pltpu.SemaphoreType.DMA((6,)),
                pltpu.SemaphoreType.DMA((6,)),
            ],
            compiler_params=pltpu.CompilerParams(vmem_limit_bytes=60 << 20),
        )(qg, loss, land2)
        return qg, ig, loss.reshape(qd)

    rows = P(("wide", "narrow"), None)
    flat = P(("wide", "narrow"))
    return jax.shard_map(
        body, mesh=mesh, in_specs=(rows, flat, flat, rows), out_specs=(rows, rows, flat), check_vma=False)
```

```python
import functools

import jax
import jax.numpy as jnp
from jax import lax
from jax.experimental import pallas as pl
from jax.experimental.pallas import tpu as pltpu
from jax.sharding import PartitionSpec as P

MESH = pl.DeviceIdType.MESH
SEQ_LEN = 256
SHARPNESS = 20.0
LOG2E = 1.4426950408889634
ZHI = 2
OWNED = 3
BLK = 16


def hops(d, n):
    return min(d % n, -d % n)


def far_first(A, B):
    offsets = [(a, b) for a in range(A) for b in range(B) if a or b]
    return sorted(offsets, key=lambda o: -hops(o[0], A) - hops(o[1], B))


def far_ring(n):
    return sorted(range(1, n), key=lambda d: -hops(d, n))


def kernel(X, Y, Z, q_hbm, tgt_hbm, len_hbm, it_hbm, qg_hbm, loss_hbm, land2,
           tgt_ref, len_ref, it_ref, qg_ref, loss_ref, q_all, info, stat, pool, pack, blk, land, scores, tops, grads, out_items, in_items,
           pieces, qpart, qland,
           q_sem, in_sem, out_sem, pair_ssem, pair_rsem, s1_ssem, s1_rsem, s2_ssem, s2_rsem,
           r1_ssem, r1_rsem, r2_ssem, r2_rsem):
    zlo = Z // ZHI
    wide, narrow = lax.axis_index("wide"), lax.axis_index("narrow")
    x, c = wide // ZHI, narrow % 2
    y, z = (narrow // 2) % Y, (wide % ZHI) * zlo + narrow // (2 * Y)
    qd, width = q_hbm.shape
    chunks = width // 128
    slab = Y * Z * OWNED
    half = X * slab // 2
    yrows, zrows = half // Y, half // Z
    items = X * slab
    groups, members = Z // 2, 2 * Y
    grows = members * OWNED
    tile = X * grows
    last = Z - 1
    near = sorted(range(groups), key=lambda k: hops(k, groups))
    even = x % 2 == 0

    def dev(px, py, pz, pc):
        return (px * ZHI + pz // zlo, ((pz % zlo) * Y + py) * 2 + pc)

    yz, xz, xy = far_first(Y, Z), far_first(X, Z), far_first(X, Y)

    def remote(src, dst, ssem, rsem, to):
        return pltpu.make_async_remote_copy(
            src_ref=src, dst_ref=dst, send_sem=ssem, recv_sem=rsem, device_id=to, device_id_type=MESH)

    def bytes_of(ref, sem):
        return pltpu.make_async_copy(ref, ref, sem)

    def loop(lo, hi, f):
        def step(i, carry):
            f(i)
            return carry
        lax.fori_loop(lo, hi, step, 0)

    loads = [pltpu.make_async_copy(a, b, in_sem.at[k])
             for k, (a, b) in enumerate([(it_hbm, it_ref), (tgt_hbm, tgt_ref), (len_hbm, len_ref)])]
    load_q = pltpu.make_async_copy(q_hbm, q_all.at[c], q_sem)
    loads[0].start()

    barrier = pltpu.get_barrier_semaphore()
    partner = dev(x, y, z, 1 - c)

    def greet(to):
        pl.semaphore_signal(barrier, inc=1, device_id=to, device_id_type=MESH)

    @pl.when(c == 0)
    def _():
        for dy, dz in yz:
            greet(dev(x, (y + dy) % Y, (z + dz) % Z, 0))
        for dx in far_ring(X):
            greet(dev((x + dx) % X, y, z, 0))

    @pl.when(c == 1)
    def _():
        for dx, dz in xz:
            greet(dev((x + dx) % X, y, (z + dz) % Z, 1))
        for dx, dy in xy:
            greet(dev((x + dx) % X, (y + dy) % Y, z, 1))

    greet(partner)
    loads[1].start()
    loads[2].start()
    load_q.start()

    loads[0].wait()
    own = it_ref[...].astype(jnp.float32)
    pack[pl.ds(0, BLK), :] = jnp.zeros((BLK, 128), jnp.float32)
    for a in range(chunks):
        pack[pl.ds(a * OWNED, OWNED), :] = own[:, a * 128:(a + 1) * 128]
    blk[...] = pack[pl.ds(0, BLK), :].astype(jnp.bfloat16)

    @pl.when(c == 0)
    def _():
        pl.semaphore_wait(barrier, Y * Z - 1 + X - 1 + 1)

    @pl.when(c == 1)
    def _():
        pl.semaphore_wait(barrier, X * Z - 1 + X * Y - 1 + 1)

    def rows(i):
        return pl.ds(pl.multiple_of(i * BLK, BLK), BLK)

    @pl.when(c == 0)
    def _():
        me = z * Y + y
        land[rows(me), :] = blk[...]

        def send(py, pz):
            remote(blk, land.at[rows(me)], s1_ssem, s1_rsem.at[z // 2], dev(x, py, pz, 0)).start()

        for dy in far_ring(Y):
            send((y + dy) % Y, last)
        pl.when(z != last)(functools.partial(send, y, last))
        for dy, dz in yz:
            pz = (z + dz) % Z
            pl.when(pz != last)(functools.partial(send, (y + dy) % Y, pz))

    @pl.when(jnp.logical_and(c == 1, even))
    def _():
        me = (x // 2) * Z + z
        land[rows(me), :] = blk[...]

        def send(px, pz):
            remote(blk, land.at[rows(me)], s1_ssem, s1_rsem.at[1], dev(px, y, pz, 1)).start()

        for dx in far_ring(X):
            send((x + dx) % X, last)
        pl.when(z != last)(functools.partial(send, x, last))
        for dx, dz in xz:
            pz = (z + dz) % Z
            pl.when(pz != last)(functools.partial(send, (x + dx) % X, pz))

    @pl.when(jnp.logical_and(c == 1, jnp.logical_not(even)))
    def _():
        me = X // 2 * Z + (x // 2) * Y + y
        land[rows(me), :] = blk[...]

        for dx, dy in xy:
            remote(blk, land.at[rows(me)], s1_ssem, s1_rsem.at[0], dev((x + dx) % X, (y + dy) % Y, z, 1)).start()

    loads[1].wait()
    loads[2].wait()
    pos = lax.broadcasted_iota(jnp.int32, (1, qd), 1)
    live = jnp.where(pos < SEQ_LEN, (pos < len_ref[0]).astype(jnp.float32),
                     (pos - SEQ_LEN < len_ref[1]).astype(jnp.float32))
    info[c, pl.ds(0, 1), :] = tgt_ref[...].astype(jnp.float32)
    info[c, pl.ds(1, 1), :] = live
    info[c, pl.ds(2, 6), :] = jnp.zeros((6, qd), jnp.float32)
    load_q.wait()

    q_copy = remote(q_all.at[c], q_all.at[c], pair_ssem.at[0], pair_rsem.at[0], partner)
    q_copy.start()
    info_copy = remote(info.at[c], info.at[c], pair_ssem.at[1], pair_rsem.at[1], partner)
    info_copy.start()

    def landed(count, k):
        bytes_of(land.at[pl.ds(0, count * BLK)], s1_rsem.at[k]).wait()

    def unpack(first, owners, base):
        n = owners * BLK
        pack[pl.ds(0, n), :] = land[pl.ds(pl.multiple_of(first * BLK, BLK), n), :].astype(jnp.float32)
        for r in range(OWNED):
            for a in range(chunks):
                piece = pack[pl.ds(a * OWNED + r, owners, stride=BLK), :]
                at = base + r * owners
                pool[pl.ds(pl.multiple_of(at, 16), owners), a * 128:(a + 1) * 128] = piece.astype(jnp.bfloat16)

    xz_own, xy_own = X // 2 * Z, X // 2 * Y

    def piece(g, px):
        return pl.ds(pl.multiple_of(g * tile + px * grows, 16), grows)

    def y_at(py):
        return py * yrows

    def z_at(pz):
        return half + pz * zrows

    def slab_y(py):
        return pl.ds(pl.multiple_of(y_at(py), 16), yrows)

    def slab_z(pz):
        return pl.ds(pl.multiple_of(z_at(pz), 16), zrows)

    @pl.when(c == 0)
    def _():
        for k in near:
            g = (z // 2 + k) % groups
            landed(members - (k == 0), g)
            unpack(g * members, members, g * tile + x * grows)
            for dx in far_ring(X):
                remote(pool.at[piece(g, x)], pool.at[piece(g, x)],
                       s2_ssem, s2_rsem.at[g], dev((x + dx) % X, y, z, 0)).start()

    @pl.when(c == 1)
    def _():
        pl.when(even)(functools.partial(landed, xz_own - 1, 1))
        pl.when(jnp.logical_not(even))(functools.partial(landed, xz_own, 1))
        unpack(0, xz_own, y_at(y))
        for dy in far_ring(Y):
            remote(pool.at[slab_y(y)], pool.at[slab_y(y)],
                   s2_ssem, s2_rsem.at[1], dev(x, (y + dy) % Y, z, 1)).start()

        pl.when(even)(functools.partial(landed, xy_own, 0))
        pl.when(jnp.logical_not(even))(functools.partial(landed, xy_own - 1, 0))
        unpack(xz_own, xy_own, z_at(z))

        def send(pz):
            remote(pool.at[slab_z(z)], pool.at[slab_z(z)], s2_ssem, s2_rsem.at[0], dev(x, y, pz, 1)).start()

        pl.when(z != last)(functools.partial(send, last))
        for dz in far_ring(Z):
            pz = (z + dz) % Z
            pl.when(pz != last)(functools.partial(send, pz))

    q_copy.wait()
    info_copy.wait()

    def local_row(h):
        t = info[h, pl.ds(0, 1), :].astype(jnp.int32)
        o = (t * 21846) >> 16
        r = t - o * OWNED
        w, n = o // (zlo * Y * 2), o % (zlo * Y * 2)
        tx, tc = w // ZHI, n % 2
        ty, tz = (n // 2) % Y, (w % ZHI) * zlo + n // (2 * Y)
        on0 = (tz // 2) * tile + tx * grows + r * members + (tz % 2) * Y + ty
        on1 = jnp.where(tx % 2 == 0, y_at(ty) + r * xz_own + (tx // 2) * Z + tz,
                        z_at(tz) + r * xy_own + (tx // 2) * Y + ty)
        return jnp.where(tc == c, jnp.where(tc == 0, on0, on1), -1)

    step = max(8, items // 12)
    fold = functools.partial(jnp.reshape, shape=(step // 8, 8, qd))
    row_iota = lax.broadcasted_iota(jnp.int32, (step, qd), 0)
    K = SHARPNESS * LOG2E

    halves = (1 - c, c)
    targets = [local_row(h) for h in halves]
    zero = jnp.zeros((8, qd), jnp.float32)
    found = [zero, zero]
    def join(h, t8):
        m = tops[0, h, pl.ds(0, 1), :]
        for g in range(1, groups):
            m = jnp.maximum(m, tops[g, h, pl.ds(0, 1), :])
        l = jnp.zeros((1, qd), jnp.float32)
        for g in range(groups):
            l = l + tops[g, h, pl.ds(1, 1), :] * jnp.exp2((tops[g, h, pl.ds(0, 1), :] - m) * K)
        stat[0, h, pl.ds(0, 1), :] = m
        stat[0, h, pl.ds(1, 1), :] = l
        stat[0, h, pl.ds(2, 1), :] = jnp.sum(t8, axis=0, keepdims=True)
        stat[0, h, pl.ds(3, 5), :] = jnp.zeros((5, qd), jnp.float32)
        remote(stat.at[0, h], stat.at[1, h], pair_ssem.at[2 + h], pair_rsem.at[2 + h], partner).start()

    for k in range(groups):
        g = jnp.where(c == 0, (z // 2 + near[k]) % groups, k)

        @pl.when(c == 0)
        def _():
            bytes_of(pool.at[pl.ds(0, (X - 1) * grows)], s2_rsem.at[g]).wait()

        @pl.when(c == 1)
        def _():
            if k == 0:
                bytes_of(pool.at[pl.ds(0, (Y - 1) * yrows)], s2_rsem.at[1]).wait()
            if k == groups // 2:
                bytes_of(pool.at[pl.ds(0, (Z - 1) * zrows)], s2_rsem.at[0]).wait()

        at = pl.ds(pl.multiple_of(g * tile, 16), tile)
        for i, h in enumerate(halves):
            s = lax.dot_general(pool[at, :], q_all[h], (((1,), (1,)), ((), ())), preferred_element_type=jnp.float32)
            scores[h, at, :] = s
            m = jnp.max(jnp.max(s.reshape(tile // 8, 8, qd), axis=0), axis=0, keepdims=True)

            def body(j, carry, g=g, h=h, m=m, target=targets[i]):
                l8, t8 = carry
                first = pl.multiple_of(g * tile + j * step, 8)
                at = pl.ds(first, step)
                s = scores[h, at, :]
                e = jnp.exp2((s - m) * K)
                scores[h, at, :] = e
                hit = row_iota == target - first
                return l8 + jnp.sum(fold(e), axis=0), t8 + jnp.sum(fold(jnp.where(hit, s, 0.0)), axis=0)

            l8 = zero
            for j in range(tile // step):
                l8, found[i] = body(j, (l8, found[i]))
            tops[g, h, pl.ds(0, 1), :] = m
            tops[g, h, pl.ds(1, 1), :] = jnp.sum(l8, axis=0, keepdims=True)
            if k == groups - 1:
                join(h, found[i])

    def shares(h):
        remote(stat.at[0, h], stat.at[1, h], pair_ssem.at[2 + h], pair_rsem.at[2 + h], partner).wait()
        m, l, t = (stat[0, h, pl.ds(k, 1), :] for k in range(3))
        m2, l2, t2 = (stat[1, h, pl.ds(k, 1), :] for k in range(3))
        top = jnp.maximum(m, m2)
        total = l * jnp.exp2((m - top) * K) + l2 * jnp.exp2((m2 - top) * K)
        valid = info[h, pl.ds(1, 1), :]
        return top, total, valid, t + t2

    sums = [shares(h) for h in halves]

    def gradients(g, i):
        top, total, valid, _ = sums[i]
        h, target, weight = halves[i], targets[i], SHARPNESS * valid
        factor = weight / total * jnp.exp2((tops[g, h, pl.ds(0, 1), :] - top) * K)

        def body(j):
            first = pl.multiple_of(g * tile + j * step, 16)
            at = pl.ds(first, step)
            hit = row_iota == target - first
            grad = scores[h, at, :] * factor - jnp.where(hit, weight, 0.0)
            grads[h, at, :] = grad.astype(jnp.bfloat16)
        for j in range(tile // step):
            body(j)

    slabs = [(1, i) for i in range(Y)] + [(0, i) for i in range(Z)]
    per = len(slabs) // groups
    for g in range(groups):
        at = pl.ds(g * tile, tile)
        for i in range(2):
            gradients(g, i)
        total = jnp.dot(grads[0, at, :], q_all[0], preferred_element_type=jnp.float32)
        total = total + jnp.dot(grads[1, at, :], q_all[1], preferred_element_type=jnp.float32)
        out_items[at, :] = total.astype(jnp.bfloat16)

        @pl.when(c == 0)
        def _():
            for dx in far_ring(X):
                px = (x + dx) % X
                remote(out_items.at[piece(g, px)], in_items.at[piece(g, x)],
                       r1_ssem, r1_rsem.at[g], dev(px, y, z, 0)).start()

        @pl.when(c == 1)
        def _():
            for kind, i in slabs[g * per:(g + 1) * per]:
                if kind == 0:
                    @pl.when(z != i)
                    def _():
                        remote(out_items.at[slab_z(i)], in_items.at[slab_z(z)],
                               r1_ssem, r1_rsem.at[0], dev(x, y, i, 1)).start()
                else:
                    @pl.when(y != i)
                    def _():
                        remote(out_items.at[slab_y(i)], in_items.at[slab_y(y)],
                               r1_ssem, r1_rsem.at[1], dev(x, i, z, 1)).start()

    top, total, valid, found_score = sums[1]
    loss_ref[...] = valid * (SHARPNESS * (top - found_score) + jnp.log(total))

    def query_part(h):
        return lax.dot_general(grads[h], pool[...], (((0,), (0,)), ((), ())), preferred_element_type=jnp.float32)

    qpart[...] = query_part(1 - c)
    part_copy = remote(qpart, qland, pair_ssem.at[4], pair_rsem.at[4], partner)
    part_copy.start()
    scores[0, pl.ds(0, qd), :] = query_part(c)

    def spread(rows_sum, owners, first):
        n = owners * BLK
        pack[pl.ds(0, n), :] = jnp.zeros((n, 128), jnp.float32)
        for r in range(OWNED):
            for a in range(chunks):
                pack[pl.ds(a * OWNED + r, owners, stride=BLK), :] = \
                    rows_sum[r * owners:(r + 1) * owners, a * 128:(a + 1) * 128]
        pieces[pl.ds(first * BLK, n), :] = pack[pl.ds(0, n), :].astype(jnp.bfloat16)

    def keep(block, slot):
        pltpu.make_async_copy(pieces.at[rows(block)], land2.at[rows(slot)], out_sem.at[2]).start()

    def deliver(block, slot, to):
        remote(pieces.at[rows(block)], land2.at[rows(slot)], r2_ssem, r2_rsem, to).start()

    @pl.when(c == 0)
    def _():
        me = z * Y + y
        for g in range(groups):
            bytes_of(in_items.at[pl.ds(0, (X - 1) * grows)], r1_rsem.at[g]).wait()
            total = out_items[piece(g, x), :].astype(jnp.float32)
            for i in range(1, X):
                total = total + in_items[piece(g, (x + i) % X), :].astype(jnp.float32)
            spread(total, members, g * members)
            for pz in (2 * g, 2 * g + 1):
                for dy in far_ring(Y):
                    py = (y + dy) % Y
                    deliver(pz * Y + py, me, dev(x, py, pz, 0))
                pl.when(z != pz)(functools.partial(deliver, pz * Y + y, me, dev(x, y, pz, 0)))
            pl.when(z // 2 == g)(functools.partial(keep, me, me))

    @pl.when(c == 1)
    def _():
        def deliver_all(rows_of, n, me, k, first, dests):
            bytes_of(in_items.at[pl.ds(0, (n - 1) * yrows)], r1_rsem.at[k]).wait()
            total = out_items[rows_of(me), :].astype(jnp.float32)
            for i in range(1, n):
                total = total + in_items[rows_of((me + i) % n), :].astype(jnp.float32)
            spread(total, len(dests), first)
            for i, px, py, pz, slot in dests:
                here = jnp.logical_and(px == x, jnp.logical_and(py == y, pz == z))
                pl.when(jnp.logical_not(here))(functools.partial(deliver, first + i, slot, dev(px, py, pz, 1)))
                pl.when(here)(functools.partial(keep, first + i, slot))

        deliver_all(slab_y, Y, y, 1, 0,
                    [(px // 2 * Z + pz, px, y, pz, x * Z + z) for pz in range(Z) for px in range(0, X, 2)])
        deliver_all(slab_z, Z, z, 0, xz_own,
                    [(px // 2 * Y + py, px, py, z, x * Y + y) for py in range(Y) for px in range(1, X, 2)])

    part_copy.wait()
    qg_ref[...] = (scores[0, pl.ds(0, qd), :] + qland[...]).astype(jnp.bfloat16)
    results = [pltpu.make_async_copy(a, b, out_sem.at[k])
               for k, (a, b) in enumerate([(qg_ref, qg_hbm), (loss_ref, loss_hbm)])]
    for result in results:
        result.start()

    @pl.when(c == 0)
    def _():
        bytes_of(land2.at[pl.ds(0, (Y * Z - 1) * BLK)], r2_rsem).wait()

    @pl.when(c == 1)
    def _():
        bytes_of(land2.at[pl.ds(0, (X * Z - 1) * BLK)], r2_rsem).wait()

    @pl.when(c == 0)
    def _():
        bytes_of(land.at[pl.ds(0, (Y * Z - 1) * BLK)], s1_ssem).wait()
        bytes_of(pool.at[pl.ds(0, (X - 1) * slab)], s2_ssem).wait()
        bytes_of(pool.at[pl.ds(0, (X - 1) * slab)], r1_ssem).wait()
        bytes_of(land2.at[pl.ds(0, (Y * Z - 1) * BLK)], r2_ssem).wait()

    @pl.when(c == 1)
    def _():
        bytes_of(land.at[pl.ds(0, (X * Z - 1) * BLK)], s1_ssem).wait()
        bytes_of(pool.at[pl.ds(0, (Y - 1) * yrows + (Z - 1) * zrows)], s2_ssem).wait()
        bytes_of(pool.at[pl.ds(0, (Y - 1) * yrows + (Z - 1) * zrows)], r1_ssem).wait()
        bytes_of(land2.at[pl.ds(0, (X * Z - 1) * BLK)], r2_ssem).wait()
    bytes_of(pieces.at[pl.ds(0, BLK)], out_sem.at[2]).wait()
    for result in results:
        result.wait()


def finish(n0, n1, qg, loss, land2, qg_out, ig_out, loss_out, qg_v, ig_v, loss_v, land_v, total, in_sem, out_sem):
    n = qg.shape[0] // 4
    legs = [(qg.at[pl.ds(i * n, n)], qg_v.at[pl.ds(i * n, n)], qg_out.at[pl.ds(i * n, n)]) for i in range(4)]
    legs += [(loss, loss_v, loss_out)]
    core = lax.axis_index("narrow") % 2
    counts = (n0, n1)

    def land_in(k):
        part = pl.ds(0, counts[k] * BLK)
        return pltpu.make_async_copy(land2.at[part], land_v.at[part], in_sem.at[5])

    for k in range(2):
        pl.when(core == k)(land_in(k).start)
    ins = [pltpu.make_async_copy(a, b, in_sem.at[k]) for k, (a, b, _) in enumerate(legs)]
    outs = [pltpu.make_async_copy(b, d, out_sem.at[k]) for k, (_, b, d) in enumerate(legs)]
    for copy in ins:
        copy.start()
    for k in range(2):
        pl.when(core == k)(land_in(k).wait)
    group = min(n0, n1, 8)

    def body(i, carry):
        part = land_v[pl.ds(pl.multiple_of(i * group * BLK, BLK), group * BLK), :].astype(jnp.float32)
        return carry + jnp.sum(part.reshape(group, BLK, 128), axis=0)

    count = jnp.where(core == 0, n0 // group, n1 // group)
    total[...] = lax.fori_loop(0, count, body, jnp.zeros((BLK, 128), jnp.float32))
    for a in range(ig_v.shape[1] // 128):
        ig_v[:, a * 128:(a + 1) * 128] = total[pl.ds(a * OWNED, OWNED), :]
    ig_copy = pltpu.make_async_copy(ig_v, ig_out, out_sem.at[5])
    ig_copy.start()
    for copy, after in zip(ins, outs):
        copy.wait()
        after.start()
    for copy in outs:
        copy.wait()
    ig_copy.wait()


def solution(mesh):
    X = mesh.shape["wide"] // ZHI

    def body(queries, targets, lengths, contrast_items):
        qd, width = queries.shape
        zlo = 4 if mesh.shape["narrow"] == 64 else 1
        Y = mesh.shape["narrow"] // (2 * zlo)
        Z = zlo * ZHI
        items = X * Y * Z * OWNED
        blocks = max(Y * Z, X * Z, X * Y) * BLK
        anywhere = pl.BlockSpec(memory_space=pl.ANY)
        f32, bf16 = jnp.float32, jnp.bfloat16
        outs = (
            jax.ShapeDtypeStruct((qd, width), bf16),
            jax.ShapeDtypeStruct((OWNED, width), f32),
            jax.ShapeDtypeStruct((1, qd), f32),
        )
        qg, loss, land2 = pl.pallas_call(
            functools.partial(kernel, X, Y, Z),
            out_shape=(outs[0], outs[2], jax.ShapeDtypeStruct((blocks, 128), bf16)),
            in_specs=[anywhere] * 4,
            out_specs=(anywhere,) * 3,
            scratch_shapes=[
                pltpu.VMEM((1, qd), jnp.int32),
                pltpu.SMEM(lengths.shape, jnp.int32),
                pltpu.VMEM((OWNED, width), bf16),
                pltpu.VMEM((qd, width), bf16),
                pltpu.VMEM((1, qd), f32),
                pltpu.VMEM((2, qd, width), bf16),
                pltpu.VMEM((2, 8, qd), f32),
                pltpu.VMEM((2, 2, 8, qd), f32),
                pltpu.VMEM((items, width), bf16),
                pltpu.VMEM((blocks, 128), f32),
                pltpu.VMEM((BLK, 128), bf16),
                pltpu.VMEM((blocks, 128), bf16),
                pltpu.VMEM((2, max(items, qd), qd), f32),
                pltpu.VMEM((Z // 2, 2, 8, qd), f32),
                pltpu.VMEM((2, items, qd), bf16),
                pltpu.VMEM((items, width), bf16),
                pltpu.VMEM((items, width), bf16),
                pltpu.VMEM((blocks, 128), bf16),
                pltpu.VMEM((qd, width), f32),
                pltpu.VMEM((qd, width), f32),
                pltpu.SemaphoreType.DMA,
                pltpu.SemaphoreType.DMA((3,)),
                pltpu.SemaphoreType.DMA((3,)),
                pltpu.SemaphoreType.DMA((5,)),
                pltpu.SemaphoreType.DMA((5,)),
                *[pltpu.SemaphoreType.DMA, pltpu.SemaphoreType.DMA((max(Z // 2, 2),))] * 3,
                *[pltpu.SemaphoreType.DMA] * 2,
            ],
            compiler_params=pltpu.CompilerParams(
                collective_id=0, has_side_effects=True, vmem_limit_bytes=60 << 20),
        )(queries, targets.reshape(1, qd), lengths, contrast_items)
        qg, ig, loss = pl.pallas_call(
            functools.partial(finish, Y * Z, X * Z), out_shape=outs, in_specs=[anywhere] * 3, out_specs=(anywhere,) * 3,
            scratch_shapes=[
                *[pltpu.VMEM(o.shape, o.dtype) for o in outs],
                pltpu.VMEM((blocks, 128), bf16),
                pltpu.VMEM((BLK, 128), f32),
                pltpu.SemaphoreType.DMA((6,)),
                pltpu.SemaphoreType.DMA((6,)),
            ],
            compiler_params=pltpu.CompilerParams(vmem_limit_bytes=60 << 20),
        )(qg, loss, land2)
        return qg, ig, loss.reshape(qd)

    rows = P(("wide", "narrow"), None)
    flat = P(("wide", "narrow"))
    return jax.shard_map(
        body, mesh=mesh, in_specs=(rows, flat, flat, rows), out_specs=(rows, rows, flat), check_vma=False)
```
